32 devices in a mesh: groups: 2 (over y), rec: 4 (over z), attr: 4 (over x, core).
Axes of the slice: x: 2, y: 2, z: 4, core: 2. Of those that a mesh axis runs over, the one named last changes fastest.
Arguments:
- cells: bfloat16 [64, 49152], P(('groups', 'rec'), 'attr'), parts along dimension 0, may hold values from -1000 to 1000
- cotangent: bfloat16 [64, 49152], P(('groups', 'rec'), 'attr'), parts along dimension 0, may hold values from -6 to 6
- qkv_attr: bfloat16 [192, 576], replicated, may hold values from -8 to 8
- out_attr: bfloat16 [192, 192], replicated, may hold values from -0.4375 to 0.4375
- qkv_samp: bfloat16 [192, 576], replicated, may hold values from -8 to 8
- out_samp: bfloat16 [192, 192], replicated, may hold values from -0.4375 to 0.4375
- up_weight: bfloat16 [192, 768], replicated, may hold values from -0.4375 to 0.4375
- down_weight: bfloat16 [768, 192], replicated, may hold values from -0.21875 to 0.21875
- train_split: int32 [64], P('groups'), parts along dimension 0, may hold values from 0 to 1, as said below
Outputs:
- grad_cells: bfloat16 [64, 49152], P(('groups', 'rec'), 'attr'), parts along dimension 0
- grad_qkv_attr: float32 [384, 576], P('groups'), parts along dimension 0
- grad_out_attr: float32 [384, 192], P('groups'), parts along dimension 0
- grad_qkv_samp: float32 [384, 576], P('groups'), parts along dimension 0
- grad_out_samp: float32 [384, 192], P('groups'), parts along dimension 0
- grad_up: float32 [384, 768], P('groups'), parts along dimension 0
- grad_down: float32 [1536, 192], P('groups'), parts along dimension 0
The draws below stay inside these ranges and needn't reach their ends.
There are 2 independent parts, one for each index of `groups`. The reference program is written for one: setup_inputs(seed, part) draws one part's arguments, and reference() takes and returns one part's arrays. A program takes and returns all parts, laid end to end along the dimension named above; an argument that names none is the same for every part. Nothing has to cross between parts.
Inputs may be any that keep to these rules, and one draw needn't show every extreme that they name: `train_split`: every table window has at least one training record.
All inputs are finite; a program needn't handle non-finite values.
Results may differ from the reference program's by a relative error of at most 0.018.
The reference program's roundings to bfloat16 on the way count: a program that leaves them out, or rounds other values in their place, can miss the bound.
Values may be sent and summed in bfloat16 or wider, within the bound.
No kernel may reach another device: no remote copies, remote signals or barrier semaphores. Data moves between devices by JAX's collectives and lax.ppermute only.
A program may use at most 64 MiB of HBM per device.

```python
import math
import jax
import jax.numpy as jnp
from jax import lax

E = 192
HEADS = 6
FF = 768
RECORDS = 32
ATTRS = 256


def qkv_draw(key):
    base_key = jax.random.fold_in(key, 0)
    matrix = jax.random.normal(base_key, (E, 3 * E), jnp.float32) / math.sqrt(E)
    return matrix


def draw_qkv_attr(key, part):
    return qkv_draw(jax.random.fold_in(key, 11)).astype(jnp.bfloat16)


def draw_qkv_samp(key, part):
    return qkv_draw(jax.random.fold_in(key, 12)).astype(jnp.bfloat16)


def draw_cells(key, part):
    keys_all = jax.random.split(jax.random.fold_in(key, 13), 3)
    cell_scale = jnp.exp(jax.random.uniform(keys_all[1], (RECORDS, ATTRS, 1), jnp.float32, 0.0, math.log(10.0)))
    feature_scale = jnp.exp(jax.random.uniform(keys_all[2], (1, 1, E), jnp.float32, 0.0, math.log(10.0)))
    base = jax.random.normal(keys_all[0], (RECORDS, ATTRS, E), jnp.float32)
    return (base * cell_scale * feature_scale).reshape(RECORDS, ATTRS * E).astype(jnp.bfloat16)


def draw_train_split(key, part):
    first_key, second_key = jax.random.split(jax.random.fold_in(key, 14))
    coins = jax.random.randint(first_key, (RECORDS,), 0, 2)
    chosen = jax.random.randint(second_key, (), 0, RECORDS)
    return jnp.where(jnp.arange(RECORDS) == chosen, 1, coins).astype(jnp.int32)


def steps_of(stream_key, extent, cuts, low, high):
    factor_of, own = 1.0, jax.random.fold_in(stream_key, 6)
    for position, shards_of in cuts:
        steps = jnp.exp(jax.random.uniform(jax.random.fold_in(own, position), (shards_of,), jnp.float32, low / len(cuts), high / len(cuts)))
        factor_of = factor_of * jnp.repeat(steps, extent[position] // shards_of).reshape([-1 if axis == position else 1 for axis in range(len(extent))])
    return factor_of


def bell_draw(own_key, dims, deviation, limit, pieces=(), dtype=jnp.bfloat16):
    level = steps_of(own_key, dims, pieces, -0.22, 0.18) if pieces else 1.0
    result = jax.random.normal(own_key, dims, jnp.float32) * deviation * level
    return jnp.minimum(jnp.maximum(result, -limit), limit).astype(dtype)


def setup_inputs(seed: int = 0, part: int = 0) -> dict:
    seeds = jax.random.split(jax.random.key(seed), 10)
    own_keys = jax.random.split(jax.random.fold_in(seeds[9], part), 10)
    cells = draw_cells(jax.random.fold_in(jax.random.fold_in(seeds[9], part), 71), part)
    cotangent = bell_draw(own_keys[1], (RECORDS, ATTRS * E), 1.0, 6.0, ((0, 4), (1, 4)))
    qkv_attr = draw_qkv_attr(jax.random.fold_in(seeds[9], 71), part)
    out_attr = bell_draw(seeds[3], (E, E), E ** -0.5, 0.4375)
    qkv_samp = draw_qkv_samp(jax.random.fold_in(seeds[9], 71), part)
    out_samp = bell_draw(seeds[5], (E, E), E ** -0.5, 0.4375)
    up_weight = bell_draw(seeds[6], (E, FF), E ** -0.5, 0.4375)
    down_weight = bell_draw(seeds[7], (FF, E), FF ** -0.5, 0.21875)
    train_split = draw_train_split(jax.random.fold_in(jax.random.fold_in(seeds[9], part), 71), part)
    return {"cells": cells, "cotangent": cotangent, "qkv_attr": qkv_attr, "out_attr": out_attr, "qkv_samp": qkv_samp, "out_samp": out_samp, "up_weight": up_weight, "down_weight": down_weight, "train_split": train_split}


def product(form, left, right):
    return jnp.einsum(form, left.astype(jnp.float32), right.astype(jnp.float32))

def layer_norm(values):
    center = values - lax.optimization_barrier(jnp.mean(values, axis=-1, keepdims=True))
    spread = lax.optimization_barrier(jnp.mean(center * center, axis=-1, keepdims=True))
    return center * lax.rsqrt(spread + 1e-05)

def attend(cells_in, qkv_weight, out_weight, allowed):
    groups, length, width = cells_in.shape
    head_dim = width // HEADS
    as_float = cells_in.astype(jnp.float32)
    normed = layer_norm(as_float).astype(jnp.bfloat16)
    project = product('gle,ef->glf', normed, qkv_weight).astype(jnp.bfloat16)
    project = project.reshape(groups, length, 3, HEADS, head_dim)
    scores = product('gqhd,gkhd->ghqk', project[:, :, 0], project[:, :, 1]) * (1.0 / math.sqrt(head_dim))
    if allowed is not None:
        scores = jnp.where(allowed[None, None, None, :] > 0, scores, -1e+30)
    top_score = lax.stop_gradient(lax.optimization_barrier(jnp.max(scores, axis=-1, keepdims=True)))
    expo = jnp.exp(scores - top_score)
    probs = (expo / lax.optimization_barrier(jnp.sum(expo, axis=-1, keepdims=True))).astype(jnp.bfloat16)
    mixed = product('ghqk,gkhd->gqhd', probs, project[:, :, 2]).astype(jnp.bfloat16)
    mixed = mixed.reshape(groups, length, width)
    return (as_float + product('gle,ef->glf', mixed, out_weight)).astype(jnp.bfloat16)

def feed_forward(block, up_weight, down_weight):
    flat = block.reshape(-1, E)
    as_float = flat.astype(jnp.float32)
    normed = layer_norm(as_float).astype(jnp.bfloat16)
    hidden = jax.nn.gelu(product('re,ef->rf', normed, up_weight), approximate=False).astype(jnp.bfloat16)
    return (as_float + product('rf,fe->re', hidden, down_weight)).astype(jnp.bfloat16).reshape(block.shape)

def reference(cells, cotangent, qkv_attr, out_attr, qkv_samp, out_samp, up_weight, down_weight, train_split):
    rec_block = math.gcd(RECORDS, 8)
    attr_block = math.gcd(ATTRS, 8)

    def forward(table_flat, qa_weight, oa_weight, qs_weight, os_weight, first_weight, second_weight):
        table = table_flat.reshape(RECORDS // rec_block, rec_block, ATTRS, E)

        def attr_step(piece):
            return attend(piece, qa_weight, oa_weight, None)
        first = lax.map(jax.checkpoint(attr_step), table).reshape(RECORDS, ATTRS, E)
        turned = jnp.swapaxes(first, 0, 1).reshape(ATTRS // attr_block, attr_block, RECORDS, E)

        def samp_step(piece):
            return attend(piece, qs_weight, os_weight, train_split)
        second = lax.map(jax.checkpoint(samp_step), turned).reshape(ATTRS, RECORDS, E)
        second = jnp.swapaxes(second, 0, 1)
        return feed_forward(second, first_weight, second_weight).reshape(RECORDS, ATTRS * E)
    weights = (qkv_attr, out_attr, qkv_samp, out_samp, up_weight, down_weight)
    weights = tuple((matrix.astype(jnp.float32) for matrix in weights))
    output_cells, puller = jax.vjp(forward, cells, *weights)
    grads = puller(cotangent)
    factor = 1.0 / math.sqrt(RECORDS * ATTRS)
    return (grads[0], grads[1] * factor, grads[2] * factor, grads[3] * factor, grads[4] * factor, grads[5] * factor, grads[6] * factor)
```

```python
import functools
import math

import jax
import jax.numpy as jnp
from jax import lax
from jax.experimental import pallas as pl
from jax.experimental.pallas import tpu as pltpu
from jax.sharding import PartitionSpec as P

E = 192
HEADS = 6
FF = 768
HEAD = E // HEADS
LANES = 128
BF = jnp.bfloat16
F32 = jnp.float32
EXP2 = math.log2(math.e) / math.sqrt(HEAD)
SCALE = 1.0 / math.sqrt(HEAD)
HALF_ROOT = math.sqrt(0.5)
BELL = 1.0 / math.sqrt(2.0 * math.pi)


def nn(left, right):
    return lax.dot_general(left, right, (((1,), (0,)), ((), ())), preferred_element_type=F32)


def nt(left, right):
    return lax.dot_general(left, right, (((1,), (1,)), ((), ())), preferred_element_type=F32)


def tn(left, right):
    return lax.dot_general(left, right, (((0,), (0,)), ((), ())), preferred_element_type=F32)


def digits(index, sizes):
    out = []
    for size in reversed(sizes):
        if size & (size - 1) == 0:
            out.append(index & (size - 1))
            index = index >> (size.bit_length() - 1)
        else:
            out.append(lax.rem(index, size))
            index = lax.div(index, size)
    return out[::-1]


def wrap(index, size):
    return digits(index + size, (size,))[0]


def one_hot(rows, source):
    own = lax.broadcasted_iota(jnp.int32, (rows, source.shape[1]), 0)
    return jnp.where(own == source, 1.0, 0.0).astype(BF)


def lane_index(size):
    return lax.broadcasted_iota(jnp.int32, (1, size), 1)


def eye(size):
    return one_hot(size, lane_index(size))


def side_by_side(refs):
    return jnp.concatenate([ref[...] for ref in refs], axis=1)


def put_tiles(refs, table):
    width = refs[0].shape[1]
    for position, ref in enumerate(refs):
        ref[...] = table[:, position * width : (position + 1) * width].astype(ref.dtype)


class Plan:
    def __init__(self, cells, ranks_rec, ranks_attr):
        self.ranks_rec, self.ranks_attr = ranks_rec, ranks_attr
        self.rec, self.attr = cells.shape[0], cells.shape[1] // E
        self.cells = self.rec * self.attr
        self.own_rec = self.rec // ranks_attr
        self.own_attr = self.attr // ranks_rec
        self.all_rec = self.rec * ranks_rec
        self.all_attr = self.attr * ranks_attr
        self.row_tile = self.own_rec * self.attr
        self.col_tile = self.rec * self.own_attr

    def row_digits(self, index):
        return digits(index, (self.ranks_attr, self.own_rec, self.attr))

    def col_digits(self, index):
        return digits(index, (self.ranks_rec, self.ranks_attr, self.own_rec, self.own_attr))

    def record_of(self, step, own):
        return self.own_rec * wrap(step + lax.axis_index("attr"), self.ranks_attr) + own

    def attr_of(self, step, own):
        return self.own_attr * wrap(step + lax.axis_index("rec"), self.ranks_rec) + own

    def rows_from_owned(self):
        step, own, attr = self.row_digits(lane_index(self.cells))
        return attr * self.rec + self.record_of(step, own)

    def cols_from_owned(self):
        far, near, own, attr = self.col_digits(lane_index(self.cells))
        return self.attr_of(far, attr) * self.rec + self.record_of(near, own)

    def cols_from_rows(self):
        far, near, own, attr = self.col_digits(lane_index(self.cells))
        return (near * self.own_rec + own) * self.attr + self.attr_of(far, attr)

    def grouped_from_rows(self):
        own, step, attr = digits(lane_index(self.cells), (self.own_rec, self.ranks_attr, self.attr))
        return (step * self.own_rec + own) * self.attr + attr

    def grouped_from_cols(self):
        attr, place = digits(lane_index(self.cells), (self.own_attr, self.all_rec))
        return place * self.own_attr + attr


def split_kernel(plan, to_rows, table_ref, *refs):
    outs, rows = refs[:-1], refs[-1]
    for pair in range(plan.attr // 2):
        both = table_ref[:, 2 * E * pair : 2 * E * (pair + 1)].astype(F32)
        for side in range(2):
            start = (2 * pair + side) * plan.rec
            rows[start : start + plan.rec, :] = both[:, side * E : (side + 1) * E]
    turned = nt(eye(E), rows[...].astype(BF)).astype(BF)
    source = plan.rows_from_owned() if to_rows else plan.cols_from_owned()
    put_tiles(outs, nn(turned, one_hot(plan.cells, source)))


def join_kernel(plan, *refs):
    tiles, out_ref, rows = refs[:-2], refs[-2], refs[-1]
    rows[...] = nt(one_hot(plan.cells, plan.rows_from_owned()), side_by_side(tiles))
    for pair in range(plan.attr // 2):
        start = 2 * pair * plan.rec
        both = [rows[start + side * plan.rec : start + (side + 1) * plan.rec, :] for side in range(2)]
        out_ref[:, 2 * E * pair : 2 * E * (pair + 1)] = jnp.concatenate(both, axis=1).astype(BF)


def to_cols_kernel(plan, *refs):
    tiles, outs = refs[: plan.ranks_attr], refs[plan.ranks_attr :]
    put_tiles(outs, nn(side_by_side(tiles), one_hot(plan.cells, plan.cols_from_rows())))


def to_rows_kernel(plan, *refs):
    tiles, outs = refs[: plan.ranks_rec], refs[plan.ranks_rec :]
    put_tiles(outs, nt(side_by_side(tiles), one_hot(plan.cells, plan.cols_from_rows())))


def turn_kernel(count, *refs):
    for source, target in zip(refs[:count], refs[count:]):
        target[...] = source[...].astype(F32).T.astype(BF)


def norm(table):
    center = table - jnp.mean(table, axis=0, keepdims=True)
    spread = jnp.mean(center * center, axis=0, keepdims=True)
    root = lax.rsqrt(spread + 1e-05)
    return center * root, root


def norm_back(grad, normed, root):
    along = jnp.mean(grad * normed, axis=0, keepdims=True)
    return root * (grad - jnp.mean(grad, axis=0, keepdims=True) - normed * along)


def blocks_of(width, total):
    return [slice(start, start + width) for start in range(0, total, width)]


def heads_of(ref, part, head, cols):
    start = part * E + head * HEAD
    return ref[start : start + HEAD, cols]


def attend(x_ref, normed_ref, proj_ref, probs_ref, mixed_ref, qkv_t, out_t, width, mask):
    results = []
    for place, cols in enumerate(blocks_of(width, x_ref.shape[1])):
        table = x_ref[:, cols].astype(F32)
        normed_ref[:, cols] = norm(table)[0].astype(BF)
        proj_ref[:, cols] = nn(qkv_t[...], normed_ref[:, cols]).astype(BF)
        for head in range(HEADS):
            query, key, value = (heads_of(proj_ref, part, head, cols) for part in range(3))
            scores = tn(key, query)
            if mask is not None:
                scores = scores + mask
            expo = jnp.exp2((scores - jnp.max(scores, axis=0, keepdims=True)) * EXP2)
            probs = (expo * (1.0 / jnp.sum(expo, axis=0, keepdims=True))).astype(BF)
            probs_ref[place * HEADS + head] = probs
            mixed_ref[head * HEAD : (head + 1) * HEAD, cols] = nn(value, probs).astype(BF)
        results.append(x_ref[:, cols].astype(F32) + nn(out_t[...], mixed_ref[:, cols]))
    return results


def attend_back(grad_ref, x_ref, proj_ref, probs_ref, grad_proj_ref, qkv, out, width):
    results = []
    for place, cols in enumerate(blocks_of(width, x_ref.shape[1])):
        grad_mixed = nn(out[...], grad_ref[:, cols]).astype(BF)
        for head in range(HEADS):
            query, key, value = (heads_of(proj_ref, part, head, cols) for part in range(3))
            grad_head = grad_mixed[head * HEAD : (head + 1) * HEAD]
            probs = probs_ref[place * HEADS + head]
            grad_probs = tn(value, grad_head).astype(BF).astype(F32)
            wide = probs.astype(F32)
            moved = grad_probs * wide
            grad_scores = (moved - wide * jnp.sum(moved, axis=0, keepdims=True)) * SCALE
            grad_scores = grad_scores.astype(BF)
            for part, value_of in enumerate(
                (nn(key, grad_scores), nt(query, grad_scores), nt(grad_head, probs))
            ):
                start = part * E + head * HEAD
                grad_proj_ref[start : start + HEAD, cols] = value_of.astype(BF)
        grad_normed = nn(qkv[...], grad_proj_ref[:, cols]).astype(BF).astype(F32)
        normed, root = norm(x_ref[:, cols].astype(F32))
        results.append(norm_back(grad_normed, normed, root) + grad_ref[:, cols].astype(F32))
    return results


def put_attend_grads(out_ref, normed_ref, grad_proj_ref, mixed_ref, grad_ref):
    qkv = nt(normed_ref[...], grad_proj_ref[...])
    out = nt(mixed_ref[...], grad_ref[...])
    whole = 3 * E // LANES
    for tile in range(whole):
        out_ref[tile * E : (tile + 1) * E, :] = qkv[:, tile * LANES : (tile + 1) * LANES].astype(BF)
    mixed = jnp.concatenate([qkv[:, whole * LANES :], out[:, LANES:]], axis=1)
    out_ref[whole * E : (whole + 1) * E, :] = mixed.astype(BF)
    out_ref[(whole + 1) * E : (whole + 2) * E, :] = out[:, :LANES].astype(BF)


def take_attend_grads(in_ref, first, qkv_ref, out_ref, factor):
    whole = 3 * E // LANES

    def tile(number):
        return in_ref[first + number * E : first + (number + 1) * E, :].astype(F32) * factor

    for number in range(whole):
        qkv_ref[:, number * LANES : (number + 1) * LANES] = tile(number)
    mixed = tile(whole)
    qkv_ref[:, whole * LANES :] = mixed[:, : LANES // 2]
    out_ref[:, :LANES] = tile(whole + 1)
    out_ref[:, LANES:] = mixed[:, LANES // 2 :]


def rows_forward_kernel(plan, *refs):
    tiles, refs = refs[: plan.ranks_attr], refs[plan.ranks_attr :]
    (qkv_t, out_t), refs = refs[:2], refs[2:]
    outs, (x_ref, normed_ref, proj_ref, probs_ref, mixed_ref) = refs[: plan.ranks_attr], refs[plan.ranks_attr :]
    order = one_hot(plan.cells, plan.grouped_from_rows())
    x_ref[...] = nn(side_by_side(tiles), order).astype(BF)
    first = attend(x_ref, normed_ref, proj_ref, probs_ref, mixed_ref, qkv_t, out_t, plan.all_attr, None)
    put_tiles(outs, nt(jnp.concatenate(first, axis=1).astype(BF), order))


def rows_back_kernel(plan, *refs):
    tiles, refs = refs[: plan.ranks_attr], refs[plan.ranks_attr :]
    (qkv, out, x_ref, normed_ref, proj_ref, probs_ref, mixed_ref), refs = refs[:7], refs[7:]
    outs, (sums_ref, grad_ref, grad_proj_ref) = refs[: plan.ranks_attr], refs[plan.ranks_attr :]
    order = one_hot(plan.cells, plan.grouped_from_rows())
    grad_ref[...] = nn(side_by_side(tiles), order).astype(BF)
    grads = attend_back(grad_ref, x_ref, proj_ref, probs_ref, grad_proj_ref, qkv, out, plan.all_attr)
    put_tiles(outs, nt(jnp.concatenate(grads, axis=1).astype(BF), order))
    put_attend_grads(sums_ref, normed_ref, grad_proj_ref, mixed_ref, grad_ref)


def cols_kernel(plan, *refs):
    count = plan.ranks_rec
    tiles, cot_tiles, refs = refs[:count], refs[count : 2 * count], refs[2 * count :]
    (train_ref, qkv, out, up, down, qkv_t, out_t, up_t), refs = refs[:8], refs[8:]
    outs, (sums_ref,), refs = refs[:count], refs[count : count + 1], refs[count + 1 :]
    x_ref, cot_ref, normed_ref, proj_ref, probs_ref, mixed_ref, second_ref = refs[:7]
    pre_ref, hidden_ref, grad_pre_ref, grad_ref, grad_proj_ref = refs[7:]
    width = max(LANES, plan.all_rec)
    order = one_hot(plan.cells, plan.grouped_from_cols())
    x_ref[...] = nn(side_by_side(tiles), order).astype(BF)
    cot_ref[...] = nn(side_by_side(cot_tiles), order).astype(BF)

    row = lax.broadcasted_iota(jnp.int32, (width, 1), 0)
    sequence, far, near, own = digits(row, (width // plan.all_rec, plan.ranks_rec, plan.ranks_attr, plan.own_rec))
    record = plan.rec * wrap(lax.axis_index("rec") - far, plan.ranks_rec) + plan.record_of(near, own)
    chosen = (record == lane_index(plan.all_rec)) & (train_ref[...] > 0)
    allowed = jnp.max(jnp.where(chosen, 1.0, 0.0), axis=1, keepdims=True) > 0.5
    asker = digits(lane_index(width), (width // plan.all_rec, plan.all_rec))[0]
    mask = jnp.where(allowed & (sequence == asker), 0.0, -1e30)

    second = attend(x_ref, normed_ref, proj_ref, probs_ref, mixed_ref, qkv_t, out_t, width, mask)
    for cols, value in zip(blocks_of(width, plan.cells), second):
        second_ref[:, cols] = value.astype(BF)

    table, root = norm(second_ref[...].astype(F32))
    normed_second = table.astype(BF)
    pre_ref[...] = nn(up_t[...], normed_second)
    grad_pre_ref[...] = nn(down[...], cot_ref[...])
    step = 32
    for start in range(0, FF, step):
        rows = slice(start, start + step)
        pre = pre_ref[rows, :]
        gate = 0.5 + 0.5 * lax.erf(pre * HALF_ROOT)
        hidden_ref[rows, :] = (pre * gate).astype(BF)
        slope = gate + pre * (jnp.exp(-0.5 * pre * pre) * BELL)
        grad_pre_ref[rows, :] = grad_pre_ref[rows, :].astype(BF).astype(F32) * slope
    grad_pre = grad_pre_ref[...].astype(BF)

    base = 6 * E
    grad_up = nt(normed_second, grad_pre)
    for tile in range(FF // LANES):
        rows = slice(base + tile * E, base + (tile + 1) * E)
        sums_ref[rows, :] = grad_up[:, tile * LANES : (tile + 1) * LANES].astype(BF)
    base = 12 * E
    grad_down = nt(hidden_ref[...], cot_ref[...])
    sums_ref[base : base + FF, :] = grad_down[:, :LANES].astype(BF)
    rest = jnp.concatenate([grad_down[: FF // 2, LANES:], grad_down[FF // 2 :, LANES:]], axis=1)
    sums_ref[base + FF : base + FF + FF // 2, :] = rest.astype(BF)

    grad_normed = nn(up[...], grad_pre).astype(BF).astype(F32)
    grad = norm_back(grad_normed, table, root) + cot_ref[...].astype(F32)
    grad_ref[...] = grad.astype(BF)
    grads = attend_back(grad_ref, x_ref, proj_ref, probs_ref, grad_proj_ref, qkv, out, width)
    put_tiles(outs, nt(jnp.concatenate(grads, axis=1).astype(BF), order))
    put_attend_grads(sums_ref, normed_ref, grad_proj_ref, mixed_ref, grad_ref)


def finish_cols_kernel(factor, sums_ref, qkv_ref, out_ref, up_ref, down_ref):
    take_attend_grads(sums_ref, 0, qkv_ref, out_ref, factor)
    base = 6 * E
    for tile in range(FF // LANES):
        rows = slice(base + tile * E, base + (tile + 1) * E)
        up_ref[:, tile * LANES : (tile + 1) * LANES] = sums_ref[rows, :].astype(F32) * factor
    base = 12 * E
    down_ref[:, :LANES] = sums_ref[base : base + FF, :].astype(F32) * factor
    rest = sums_ref[base + FF : base + FF + FF // 2, :].astype(F32) * factor
    down_ref[: FF // 2, LANES:] = rest[:, : LANES // 2]
    down_ref[FF // 2 :, LANES:] = rest[:, LANES // 2 :]


def finish_rows_kernel(factor, sums_ref, qkv_ref, out_ref):
    take_attend_grads(sums_ref, 0, qkv_ref, out_ref, factor)


def call(body, outs, scratch, *args):
    whole = pl.BlockSpec(memory_space=pltpu.VMEM)
    return pl.pallas_call(
        body,
        out_shape=[jax.ShapeDtypeStruct(shape, dtype) for shape, dtype in outs],
        in_specs=[whole] * len(args),
        out_specs=[whole] * len(outs),
        scratch_shapes=[pltpu.VMEM(shape, dtype) for shape, dtype in scratch],
        compiler_params=pltpu.CompilerParams(vmem_limit_bytes=48 * 1024 * 1024),
    )(*args)


def exchange(tiles, axis, sign):
    size = len(tiles)
    return [tiles[0]] + [
        lax.ppermute(tiles[k], axis, [(i, (i + sign * k) % size) for i in range(size)])
        for k in range(1, size)
    ]


def scatter_sum(parts, axis):
    size, own = parts.shape[0], lax.axis_index(axis)
    tiles = [
        lax.dynamic_index_in_dim(parts, (own + k) % size, 0, keepdims=False) for k in range(size)
    ]
    return sum(tile.astype(F32) for tile in exchange(tiles, axis, 1)).astype(BF)


def gather(part, axis, size):
    got = exchange([part] * size, axis, 1)
    ordered = [got[0]] + got[:0:-1]
    both = jnp.concatenate(ordered + ordered[:-1], axis=0)
    rows = part.shape[0]
    start = (size - lax.axis_index(axis)) % size * rows
    return lax.dynamic_slice_in_dim(both, start, size * rows, 0)


def total(sums, ranks_rec, ranks_attr):
    rows = sums.shape[0]
    part = scatter_sum(sums.reshape(ranks_attr, rows // ranks_attr, LANES), "attr")
    part = scatter_sum(part.reshape(ranks_rec, rows // ranks_attr // ranks_rec, LANES), "rec")
    return gather(gather(part, "rec", ranks_rec), "attr", ranks_attr)


def local(
    cells, cotangent, qkv_attr, out_attr, qkv_samp, out_samp, up_weight, down_weight, train_split
):
    ranks_rec, ranks_attr = lax.axis_size("rec"), lax.axis_size("attr")
    plan = Plan(cells, ranks_rec, ranks_attr)
    count = plan.cells
    factor = 1.0 / math.sqrt(plan.all_rec * plan.all_attr)
    row_tiles = [((E, plan.row_tile), BF)] * ranks_attr
    col_tiles = [((E, plan.col_tile), BF)] * ranks_rec
    table, wide = ((E, count), BF), ((3 * E, count), BF)

    def probs(width):
        return ((count // width * HEADS, width, width), BF)

    def kernel(body, *static):
        return functools.partial(body, plan, *static)

    rows = call(kernel(split_kernel, True), row_tiles, [((count, E), F32)], cells)
    rows = exchange(rows, "attr", 1)
    weights = (qkv_attr, out_attr, qkv_samp, out_samp, up_weight)
    qkv_attr_t, out_attr_t, qkv_samp_t, out_samp_t, up_t = call(
        functools.partial(turn_kernel, len(weights)), [(w.shape[::-1], BF) for w in weights], [], *weights
    )
    cot = call(kernel(split_kernel, False), col_tiles, [((count, E), F32)], cotangent)
    cot = exchange(cot, "rec", 1)

    got = call(
        kernel(rows_forward_kernel),
        row_tiles + [table, table, wide, probs(plan.all_attr), table],
        [],
        *rows,
        qkv_attr_t,
        out_attr_t,
    )
    first, saved = got[:ranks_attr], got[ranks_attr:]
    first = exchange(first, "attr", -1)
    cols = exchange(call(kernel(to_cols_kernel), col_tiles, [], *first), "rec", 1)

    width = max(LANES, plan.all_rec)
    sums_rows = 6 * E
    got = call(
        kernel(cols_kernel),
        col_tiles + [((3 * sums_rows, LANES), BF)],
        [table, table, table, wide, probs(width), table, table]
        + [((FF, count), F32), ((FF, count), BF), ((FF, count), F32), table, wide],
        *cols,
        *cot,
        train_split.reshape(1, -1),
        qkv_samp,
        out_samp,
        up_weight,
        down_weight,
        qkv_samp_t,
        out_samp_t,
        up_t,
    )
    grads, sums = exchange(got[:ranks_rec], "rec", -1), got[ranks_rec]
    grads = exchange(call(kernel(to_rows_kernel), row_tiles, [], *grads), "attr", 1)

    got = call(
        kernel(rows_back_kernel),
        row_tiles + [((sums_rows, LANES), BF)],
        [table, wide],
        *grads,
        qkv_attr,
        out_attr,
        *saved,
    )
    grads, row_sums = exchange(got[:ranks_attr], "attr", -1), got[ranks_attr]
    (grad_cells,) = call(kernel(join_kernel), [(cells.shape, BF)], [((count, E), F32)], *grads)

    sums = total(sums, ranks_rec, ranks_attr)
    grad_qkv_samp, grad_out_samp, grad_up, grad_down = call(
        functools.partial(finish_cols_kernel, factor),
        [((E, 3 * E), F32), ((E, E), F32), ((E, FF), F32), ((FF, E), F32)],
        [],
        sums,
    )
    row_sums = total(row_sums, ranks_rec, ranks_attr)
    grad_qkv_attr, grad_out_attr = call(
        functools.partial(finish_rows_kernel, factor), [((E, 3 * E), F32), ((E, E), F32)], [], row_sums
    )
    return (grad_cells, grad_qkv_attr, grad_out_attr, grad_qkv_samp, grad_out_samp, grad_up, grad_down)


def solution(mesh):
    own = P(("groups", "rec"), "attr")
    in_specs = (own, own) + (P(),) * 6 + (P("groups"),)
    out_specs = (own,) + (P("groups", None),) * 6
    return jax.shard_map(local, mesh=mesh, in_specs=in_specs, out_specs=out_specs, check_vma=False)
```

```python
import functools
import math
from typing import NamedTuple

import jax
import jax.numpy as jnp
from jax import lax
from jax.experimental import pallas as pl
from jax.experimental.pallas import tpu as pltpu
from jax.sharding import PartitionSpec as P

E = 192
HEADS = 6
FF = 768
HEAD = E // HEADS
LANES = 128
VMEM = 24 * 1024 * 1024
BF = jnp.bfloat16
F32 = jnp.float32
EXP2 = math.log2(math.e) / math.sqrt(HEAD)
SCALE = 1.0 / math.sqrt(HEAD)
HALF_ROOT = math.sqrt(0.5)
BELL = 1.0 / math.sqrt(2.0 * math.pi)


def nn(left, right):
    return lax.dot_general(left, right, (((1,), (0,)), ((), ())), preferred_element_type=F32)


def nt(left, right):
    return lax.dot_general(left, right, (((1,), (1,)), ((), ())), preferred_element_type=F32)


def tn(left, right):
    return lax.dot_general(left, right, (((0,), (0,)), ((), ())), preferred_element_type=F32)


def digits(index, sizes):
    out = []
    for size in reversed(sizes):
        if size & (size - 1) == 0:
            out.append(index & (size - 1))
            index = index >> (size.bit_length() - 1)
        else:
            out.append(lax.rem(index, size))
            index = lax.div(index, size)
    return out[::-1]


def wrap(index, size):
    return digits(index + size, (size,))[0]


def one_hot(rows, source):
    own = lax.broadcasted_iota(jnp.int32, (rows, source.shape[1]), 0)
    return jnp.where(own == source, 1.0, 0.0).astype(BF)


def lane_index(size):
    return lax.broadcasted_iota(jnp.int32, (1, size), 1)


def eye(size):
    return one_hot(size, lane_index(size))


def side_by_side(refs):
    return jnp.concatenate([ref[...] for ref in refs], axis=1)


def put_tiles(refs, table):
    width = refs[0].shape[1]
    for position, ref in enumerate(refs):
        ref[...] = table[:, position * width : (position + 1) * width].astype(ref.dtype)


class Plan:
    def __init__(self, cells, ranks_rec, ranks_attr):
        self.ranks_rec, self.ranks_attr = ranks_rec, ranks_attr
        self.rec, self.attr = cells.shape[0], cells.shape[1] // E
        self.cells = self.rec * self.attr
        self.own_rec = self.rec // ranks_attr
        self.own_attr = self.attr // ranks_rec
        self.all_rec = self.rec * ranks_rec
        self.all_attr = self.attr * ranks_attr
        self.row_tile = self.own_rec * self.attr
        self.col_tile = self.rec * self.own_attr

    def row_digits(self, index):
        return digits(index, (self.ranks_attr, self.own_rec, self.attr))

    def col_digits(self, index):
        return digits(index, (self.ranks_rec, self.ranks_attr, self.own_rec, self.own_attr))

    def record_of(self, step, own):
        return self.own_rec * wrap(step + lax.axis_index("attr"), self.ranks_attr) + own

    def attr_of(self, step, own):
        return self.own_attr * wrap(step + lax.axis_index("rec"), self.ranks_rec) + own

    def rows_from_owned(self):
        step, own, attr = self.row_digits(lane_index(self.cells))
        return attr * self.rec + self.record_of(step, own)

    def cols_from_owned(self):
        far, near, own, attr = self.col_digits(lane_index(self.cells))
        return self.attr_of(far, attr) * self.rec + self.record_of(near, own)

    def cols_from_rows(self):
        far, near, own, attr = self.col_digits(lane_index(self.cells))
        return (near * self.own_rec + own) * self.attr + self.attr_of(far, attr)

    def grouped_from_rows(self):
        own, step, attr = digits(lane_index(self.cells), (self.own_rec, self.ranks_attr, self.attr))
        return (step * self.own_rec + own) * self.attr + attr

    def grouped_from_cols(self):
        attr, place = digits(lane_index(self.cells), (self.own_attr, self.all_rec))
        return place * self.own_attr + attr


def split_kernel(plan, to_rows, wait, table_ref, *refs):
    wait()
    outs, rows = refs[:-1], refs[-1]
    for pair in range(plan.attr // 2):
        both = table_ref[:, 2 * E * pair : 2 * E * (pair + 1)].astype(F32)
        for side in range(2):
            start = (2 * pair + side) * plan.rec
            rows[start : start + plan.rec, :] = both[:, side * E : (side + 1) * E]
    turned = nt(eye(E), rows[...].astype(BF)).astype(BF)
    source = plan.rows_from_owned() if to_rows else plan.cols_from_owned()
    put_tiles(outs, nn(turned, one_hot(plan.cells, source)))


def join_kernel(plan, wait, *refs):
    tiles, out_ref, rows = refs[:-2], refs[-2], refs[-1]
    rows[...] = nt(one_hot(plan.cells, plan.rows_from_owned()), side_by_side(tiles))
    for pair in range(plan.attr // 2):
        start = 2 * pair * plan.rec
        both = [rows[start + side * plan.rec : start + (side + 1) * plan.rec, :] for side in range(2)]
        out_ref[:, 2 * E * pair : 2 * E * (pair + 1)] = jnp.concatenate(both, axis=1).astype(BF)


def to_cols_kernel(plan, wait, *refs):
    tiles, outs = refs[: plan.ranks_attr], refs[plan.ranks_attr :]
    put_tiles(outs, nn(side_by_side(tiles), one_hot(plan.cells, plan.cols_from_rows())))


def to_rows_kernel(plan, wait, *refs):
    tiles, outs = refs[: plan.ranks_rec], refs[plan.ranks_rec :]
    put_tiles(outs, nt(side_by_side(tiles), one_hot(plan.cells, plan.cols_from_rows())))


def split_turn_kernel(plan, count, wait, table_ref, *refs):
    weights, refs = refs[:count], refs[count:]
    split_kernel(plan, False, wait, table_ref, *refs[: plan.ranks_rec], refs[-1])
    for source, target in zip(weights, refs[plan.ranks_rec : -1]):
        target[...] = source[...].astype(F32).T.astype(BF)


def norm(table):
    center = table - jnp.mean(table, axis=0, keepdims=True)
    spread = jnp.mean(center * center, axis=0, keepdims=True)
    root = lax.rsqrt(spread + 1e-05)
    return center * root, root


def norm_back(grad, normed, root):
    along = jnp.mean(grad * normed, axis=0, keepdims=True)
    return root * (grad - jnp.mean(grad, axis=0, keepdims=True) - normed * along)


def blocks_of(width, total):
    return [slice(start, start + width) for start in range(0, total, width)]


def heads_of(ref, part, head, cols):
    start = part * E + head * HEAD
    return ref[start : start + HEAD, cols]


def attend(x_ref, normed_ref, proj_ref, probs_ref, mixed_ref, qkv_t, out_t, width, mask):
    results = []
    for place, cols in enumerate(blocks_of(width, x_ref.shape[1])):
        table = x_ref[:, cols].astype(F32)
        normed_ref[:, cols] = norm(table)[0].astype(BF)
        proj_ref[:, cols] = nn(qkv_t[...], normed_ref[:, cols]).astype(BF)
        for head in range(HEADS):
            query, key, value = (heads_of(proj_ref, part, head, cols) for part in range(3))
            scores = tn(key, query)
            if mask is not None:
                scores = scores + mask
            expo = jnp.exp2((scores - jnp.max(scores, axis=0, keepdims=True)) * EXP2)
            probs = (expo * (1.0 / jnp.sum(expo, axis=0, keepdims=True))).astype(BF)
            probs_ref[place * HEADS + head] = probs
            mixed_ref[head * HEAD : (head + 1) * HEAD, cols] = nn(value, probs).astype(BF)
        results.append(x_ref[:, cols].astype(F32) + nn(out_t[...], mixed_ref[:, cols]))
    return results


def attend_back(grad_ref, x_ref, proj_ref, probs_ref, grad_proj_ref, qkv, out, width):
    results = []
    for place, cols in enumerate(blocks_of(width, x_ref.shape[1])):
        grad_mixed = nn(out[...], grad_ref[:, cols]).astype(BF)
        for head in range(HEADS):
            query, key, value = (heads_of(proj_ref, part, head, cols) for part in range(3))
            grad_head = grad_mixed[head * HEAD : (head + 1) * HEAD]
            probs = probs_ref[place * HEADS + head]
            grad_probs = tn(value, grad_head).astype(BF).astype(F32)
            wide = probs.astype(F32)
            moved = grad_probs * wide
            grad_scores = (moved - wide * jnp.sum(moved, axis=0, keepdims=True)) * SCALE
            grad_scores = grad_scores.astype(BF)
            for part, value_of in enumerate(
                (nn(key, grad_scores), nt(query, grad_scores), nt(grad_head, probs))
            ):
                start = part * E + head * HEAD
                grad_proj_ref[start : start + HEAD, cols] = value_of.astype(BF)
        grad_normed = nn(qkv[...], grad_proj_ref[:, cols]).astype(BF).astype(F32)
        normed, root = norm(x_ref[:, cols].astype(F32))
        results.append(norm_back(grad_normed, normed, root) + grad_ref[:, cols].astype(F32))
    return results


def put_halves(bit, sums_ref, keep_ref, send_ref):
    rows, mine = keep_ref.shape[0], has_bit("attr", bit)
    for ref, half in ((keep_ref, mine), (send_ref, 1 - mine)):
        ref[...] = sums_ref[pl.ds(pl.multiple_of(half * rows, rows), rows), :]


def put_attend_grads(out_ref, normed_ref, grad_proj_ref, mixed_ref, grad_ref):
    qkv = nt(normed_ref[...], grad_proj_ref[...])
    out = nt(mixed_ref[...], grad_ref[...])
    whole = 3 * E // LANES
    for tile in range(whole):
        out_ref[tile * E : (tile + 1) * E, :] = qkv[:, tile * LANES : (tile + 1) * LANES].astype(BF)
    mixed = jnp.concatenate([qkv[:, whole * LANES :], out[:, LANES:]], axis=1)
    out_ref[whole * E : (whole + 1) * E, :] = mixed.astype(BF)
    out_ref[(whole + 1) * E : (whole + 2) * E, :] = out[:, :LANES].astype(BF)


def take_attend_grads(in_ref, first, qkv_ref, out_ref, factor):
    whole = 3 * E // LANES

    def tile(number):
        return in_ref[first + number * E : first + (number + 1) * E, :].astype(F32) * factor

    for number in range(whole):
        qkv_ref[:, number * LANES : (number + 1) * LANES] = tile(number)
    mixed = tile(whole)
    qkv_ref[:, whole * LANES :] = mixed[:, : LANES // 2]
    out_ref[:, :LANES] = tile(whole + 1)
    out_ref[:, LANES:] = mixed[:, LANES // 2 :]


def rows_forward_kernel(plan, wait, *refs):
    tiles, refs = refs[: plan.ranks_attr], refs[plan.ranks_attr :]
    (qkv_t, out_t), refs = refs[:2], refs[2:]
    outs, (x_ref, normed_ref, proj_ref, probs_ref, mixed_ref) = refs[: plan.ranks_attr], refs[plan.ranks_attr :]
    order = one_hot(plan.cells, plan.grouped_from_rows())
    x_ref[...] = nn(side_by_side(tiles), order).astype(BF)
    first = attend(x_ref, normed_ref, proj_ref, probs_ref, mixed_ref, qkv_t, out_t, plan.all_attr, None)
    put_tiles(outs, nt(jnp.concatenate(first, axis=1).astype(BF), order))


def rows_back_kernel(plan, wait, *refs):
    tiles, refs = refs[: plan.ranks_attr], refs[plan.ranks_attr :]
    (qkv, out, x_ref, normed_ref, proj_ref, probs_ref, mixed_ref), refs = refs[:7], refs[7:]
    outs, refs = refs[: plan.ranks_attr], refs[plan.ranks_attr :]
    keep_ref, send_ref, sums_ref, grad_ref, grad_proj_ref = refs
    order = one_hot(plan.cells, plan.grouped_from_rows())
    grad_ref[...] = nn(side_by_side(tiles), order).astype(BF)
    wait()
    grads = attend_back(grad_ref, x_ref, proj_ref, probs_ref, grad_proj_ref, qkv, out, plan.all_attr)
    put_tiles(outs, nt(jnp.concatenate(grads, axis=1).astype(BF), order))
    put_attend_grads(sums_ref, normed_ref, grad_proj_ref, mixed_ref, grad_ref)
    put_halves(bits_of("attr")[0], sums_ref, keep_ref, send_ref)


def cols_kernel(plan, wait, *refs):
    count = plan.ranks_rec
    tiles, cot_tiles, refs = refs[:count], refs[count : 2 * count], refs[2 * count :]
    (train_ref, qkv, out, up, down, qkv_t, out_t, up_t), refs = refs[:8], refs[8:]
    outs, (sums_ref,), refs = refs[:count], refs[count : count + 1], refs[count + 1 :]
    x_ref, cot_ref, normed_ref, proj_ref, probs_ref, mixed_ref, second_ref = refs[:7]
    pre_ref, hidden_ref, grad_pre_ref, grad_ref, grad_proj_ref = refs[7:]
    width = max(LANES, plan.all_rec)
    order = one_hot(plan.cells, plan.grouped_from_cols())
    x_ref[...] = nn(side_by_side(tiles), order).astype(BF)
    wait()
    cot_ref[...] = nn(side_by_side(cot_tiles), order).astype(BF)

    row = lax.broadcasted_iota(jnp.int32, (width, 1), 0)
    sequence, far, near, own = digits(row, (width // plan.all_rec, plan.ranks_rec, plan.ranks_attr, plan.own_rec))
    record = plan.rec * wrap(lax.axis_index("rec") - far, plan.ranks_rec) + plan.record_of(near, own)
    chosen = (record == lane_index(plan.all_rec)) & (train_ref[...] > 0)
    allowed = jnp.max(jnp.where(chosen, 1.0, 0.0), axis=1, keepdims=True) > 0.5
    asker = digits(lane_index(width), (width // plan.all_rec, plan.all_rec))[0]
    mask = jnp.where(allowed & (sequence == asker), 0.0, -1e30)

    second = attend(x_ref, normed_ref, proj_ref, probs_ref, mixed_ref, qkv_t, out_t, width, mask)
    for cols, value in zip(blocks_of(width, plan.cells), second):
        second_ref[:, cols] = value.astype(BF)

    table, root = norm(second_ref[...].astype(F32))
    normed_second = table.astype(BF)
    pre_ref[...] = nn(up_t[...], normed_second)
    grad_pre_ref[...] = nn(down[...], cot_ref[...])
    step = 32
    for start in range(0, FF, step):
        rows = slice(start, start + step)
        pre = pre_ref[rows, :]
        gate = 0.5 + 0.5 * lax.erf(pre * HALF_ROOT)
        hidden_ref[rows, :] = (pre * gate).astype(BF)
        slope = gate + pre * (jnp.exp(-0.5 * pre * pre) * BELL)
        grad_pre_ref[rows, :] = grad_pre_ref[rows, :].astype(BF).astype(F32) * slope
    grad_pre = grad_pre_ref[...].astype(BF)

    for base, grad_weight in (
        (6 * E, nt(normed_second, grad_pre)),
        (12 * E, nt(cot_ref[...], hidden_ref[...])),
    ):
        for tile in range(FF // LANES):
            rows = slice(base + tile * E, base + (tile + 1) * E)
            sums_ref[rows, :] = grad_weight[:, tile * LANES : (tile + 1) * LANES].astype(BF)

    grad_normed = nn(up[...], grad_pre).astype(BF).astype(F32)
    grad = norm_back(grad_normed, table, root) + cot_ref[...].astype(F32)
    grad_ref[...] = grad.astype(BF)
    grads = attend_back(grad_ref, x_ref, proj_ref, probs_ref, grad_proj_ref, qkv, out, width)
    put_tiles(outs, nt(jnp.concatenate(grads, axis=1).astype(BF), order))
    put_attend_grads(sums_ref, normed_ref, grad_proj_ref, mixed_ref, grad_ref)


def finish_cols_kernel(factor, bits, wait, *refs):
    parts, (qkv_ref, out_ref, up_ref, down_ref, sums_ref) = refs[:-5], refs[-5:]
    lay_out(bits, parts, sums_ref)
    take_attend_grads(sums_ref, 0, qkv_ref, out_ref, factor)
    for base, ref in ((6 * E, up_ref), (12 * E, down_ref)):
        for tile in range(FF // LANES):
            rows = slice(base + tile * E, base + (tile + 1) * E)
            ref[:, tile * LANES : (tile + 1) * LANES] = sums_ref[rows, :].astype(F32) * factor


def finish_rows_kernel(factor, bits, wait, *refs):
    parts, (qkv_ref, out_ref, sums_ref) = refs[:-3], refs[-3:]
    lay_out(bits, parts, sums_ref)
    take_attend_grads(sums_ref, 0, qkv_ref, out_ref, factor)


class Far(NamedTuple):
    array: jax.Array


class Near(NamedTuple):
    array: jax.Array


def call(body, outs, scratch, *args, after=()):
    far = [n for n, arg in enumerate(args) if isinstance(arg, Far)]
    n_in, n_after, n_out, n_far = len(args), len(after), len(outs), len(far)
    whole, anywhere = pl.BlockSpec(memory_space=pltpu.VMEM), pl.BlockSpec(memory_space=pl.ANY)
    hbm = pl.BlockSpec(memory_space=pltpu.HBM)

    def kernel(*refs):
        given, refs = list(refs[:n_in]), refs[n_in + n_after :]
        copies = []
        if far:
            held, sems, refs = refs[-1 - n_far : -1], refs[-1], refs[: -1 - n_far]
            for order, (number, ref) in enumerate(zip(far, held)):
                copies.append(pltpu.make_async_copy(given[number], ref, sems.at[order]))
                given[number] = ref
        for copy in copies:
            copy.start()

        def wait():
            for copy in copies:
                copy.wait()

        body(wait, *given, *refs)

    arrays = []
    for arg in args:
        space = {Far: pltpu.HBM, Near: pltpu.VMEM}.get(type(arg))
        arrays.append(arg if space is None else pltpu.with_memory_space_constraint(arg.array, space))
    held = [pltpu.VMEM(arrays[n].shape, arrays[n].dtype) for n in far]
    return pl.pallas_call(
        kernel,
        out_shape=[
            (pltpu.VMEM if out[2:] else jax.ShapeDtypeStruct)(out[0], out[1]) for out in outs
        ],
        in_specs=[hbm if isinstance(arg, Far) else whole for arg in args] + [anywhere] * n_after,
        out_specs=[whole] * n_out,
        scratch_shapes=[pltpu.VMEM(shape, dtype) for shape, dtype in scratch]
        + held
        + ([pltpu.SemaphoreType.DMA((n_far,))] if far else []),
        compiler_params=pltpu.CompilerParams(vmem_limit_bytes=VMEM),
    )(*arrays, *after)


def exchange(tiles, axis, sign):
    size = len(tiles)
    return [tiles[0]] + [
        lax.ppermute(tiles[k], axis, [(i, (i + sign * k) % size) for i in range(size)])
        for k in range(1, size)
    ]


def swap(part, axis, bit):
    size = lax.axis_size(axis)
    return lax.ppermute(part, axis, [(i, i ^ bit) for i in range(size)])


def has_bit(axis, bit):
    return digits(lax.axis_index(axis) // bit, (2,))[0]


def halve_kernel(bit, wait, *refs):
    parts, (keep, send) = refs[:-2], refs[-2:]
    rows, mine = keep.shape[0], has_bit("attr", bit)
    for ref, half in ((keep, mine), (send, 1 - mine)):
        place = pl.ds(pl.multiple_of(half * rows, rows), rows)
        ref[...] = sum(part[place, :].astype(F32) for part in parts).astype(BF)


def add_kernel(wait, *refs):
    refs[-1][...] = sum(part[...].astype(F32) for part in refs[:-1]).astype(BF)


def lay_out(bits, parts, rows_ref):
    rows = parts[0].shape[0]
    for number, ref in enumerate(parts):
        place = 0
        for order, bit in enumerate(bits):
            own = has_bit("attr", bit)
            place = place * 2 + (1 - own if number >> order & 1 else own)
        rows_ref[pl.ds(pl.multiple_of(place * rows, rows), rows), :] = ref[...]


def bits_of(axis):
    return [1 << n for n in range(lax.axis_size(axis).bit_length() - 1)]


class Total:
    def __init__(self, *parts):
        self.parts, self.rows = list(parts), parts[0].shape[0]

    def halve(self, bit, after=()):
        self.rows //= 2
        keep, send = call(
            functools.partial(halve_kernel, bit), [((self.rows, LANES), BF)] * 2, [], *self.parts, after=after
        )
        self.parts = [keep, swap(send, "attr", bit)]
        return [keep]

    def add(self, bit=0, after=()):
        (part,) = call(add_kernel, [((self.rows, LANES), BF)], [], *self.parts, after=after)
        self.parts = [part] + ([swap(part, "rec", bit)] if bit else [])
        return [part]

    def spread(self, bits):
        done = {0: self.parts[0]}
        for order, bit in reversed(list(enumerate(bits))):
            done.update({number | 1 << order: swap(part, "attr", bit) for number, part in sorted(done.items())})
        return [done[number] for number in sorted(done)]


def padded(rows):
    devices = lax.axis_size("attr")
    return -(-rows // (16 * devices)) * 16 * devices


def local(
    cells, cotangent, qkv_attr, out_attr, qkv_samp, out_samp, up_weight, down_weight, train_split
):
    ranks_rec, ranks_attr = lax.axis_size("rec"), lax.axis_size("attr")
    plan = Plan(cells, ranks_rec, ranks_attr)
    count = plan.cells
    factor = 1.0 / math.sqrt(plan.all_rec * plan.all_attr)
    row_tiles = [((E, plan.row_tile), BF)] * ranks_attr
    col_tiles = [((E, plan.col_tile), BF)] * ranks_rec
    table, wide = ((E, count), BF), ((3 * E, count), BF)

    def probs(width):
        return ((count // width * HEADS, width, width), BF)

    def kernel(body, *static):
        return functools.partial(body, plan, *static)

    rows = call(kernel(split_kernel, True), row_tiles, [((count, E), F32)], Far(cells))
    rows = exchange(rows, "attr", 1)
    weights = (qkv_attr, out_attr, qkv_samp, out_samp, up_weight, down_weight.T)
    got = call(
        kernel(split_turn_kernel, len(weights)),
        col_tiles + [(w.shape[::-1], BF, "near") for w in weights],
        [((count, E), F32)],
        Far(cotangent),
        *[Far(w) for w in weights],
        after=[rows[0]],
    )
    cot = exchange(got[:ranks_rec], "rec", 1)
    turned = [Near(w) for w in got[ranks_rec:]]

    got = call(
        kernel(rows_forward_kernel),
        row_tiles + [out + ("near",) for out in (table, table, wide, probs(plan.all_attr), table)],
        [],
        *rows,
        *turned[:2],
    )
    first, saved = got[:ranks_attr], [Near(array) for array in got[ranks_attr:]]
    first = exchange(first, "attr", -1)
    cols = exchange(call(kernel(to_cols_kernel), col_tiles, [], *first), "rec", 1)

    width = max(LANES, plan.all_rec)
    rows_sums, cols_sums = padded(6 * E), padded(18 * E)
    got = call(
        kernel(cols_kernel),
        col_tiles + [((cols_sums, LANES), BF)],
        [table, table, table, wide, probs(width), table, table]
        + [((FF, count), F32), ((FF, count), BF), ((FF, count), F32), table, wide],
        *cols,
        *cot,
        train_split.reshape(1, -1),
        Far(qkv_samp),
        Far(out_samp),
        Far(up_weight),
        turned[5],
        turned[2],
        turned[3],
        turned[4],
    )
    near, far = bits_of("attr"), bits_of("rec")
    grads, sums = exchange(got[:ranks_rec], "rec", -1), Total(got[ranks_rec])
    mark = sums.halve(near[0])
    for bit in near[1:]:
        mark = sums.halve(bit, after=mark)
    grads = exchange(call(kernel(to_rows_kernel), row_tiles, [], *grads, after=mark), "attr", 1)
    mark = sums.add(far[0])

    got = call(
        kernel(rows_back_kernel),
        row_tiles + [((rows_sums // 2, LANES), BF)] * 2,
        [((rows_sums, LANES), BF), table, wide],
        *grads,
        Far(qkv_attr),
        Far(out_attr),
        *saved,
        after=mark,
    )
    grads, row_sums = exchange(got[:ranks_attr], "attr", -1), Total(*got[ranks_attr:])
    row_sums.parts[1] = swap(row_sums.parts[1], "attr", near[0])
    mark = []
    for bit in near[1:]:
        mark = row_sums.halve(bit, after=mark)
    for bit in far[1:]:
        mark = sums.add(bit, after=mark)
    mark = row_sums.add(far[0], after=mark)
    (grad_cells,) = call(kernel(join_kernel), [(cells.shape, BF)], [((count, E), F32)], *grads, after=mark)
    mark = [grad_cells]
    for bit in far[1:]:
        mark = row_sums.add(bit, after=mark)
    mark = sums.add(after=mark)
    parts = sums.spread(near)
    row_sums.add(after=mark)
    row_parts = row_sums.spread(near)
    grad_qkv_samp, grad_out_samp, grad_up, grad_down = call(
        functools.partial(finish_cols_kernel, factor, near),
        [((E, 3 * E), F32), ((E, E), F32), ((E, FF), F32), ((E, FF), F32)],
        [((cols_sums, LANES), BF)],
        *parts,
    )
    grad_qkv_attr, grad_out_attr = call(
        functools.partial(finish_rows_kernel, factor, near),
        [((E, 3 * E), F32), ((E, E), F32)],
        [((rows_sums, LANES), BF)],
        *row_parts,
    )
    grad_down = grad_down.T
    return (grad_cells, grad_qkv_attr, grad_out_attr, grad_qkv_samp, grad_out_samp, grad_up, grad_down)


def solution(mesh):
    own = P(("groups", "rec"), "attr")
    in_specs = (own, own) + (P(),) * 6 + (P("groups"),)
    out_specs = (own,) + (P("groups", None),) * 6
    return jax.shard_map(local, mesh=mesh, in_specs=in_specs, out_specs=out_specs, check_vma=False)
```

```python
import functools
import math
from typing import NamedTuple

import jax
import jax.numpy as jnp
from jax import lax
from jax.experimental import pallas as pl
from jax.experimental.pallas import tpu as pltpu
from jax.sharding import PartitionSpec as P

E = 192
HEADS = 6
FF = 768
HEAD = E // HEADS
LANES = 128
VMEM = 24 * 1024 * 1024
BF = jnp.bfloat16
F32 = jnp.float32
EXP2 = math.log2(math.e) / math.sqrt(HEAD)
SCALE = 1.0 / math.sqrt(HEAD)
HALF_ROOT = math.sqrt(0.5)
BELL_EXP2 = -0.5 * math.log2(math.e)
BELL = 1.0 / math.sqrt(2.0 * math.pi)


def nn(left, right):
    return lax.dot_general(left, right, (((1,), (0,)), ((), ())), preferred_element_type=F32)


def nt(left, right):
    return lax.dot_general(left, right, (((1,), (1,)), ((), ())), preferred_element_type=F32)


def tn(left, right):
    return lax.dot_general(left, right, (((0,), (0,)), ((), ())), preferred_element_type=F32)


def digits(index, sizes):
    out = []
    for size in reversed(sizes):
        if size & (size - 1) == 0:
            out.append(index & (size - 1))
            index = index >> (size.bit_length() - 1)
        else:
            out.append(lax.rem(index, size))
            index = lax.div(index, size)
    return out[::-1]


def wrap(index, size):
    return digits(index + size, (size,))[0]


def one_hot(rows, source):
    own = lax.broadcasted_iota(jnp.int32, (rows, source.shape[1]), 0)
    return jnp.where(own == source, 1.0, 0.0).astype(BF)


def lane_index(size):
    return lax.broadcasted_iota(jnp.int32, (1, size), 1)


def eye(size):
    return one_hot(size, lane_index(size))


def side_by_side(refs):
    return jnp.concatenate([ref[...] for ref in refs], axis=1)


def put_tiles(refs, table):
    width = refs[0].shape[1]
    for position, ref in enumerate(refs):
        ref[...] = table[:, position * width : (position + 1) * width].astype(ref.dtype)


class Plan:
    def __init__(self, cells, ranks_rec, ranks_attr):
        self.ranks_rec, self.ranks_attr = ranks_rec, ranks_attr
        self.rec, self.attr = cells.shape[0], cells.shape[1] // E
        self.cells = self.rec * self.attr
        self.own_rec = self.rec // ranks_attr
        self.own_attr = self.attr // ranks_rec
        self.all_rec = self.rec * ranks_rec
        self.all_attr = self.attr * ranks_attr
        self.row_tile = self.own_rec * self.attr
        self.col_tile = self.rec * self.own_attr

    def row_digits(self, index):
        return digits(index, (self.ranks_attr, self.own_rec, self.attr))

    def col_digits(self, index):
        return digits(index, (self.ranks_rec, self.ranks_attr, self.own_rec, self.own_attr))

    def record_of(self, step, own):
        return self.own_rec * wrap(step + lax.axis_index("attr"), self.ranks_attr) + own

    def attr_of(self, step, own):
        return self.own_attr * wrap(step + lax.axis_index("rec"), self.ranks_rec) + own

    def rows_from_owned(self):
        step, own, attr = self.row_digits(lane_index(self.cells))
        return attr * self.rec + self.record_of(step, own)

    def cols_from_owned(self):
        far, near, own, attr = self.col_digits(lane_index(self.cells))
        return self.attr_of(far, attr) * self.rec + self.record_of(near, own)

    def cols_from_rows(self):
        far, near, own, attr = self.col_digits(lane_index(self.cells))
        return (near * self.own_rec + own) * self.attr + self.attr_of(far, attr)

    def grouped_from_rows(self):
        own, step, attr = digits(lane_index(self.cells), (self.own_rec, self.ranks_attr, self.attr))
        return (step * self.own_rec + own) * self.attr + attr

    def grouped_from_cols(self):
        attr, place = digits(lane_index(self.cells), (self.own_attr, self.all_rec))
        return place * self.own_attr + attr


def split_kernel(plan, to_rows, wait, table_ref, *refs):
    wait()
    outs, rows = refs[:-1], refs[-1]
    for pair in range(plan.attr // 2):
        both = table_ref[:, 2 * E * pair : 2 * E * (pair + 1)].astype(F32)
        for side in range(2):
            start = (2 * pair + side) * plan.rec
            rows[start : start + plan.rec, :] = both[:, side * E : (side + 1) * E]
    turned = nt(eye(E), rows[...].astype(BF)).astype(BF)
    source = plan.rows_from_owned() if to_rows else plan.cols_from_owned()
    put_tiles(outs, nn(turned, one_hot(plan.cells, source)))


def join_kernel(plan, wait, *refs):
    tiles, out_ref, rows = refs[:-2], refs[-2], refs[-1]
    rows[...] = nt(one_hot(plan.cells, plan.rows_from_owned()), side_by_side(tiles))
    for pair in range(plan.attr // 2):
        start = 2 * pair * plan.rec
        both = [rows[start + side * plan.rec : start + (side + 1) * plan.rec, :] for side in range(2)]
        out_ref[:, 2 * E * pair : 2 * E * (pair + 1)] = jnp.concatenate(both, axis=1).astype(BF)


def to_cols_kernel(plan, wait, *refs):
    tiles, outs = refs[: plan.ranks_attr], refs[plan.ranks_attr :]
    put_tiles(outs, nn(side_by_side(tiles), one_hot(plan.cells, plan.cols_from_rows())))


def to_rows_kernel(plan, wait, *refs):
    tiles, outs = refs[: plan.ranks_rec], refs[plan.ranks_rec :]
    put_tiles(outs, nt(side_by_side(tiles), one_hot(plan.cells, plan.cols_from_rows())))


def split_turn_kernel(plan, count, wait, table_ref, *refs):
    weights, refs = refs[:count], refs[count:]
    split_kernel(plan, False, wait, table_ref, *refs[: plan.ranks_rec], refs[-1])
    for source, target in zip(weights, refs[plan.ranks_rec : -1]):
        target[...] = source[...].astype(F32).T.astype(BF)


def norm(table):
    center = table - jnp.mean(table, axis=0, keepdims=True)
    spread = jnp.mean(center * center, axis=0, keepdims=True)
    root = lax.rsqrt(spread + 1e-05)
    return center * root, root


def norm_back(grad, normed, root):
    along = jnp.mean(grad * normed, axis=0, keepdims=True)
    return root * (grad - jnp.mean(grad, axis=0, keepdims=True) - normed * along)


def blocks_of(width, total):
    return [slice(start, start + width) for start in range(0, total, width)]


def heads_of(ref, part, head, cols):
    start = part * E + head * HEAD
    return ref[start : start + HEAD, cols]


def staged(count, *stages):
    held = {}
    for step in range(count + len(stages) - 1):
        for lag, stage in enumerate(stages):
            unit = step - lag
            if 0 <= unit < count:
                held[unit] = stage(unit, held.get(unit))
                if lag == len(stages) - 1:
                    del held[unit]


def units_of(total, width):
    step = min(2 * LANES, width)
    return [
        (place, head, start, step, start == 0, start + step == width)
        for place in range(total // width)
        for head in range(HEADS)
        for start in range(0, width, step)
    ]


def attend(x_ref, normed_ref, proj_ref, probs_ref, mixed_ref, qkv_t, out_t, width, mask_ref):
    total = x_ref.shape[1]
    for cols in blocks_of(2 * LANES, total):
        normed_ref[:, cols] = norm(x_ref[:, cols].astype(F32))[0].astype(BF)
    for cols in blocks_of(2 * LANES, total):
        proj_ref[:, cols] = nn(qkv_t[...], normed_ref[:, cols]).astype(BF)
    units = units_of(total, width)

    def score(unit, _):
        place, head, start, step, _, _ = units[unit]
        cols = slice(place * width + start, place * width + start + step)
        keys = slice(place * width, (place + 1) * width)
        return tn(heads_of(proj_ref, 1, head, keys), heads_of(proj_ref, 0, head, cols))

    def weigh(unit, scores):
        place, head, start, step, _, _ = units[unit]
        if mask_ref is not None:
            scores = scores + mask_ref[:, start : start + step]
        expo = jnp.exp2((scores - jnp.max(scores, axis=0, keepdims=True)) * EXP2)
        probs = (expo * (1.0 / jnp.sum(expo, axis=0, keepdims=True))).astype(BF)
        probs_ref[place * HEADS + head, :, start : start + step] = probs
        return probs

    def mix(unit, probs):
        place, head, start, step, _, _ = units[unit]
        value = heads_of(proj_ref, 2, head, slice(place * width, (place + 1) * width))
        cols = slice(place * width + start, place * width + start + step)
        mixed_ref[head * HEAD : (head + 1) * HEAD, cols] = nn(value, probs).astype(BF)

    staged(len(units), score, weigh, mix)
    return [
        x_ref[:, cols].astype(F32) + nn(out_t[...], mixed_ref[:, cols])
        for cols in blocks_of(2 * LANES, total)
    ]


def attend_back(grad_ref, x_ref, proj_ref, probs_ref, grad_proj_ref, grad_mixed_ref, qkv, out, width):
    total = x_ref.shape[1]
    for cols in blocks_of(2 * LANES, total):
        grad_mixed_ref[:, cols] = nn(out[...], grad_ref[:, cols]).astype(BF)
    units = units_of(total, width)
    sums = {}

    def spans(unit):
        place, head, start, step, _, _ = units[unit]
        rows = slice(head * HEAD, (head + 1) * HEAD)
        keys = slice(place * width, (place + 1) * width)
        return rows, slice(place * width + start, place * width + start + step), keys

    def probs_of(unit):
        place, head, start, step, _, _ = units[unit]
        return probs_ref[place * HEADS + head, :, start : start + step]

    def to_probs(unit, _):
        rows, cols, keys = spans(unit)
        return tn(heads_of(proj_ref, 2, units[unit][1], keys), grad_mixed_ref[rows, cols])

    def to_scores(unit, grad_probs):
        wide = probs_of(unit).astype(F32)
        moved = grad_probs * wide
        return (moved - wide * jnp.sum(moved, axis=0, keepdims=True)).astype(BF)

    def to_proj(unit, grad_scores):
        _, head, _, _, first, last = units[unit]
        rows, cols, keys = spans(unit)
        query, key = heads_of(proj_ref, 0, head, cols), heads_of(proj_ref, 1, head, keys)
        grad_proj_ref[rows, cols] = (nn(key, grad_scores) * SCALE).astype(BF)
        both = nt(query, grad_scores), nt(grad_mixed_ref[rows, cols], probs_of(unit))
        if not first:
            both = both[0] + sums["key"], both[1] + sums["value"]
        sums["key"], sums["value"] = both
        if last:
            grad_proj_ref[E + rows.start : E + rows.stop, keys] = (both[0] * SCALE).astype(BF)
            grad_proj_ref[2 * E + rows.start : 2 * E + rows.stop, keys] = both[1].astype(BF)

    staged(len(units), to_probs, to_scores, to_proj)
    results = []
    for cols in blocks_of(2 * LANES, total):
        grad_normed = nn(qkv[...], grad_proj_ref[:, cols]).astype(BF).astype(F32)
        normed, root = norm(x_ref[:, cols].astype(F32))
        results.append(norm_back(grad_normed, normed, root) + grad_ref[:, cols].astype(F32))
    return results


def put_halves(bit, sums_ref, keep_ref, send_ref):
    rows, mine = keep_ref.shape[0], has_bit("attr", bit)
    for ref, half in ((keep_ref, mine), (send_ref, 1 - mine)):
        ref[...] = sums_ref[pl.ds(pl.multiple_of(half * rows, rows), rows), :]


def put_attend_grads(out_ref, normed_ref, grad_proj_ref, mixed_ref, grad_ref):
    qkv = nt(normed_ref[...], grad_proj_ref[...])
    out = nt(mixed_ref[...], grad_ref[...])
    whole = 3 * E // LANES
    for tile in range(whole):
        out_ref[tile * E : (tile + 1) * E, :] = qkv[:, tile * LANES : (tile + 1) * LANES].astype(BF)
    mixed = jnp.concatenate([qkv[:, whole * LANES :], out[:, LANES:]], axis=1)
    out_ref[whole * E : (whole + 1) * E, :] = mixed.astype(BF)
    out_ref[(whole + 1) * E : (whole + 2) * E, :] = out[:, :LANES].astype(BF)


def take_attend_grads(in_ref, first, qkv_ref, out_ref, factor):
    whole = 3 * E // LANES

    def tile(number):
        return in_ref[first + number * E : first + (number + 1) * E, :].astype(F32) * factor

    for number in range(whole):
        qkv_ref[:, number * LANES : (number + 1) * LANES] = tile(number)
    mixed = tile(whole)
    qkv_ref[:, whole * LANES :] = mixed[:, : LANES // 2]
    out_ref[:, :LANES] = tile(whole + 1)
    out_ref[:, LANES:] = mixed[:, LANES // 2 :]


def rows_forward_kernel(plan, wait, *refs):
    tiles, refs = refs[: plan.ranks_attr], refs[plan.ranks_attr :]
    (qkv_t, out_t), refs = refs[:2], refs[2:]
    outs, (x_ref, normed_ref, proj_ref, probs_ref, mixed_ref) = refs[: plan.ranks_attr], refs[plan.ranks_attr :]
    order = one_hot(plan.cells, plan.grouped_from_rows())
    x_ref[...] = nn(side_by_side(tiles), order).astype(BF)
    first = attend(x_ref, normed_ref, proj_ref, probs_ref, mixed_ref, qkv_t, out_t, plan.all_attr, None)
    put_tiles(outs, nt(jnp.concatenate(first, axis=1).astype(BF), order))


def rows_back_kernel(plan, wait, *refs):
    tiles, refs = refs[: plan.ranks_attr], refs[plan.ranks_attr :]
    (qkv, out, x_ref, normed_ref, proj_ref, probs_ref, mixed_ref), refs = refs[:7], refs[7:]
    outs, refs = refs[: plan.ranks_attr], refs[plan.ranks_attr :]
    keep_ref, send_ref, sums_ref, grad_ref, grad_proj_ref, grad_mixed_ref = refs
    order = one_hot(plan.cells, plan.grouped_from_rows())
    grad_ref[...] = nn(side_by_side(tiles), order).astype(BF)
    wait()
    grads = attend_back(grad_ref, x_ref, proj_ref, probs_ref, grad_proj_ref, grad_mixed_ref, qkv, out, plan.all_attr)
    put_tiles(outs, nt(jnp.concatenate(grads, axis=1).astype(BF), order))
    put_attend_grads(sums_ref, normed_ref, grad_proj_ref, mixed_ref, grad_ref)
    put_halves(bits_of("attr")[0], sums_ref, keep_ref, send_ref)


def cols_kernel(plan, wait, *refs):
    count = plan.ranks_rec
    tiles, cot_tiles, refs = refs[:count], refs[count : 2 * count], refs[2 * count :]
    (train_ref, qkv, out, up, down, qkv_t, out_t, up_t), refs = refs[:8], refs[8:]
    outs, (sums_ref,), refs = refs[:count], refs[count : count + 1], refs[count + 1 :]
    x_ref, cot_ref, normed_ref, proj_ref, probs_ref, mixed_ref, second_ref = refs[:7]
    pre_ref, hidden_ref, grad_pre_ref, grad_ref, grad_proj_ref, grad_mixed_ref, mask_ref = refs[7:]
    width = max(LANES, plan.all_rec)
    order = one_hot(plan.cells, plan.grouped_from_cols())
    x_ref[...] = nn(side_by_side(tiles), order).astype(BF)
    wait()
    cot_ref[...] = nn(side_by_side(cot_tiles), order).astype(BF)

    row = lax.broadcasted_iota(jnp.int32, (width, 1), 0)
    sequence, far, near, own = digits(row, (width // plan.all_rec, plan.ranks_rec, plan.ranks_attr, plan.own_rec))
    record = plan.rec * wrap(lax.axis_index("rec") - far, plan.ranks_rec) + plan.record_of(near, own)
    chosen = (record == lane_index(plan.all_rec)) & (train_ref[...] > 0)
    allowed = jnp.max(jnp.where(chosen, 1.0, 0.0), axis=1, keepdims=True) > 0.5
    asker = digits(lane_index(width), (width // plan.all_rec, plan.all_rec))[0]
    mask_ref[...] = jnp.where(allowed & (sequence == asker), 0.0, -1e30)

    second = attend(x_ref, normed_ref, proj_ref, probs_ref, mixed_ref, qkv_t, out_t, width, mask_ref)
    for cols, value in zip(blocks_of(2 * LANES, plan.cells), second):
        second_ref[:, cols] = value.astype(BF)

    table, root = norm(second_ref[...].astype(F32))
    normed_second = table.astype(BF)
    pre_ref[...] = nn(up_t[...], normed_second)
    grad_pre_ref[...] = nn(down[...], cot_ref[...])
    step = 32
    for start in range(0, FF, step):
        rows = slice(start, start + step)
        pre = pre_ref[rows, :]
        gate = 0.5 + 0.5 * lax.erf(pre * HALF_ROOT)
        hidden_ref[rows, :] = (pre * gate).astype(BF)
        slope = gate + pre * (jnp.exp2(pre * pre * BELL_EXP2) * BELL)
        grad_pre_ref[rows, :] = grad_pre_ref[rows, :] * slope
    grad_pre = grad_pre_ref[...].astype(BF)

    for base, grad_weight in (
        (6 * E, nt(normed_second, grad_pre)),
        (12 * E, nt(cot_ref[...], hidden_ref[...])),
    ):
        for tile in range(FF // LANES):
            rows = slice(base + tile * E, base + (tile + 1) * E)
            sums_ref[rows, :] = grad_weight[:, tile * LANES : (tile + 1) * LANES].astype(BF)

    grad_normed = nn(up[...], grad_pre).astype(BF).astype(F32)
    grad = norm_back(grad_normed, table, root) + cot_ref[...].astype(F32)
    grad_ref[...] = grad.astype(BF)
    grads = attend_back(grad_ref, x_ref, proj_ref, probs_ref, grad_proj_ref, grad_mixed_ref, qkv, out, width)
    put_tiles(outs, nt(jnp.concatenate(grads, axis=1).astype(BF), order))
    put_attend_grads(sums_ref, normed_ref, grad_proj_ref, mixed_ref, grad_ref)


def finish_cols_kernel(factor, bits, wait, *refs):
    parts, (qkv_ref, out_ref, up_ref, down_ref, sums_ref) = refs[:-5], refs[-5:]
    lay_out(bits, parts, sums_ref)
    take_attend_grads(sums_ref, 0, qkv_ref, out_ref, factor)
    for base, ref in ((6 * E, up_ref), (12 * E, down_ref)):
        for tile in range(FF // LANES):
            rows = slice(base + tile * E, base + (tile + 1) * E)
            ref[:, tile * LANES : (tile + 1) * LANES] = sums_ref[rows, :].astype(F32) * factor


def finish_rows_kernel(factor, bits, wait, *refs):
    parts, (qkv_ref, out_ref, sums_ref) = refs[:-3], refs[-3:]
    lay_out(bits, parts, sums_ref)
    take_attend_grads(sums_ref, 0, qkv_ref, out_ref, factor)


class Far(NamedTuple):
    array: jax.Array


class Near(NamedTuple):
    array: jax.Array


def call(body, outs, scratch, *args, after=()):
    far = [n for n, arg in enumerate(args) if isinstance(arg, Far)]
    n_in, n_after, n_out, n_far = len(args), len(after), len(outs), len(far)
    whole, anywhere = pl.BlockSpec(memory_space=pltpu.VMEM), pl.BlockSpec(memory_space=pl.ANY)
    hbm = pl.BlockSpec(memory_space=pltpu.HBM)

    def kernel(*refs):
        given, refs = list(refs[:n_in]), refs[n_in + n_after :]
        copies = []
        if far:
            held, sems, refs = refs[-1 - n_far : -1], refs[-1], refs[: -1 - n_far]
            for order, (number, ref) in enumerate(zip(far, held)):
                copies.append(pltpu.make_async_copy(given[number], ref, sems.at[order]))
                given[number] = ref
        for copy in copies:
            copy.start()

        def wait():
            for copy in copies:
                copy.wait()

        body(wait, *given, *refs)

    arrays = []
    for arg in args:
        space = {Far: pltpu.HBM, Near: pltpu.VMEM}.get(type(arg))
        arrays.append(arg if space is None else pltpu.with_memory_space_constraint(arg.array, space))
    held = [pltpu.VMEM(arrays[n].shape, arrays[n].dtype) for n in far]
    return pl.pallas_call(
        kernel,
        out_shape=[
            (pltpu.VMEM if out[2:] else jax.ShapeDtypeStruct)(out[0], out[1]) for out in outs
        ],
        in_specs=[hbm if isinstance(arg, Far) else whole for arg in args] + [anywhere] * n_after,
        out_specs=[whole] * n_out,
        scratch_shapes=[pltpu.VMEM(shape, dtype) for shape, dtype in scratch]
        + held
        + ([pltpu.SemaphoreType.DMA((n_far,))] if far else []),
        compiler_params=pltpu.CompilerParams(vmem_limit_bytes=VMEM),
    )(*arrays, *after)


def exchange(tiles, axis, sign):
    size = len(tiles)
    return [tiles[0]] + [
        lax.ppermute(tiles[k], axis, [(i, (i + sign * k) % size) for i in range(size)])
        for k in range(1, size)
    ]


def swap(part, axis, bit):
    size = lax.axis_size(axis)
    return lax.ppermute(part, axis, [(i, i ^ bit) for i in range(size)])


def has_bit(axis, bit):
    return digits(lax.axis_index(axis) // bit, (2,))[0]


def halve_kernel(bit, wait, *refs):
    parts, (keep, send) = refs[:-2], refs[-2:]
    rows, mine = keep.shape[0], has_bit("attr", bit)
    for ref, half in ((keep, mine), (send, 1 - mine)):
        place = pl.ds(pl.multiple_of(half * rows, rows), rows)
        ref[...] = sum(part[place, :].astype(F32) for part in parts).astype(BF)


def add_kernel(wait, *refs):
    refs[-1][...] = sum(part[...].astype(F32) for part in refs[:-1]).astype(BF)


def lay_out(bits, parts, rows_ref):
    rows = parts[0].shape[0]
    for number, ref in enumerate(parts):
        place = 0
        for order, bit in enumerate(bits):
            own = has_bit("attr", bit)
            place = place * 2 + (1 - own if number >> order & 1 else own)
        rows_ref[pl.ds(pl.multiple_of(place * rows, rows), rows), :] = ref[...]


def bits_of(axis):
    return [1 << n for n in range(lax.axis_size(axis).bit_length() - 1)]


class Total:
    def __init__(self, *parts):
        self.parts, self.rows = list(parts), parts[0].shape[0]

    def halve(self, bit, after=()):
        self.rows //= 2
        keep, send = call(
            functools.partial(halve_kernel, bit), [((self.rows, LANES), BF)] * 2, [], *self.parts, after=after
        )
        self.parts = [keep, swap(send, "attr", bit)]
        return [keep]

    def add(self, bit=0, after=()):
        (part,) = call(add_kernel, [((self.rows, LANES), BF)], [], *self.parts, after=after)
        self.parts = [part] + ([swap(part, "rec", bit)] if bit else [])
        return [part]

    def spread(self, bits):
        done = {0: self.parts[0]}
        for order, bit in reversed(list(enumerate(bits))):
            done.update({number | 1 << order: swap(part, "attr", bit) for number, part in sorted(done.items())})
        return [done[number] for number in sorted(done)]


def padded(rows):
    devices = lax.axis_size("attr")
    return -(-rows // (16 * devices)) * 16 * devices


def local(
    cells, cotangent, qkv_attr, out_attr, qkv_samp, out_samp, up_weight, down_weight, train_split
):
    ranks_rec, ranks_attr = lax.axis_size("rec"), lax.axis_size("attr")
    plan = Plan(cells, ranks_rec, ranks_attr)
    count = plan.cells
    factor = 1.0 / math.sqrt(plan.all_rec * plan.all_attr)
    row_tiles = [((E, plan.row_tile), BF)] * ranks_attr
    col_tiles = [((E, plan.col_tile), BF)] * ranks_rec
    table, wide = ((E, count), BF), ((3 * E, count), BF)

    def probs(width):
        return ((count // width * HEADS, width, width), BF)

    def kernel(body, *static):
        return functools.partial(body, plan, *static)

    rows = call(kernel(split_kernel, True), row_tiles, [((count, E), F32)], Far(cells))
    rows = exchange(rows, "attr", 1)
    weights = (qkv_attr, out_attr, qkv_samp, out_samp, up_weight, down_weight.T)
    got = call(
        kernel(split_turn_kernel, len(weights)),
        col_tiles + [(w.shape[::-1], BF, "near") for w in weights],
        [((count, E), F32)],
        Far(cotangent),
        *[Far(w) for w in weights],
        after=[rows[0]],
    )
    cot = exchange(got[:ranks_rec], "rec", 1)
    turned = [Near(w) for w in got[ranks_rec:]]

    got = call(
        kernel(rows_forward_kernel),
        row_tiles + [out + ("near",) for out in (table, table, wide, probs(plan.all_attr), table)],
        [],
        *rows,
        *turned[:2],
    )
    first, saved = got[:ranks_attr], [Near(array) for array in got[ranks_attr:]]
    first = exchange(first, "attr", -1)
    cols = exchange(call(kernel(to_cols_kernel), col_tiles, [], *first), "rec", 1)

    width = max(LANES, plan.all_rec)
    rows_sums, cols_sums = padded(6 * E), padded(18 * E)
    got = call(
        kernel(cols_kernel),
        col_tiles + [((cols_sums, LANES), BF)],
        [table, table, table, wide, probs(width), table, table]
        + [((FF, count), F32), ((FF, count), BF), ((FF, count), F32), table, wide, table, ((width, width), F32)],
        *cols,
        *cot,
        train_split.reshape(1, -1),
        Far(qkv_samp),
        Far(out_samp),
        Far(up_weight),
        turned[5],
        turned[2],
        turned[3],
        turned[4],
    )
    near, far = bits_of("attr"), bits_of("rec")
    grads, sums = exchange(got[:ranks_rec], "rec", -1), Total(got[ranks_rec])
    mark = sums.halve(near[0])
    for bit in near[1:]:
        mark = sums.halve(bit, after=mark)
    grads = exchange(call(kernel(to_rows_kernel), row_tiles, [], *grads, after=mark), "attr", 1)
    mark = sums.add(far[0])

    got = call(
        kernel(rows_back_kernel),
        row_tiles + [((rows_sums // 2, LANES), BF)] * 2,
        [((rows_sums, LANES), BF), table, wide, table],
        *grads,
        Far(qkv_attr),
        Far(out_attr),
        *saved,
        after=mark,
    )
    grads, row_sums = exchange(got[:ranks_attr], "attr", -1), Total(*got[ranks_attr:])
    row_sums.parts[1] = swap(row_sums.parts[1], "attr", near[0])
    mark = []
    for bit in near[1:]:
        mark = row_sums.halve(bit, after=mark)
    for bit in far[1:]:
        mark = sums.add(bit, after=mark)
    mark = row_sums.add(far[0], after=mark)
    (grad_cells,) = call(kernel(join_kernel), [(cells.shape, BF)], [((count, E), F32)], *grads, after=mark)
    mark = [grad_cells]
    for bit in far[1:]:
        mark = row_sums.add(bit, after=mark)
    mark = sums.add(after=mark)
    parts = sums.spread(near)
    row_sums.add(after=mark)
    row_parts = row_sums.spread(near)
    grad_qkv_samp, grad_out_samp, grad_up, grad_down = call(
        functools.partial(finish_cols_kernel, factor, near),
        [((E, 3 * E), F32), ((E, E), F32), ((E, FF), F32), ((E, FF), F32)],
        [((cols_sums, LANES), BF)],
        *parts,
    )
    grad_qkv_attr, grad_out_attr = call(
        functools.partial(finish_rows_kernel, factor, near),
        [((E, 3 * E), F32), ((E, E), F32)],
        [((rows_sums, LANES), BF)],
        *row_parts,
    )
    grad_down = grad_down.T
    return (grad_cells, grad_qkv_attr, grad_out_attr, grad_qkv_samp, grad_out_samp, grad_up, grad_down)


def solution(mesh):
    own = P(("groups", "rec"), "attr")
    in_specs = (own, own) + (P(),) * 6 + (P("groups"),)
    out_specs = (own,) + (P("groups", None),) * 6
    return jax.shard_map(local, mesh=mesh, in_specs=in_specs, out_specs=out_specs, check_vma=False)
```

```python
import functools
import math
from typing import NamedTuple

import jax
import jax.numpy as jnp
from jax import lax
from jax.experimental import pallas as pl
from jax.experimental.pallas import tpu as pltpu
from jax.sharding import PartitionSpec as P

E = 192
HEADS = 6
FF = 768
HEAD = E // HEADS
LANES = 128
VMEM = 24 * 1024 * 1024
BF = jnp.bfloat16
F32 = jnp.float32
EXP2 = math.log2(math.e) / math.sqrt(HEAD)
SCALE = 1.0 / math.sqrt(HEAD)
HALF_ROOT = math.sqrt(0.5)
BELL_EXP2 = -0.5 * math.log2(math.e)
BELL = 1.0 / math.sqrt(2.0 * math.pi)


def nn(left, right):
    return lax.dot_general(left, right, (((1,), (0,)), ((), ())), preferred_element_type=F32)


def nt(left, right):
    return lax.dot_general(left, right, (((1,), (1,)), ((), ())), preferred_element_type=F32)


def tn(left, right):
    return lax.dot_general(left, right, (((0,), (0,)), ((), ())), preferred_element_type=F32)


def digits(index, sizes):
    out = []
    for size in reversed(sizes):
        if size & (size - 1) == 0:
            out.append(index & (size - 1))
            index = index >> (size.bit_length() - 1)
        else:
            out.append(lax.rem(index, size))
            index = lax.div(index, size)
    return out[::-1]


def wrap(index, size):
    return digits(index + size, (size,))[0]


def one_hot(rows, source):
    own = lax.broadcasted_iota(jnp.int32, (rows, source.shape[1]), 0)
    return jnp.where(own == source, 1.0, 0.0).astype(BF)


def lane_index(size):
    return lax.broadcasted_iota(jnp.int32, (1, size), 1)


def eye(size):
    return one_hot(size, lane_index(size))


def side_by_side(refs):
    return jnp.concatenate([ref[...] for ref in refs], axis=1)


def put_tiles(refs, table):
    width = refs[0].shape[1]
    for position, ref in enumerate(refs):
        ref[...] = table[:, position * width : (position + 1) * width].astype(ref.dtype)


class Plan:
    def __init__(self, cells, ranks_rec, ranks_attr):
        self.ranks_rec, self.ranks_attr = ranks_rec, ranks_attr
        self.rec, self.attr = cells.shape[0], cells.shape[1] // E
        self.cells = self.rec * self.attr
        self.own_rec = self.rec // ranks_attr
        self.own_attr = self.attr // ranks_rec
        self.all_rec = self.rec * ranks_rec
        self.all_attr = self.attr * ranks_attr
        self.row_tile = self.own_rec * self.attr
        self.col_tile = self.rec * self.own_attr

    def row_digits(self, index):
        return digits(index, (self.ranks_attr, self.own_rec, self.attr))

    def col_digits(self, index):
        return digits(index, (self.ranks_rec, self.ranks_attr, self.own_rec, self.own_attr))

    def record_of(self, step, own):
        return self.own_rec * wrap(step + lax.axis_index("attr"), self.ranks_attr) + own

    def attr_of(self, step, own):
        return self.own_attr * wrap(step + lax.axis_index("rec"), self.ranks_rec) + own

    def rows_from_owned(self):
        step, own, attr = self.row_digits(lane_index(self.cells))
        return attr * self.rec + self.record_of(step, own)

    def cols_from_owned(self):
        far, near, own, attr = self.col_digits(lane_index(self.cells))
        return self.attr_of(far, attr) * self.rec + self.record_of(near, own)

    def cols_from_rows(self):
        far, near, own, attr = self.col_digits(lane_index(self.cells))
        return (near * self.own_rec + own) * self.attr + self.attr_of(far, attr)

    def grouped_from_rows(self):
        own, step, attr = digits(lane_index(self.cells), (self.own_rec, self.ranks_attr, self.attr))
        return (step * self.own_rec + own) * self.attr + attr

    def grouped_from_cols(self):
        attr, place = digits(lane_index(self.cells), (self.own_attr, self.all_rec))
        return place * self.own_attr + attr


def split_kernel(plan, to_rows, wait, table_ref, *refs):
    wait()
    outs, rows = refs[:-1], refs[-1]
    for pair in range(plan.attr // 2):
        both = table_ref[:, 2 * E * pair : 2 * E * (pair + 1)].astype(F32)
        for side in range(2):
            start = (2 * pair + side) * plan.rec
            rows[start : start + plan.rec, :] = both[:, side * E : (side + 1) * E]
    turned = nt(eye(E), rows[...].astype(BF)).astype(BF)
    source = plan.rows_from_owned() if to_rows else plan.cols_from_owned()
    put_tiles(outs, nn(turned, one_hot(plan.cells, source)))


def join_kernel(plan, wait, *refs):
    tiles, out_ref, rows = refs[:-2], refs[-2], refs[-1]
    rows[...] = nt(one_hot(plan.cells, plan.rows_from_owned()), side_by_side(tiles))
    for pair in range(plan.attr // 2):
        start = 2 * pair * plan.rec
        both = [rows[start + side * plan.rec : start + (side + 1) * plan.rec, :] for side in range(2)]
        out_ref[:, 2 * E * pair : 2 * E * (pair + 1)] = jnp.concatenate(both, axis=1).astype(BF)


def to_cols_kernel(plan, wait, *refs):
    tiles, outs = refs[: plan.ranks_attr], refs[plan.ranks_attr :]
    put_tiles(outs, nn(side_by_side(tiles), one_hot(plan.cells, plan.cols_from_rows())))


def to_rows_kernel(plan, wait, *refs):
    tiles, outs = refs[: plan.ranks_rec], refs[plan.ranks_rec :]
    put_tiles(outs, nt(side_by_side(tiles), one_hot(plan.cells, plan.cols_from_rows())))


def split_turn_kernel(plan, count, wait, table_ref, *refs):
    weights, refs = refs[:count], refs[count:]
    split_kernel(plan, False, wait, table_ref, *refs[: plan.ranks_rec], refs[-1])
    for source, target in zip(weights, refs[plan.ranks_rec : -1]):
        target[...] = source[...].astype(F32).T.astype(BF)


def norm(table):
    center = table - jnp.mean(table, axis=0, keepdims=True)
    spread = jnp.mean(center * center, axis=0, keepdims=True)
    root = lax.rsqrt(spread + 1e-05)
    return center * root, root


def norm_back(grad, normed, root):
    along = jnp.mean(grad * normed, axis=0, keepdims=True)
    return root * (grad - jnp.mean(grad, axis=0, keepdims=True) - normed * along)


def blocks_of(width, total):
    return [slice(start, start + width) for start in range(0, total, width)]


def heads_of(ref, part, head, cols):
    start = part * E + head * HEAD
    return ref[start : start + HEAD, cols]


def staged(count, *stages):
    held = {}
    for step in range(count + len(stages) - 1):
        for lag, stage in enumerate(stages):
            unit = step - lag
            if 0 <= unit < count:
                held[unit] = stage(unit, held.get(unit))
                if lag == len(stages) - 1:
                    del held[unit]


def units_of(total, width):
    step = min(2 * LANES, width)
    return [
        (place, head, start, step, start == 0, start + step == width)
        for place in range(total // width)
        for head in range(HEADS)
        for start in range(0, width, step)
    ]


def attend(x_ref, normed_ref, proj_ref, probs_ref, mixed_ref, qkv_t, out_t, width, mask_ref):
    total = x_ref.shape[1]
    for cols in blocks_of(2 * LANES, total):
        normed_ref[:, cols] = norm(x_ref[:, cols].astype(F32))[0].astype(BF)
    for cols in blocks_of(2 * LANES, total):
        proj_ref[:, cols] = nn(qkv_t[...], normed_ref[:, cols]).astype(BF)
    units = units_of(total, width)

    def score(unit, _):
        place, head, start, step, _, _ = units[unit]
        cols = slice(place * width + start, place * width + start + step)
        keys = slice(place * width, (place + 1) * width)
        return tn(heads_of(proj_ref, 1, head, keys), heads_of(proj_ref, 0, head, cols))

    def weigh(unit, scores):
        place, head, start, step, _, _ = units[unit]
        if mask_ref is not None:
            scores = scores + mask_ref[:, start : start + step]
        expo = jnp.exp2((scores - jnp.max(scores, axis=0, keepdims=True)) * EXP2)
        probs = (expo * (1.0 / jnp.sum(expo, axis=0, keepdims=True))).astype(BF)
        probs_ref[place * HEADS + head, :, start : start + step] = probs
        return probs

    def mix(unit, probs):
        place, head, start, step, _, _ = units[unit]
        value = heads_of(proj_ref, 2, head, slice(place * width, (place + 1) * width))
        cols = slice(place * width + start, place * width + start + step)
        mixed_ref[head * HEAD : (head + 1) * HEAD, cols] = nn(value, probs).astype(BF)

    staged(len(units), score, weigh, mix)
    return [
        x_ref[:, cols].astype(F32) + nn(out_t[...], mixed_ref[:, cols])
        for cols in blocks_of(2 * LANES, total)
    ]


def attend_back(grad_ref, proj_ref, probs_ref, grad_proj_ref, grad_mixed_ref, out, width):
    total = grad_ref.shape[1]
    for cols in blocks_of(2 * LANES, total):
        grad_mixed_ref[:, cols] = nn(out[...], grad_ref[:, cols]).astype(BF)
    units = units_of(total, width)
    sums = {}

    def spans(unit):
        place, head, start, step, _, _ = units[unit]
        rows = slice(head * HEAD, (head + 1) * HEAD)
        keys = slice(place * width, (place + 1) * width)
        return rows, slice(place * width + start, place * width + start + step), keys

    def probs_of(unit):
        place, head, start, step, _, _ = units[unit]
        return probs_ref[place * HEADS + head, :, start : start + step]

    def to_probs(unit, _):
        rows, cols, keys = spans(unit)
        return tn(heads_of(proj_ref, 2, units[unit][1], keys), grad_mixed_ref[rows, cols])

    def to_scores(unit, grad_probs):
        wide = probs_of(unit).astype(F32)
        moved = grad_probs * wide
        return (moved - wide * jnp.sum(moved, axis=0, keepdims=True)).astype(BF)

    def to_proj(unit, grad_scores):
        _, head, _, _, first, last = units[unit]
        rows, cols, keys = spans(unit)
        query, key = heads_of(proj_ref, 0, head, cols), heads_of(proj_ref, 1, head, keys)
        grad_proj_ref[rows, cols] = (nn(key, grad_scores) * SCALE).astype(BF)
        both = nt(query, grad_scores), nt(grad_mixed_ref[rows, cols], probs_of(unit))
        if not first:
            both = both[0] + sums["key"], both[1] + sums["value"]
        sums["key"], sums["value"] = both
        if last:
            grad_proj_ref[E + rows.start : E + rows.stop, keys] = (both[0] * SCALE).astype(BF)
            grad_proj_ref[2 * E + rows.start : 2 * E + rows.stop, keys] = both[1].astype(BF)

    staged(len(units), to_probs, to_scores, to_proj)


def project_back(grad_ref, x_ref, grad_proj_ref, qkv):
    results = []
    for cols in blocks_of(2 * LANES, x_ref.shape[1]):
        grad_normed = nn(qkv[...], grad_proj_ref[:, cols]).astype(BF).astype(F32)
        normed, root = norm(x_ref[:, cols].astype(F32))
        results.append(norm_back(grad_normed, normed, root) + grad_ref[:, cols].astype(F32))
    return results


def put_halves(bit, sums_ref, keep_ref, send_ref):
    rows, mine = keep_ref.shape[0], has_bit("attr", bit)
    for ref, half in ((keep_ref, mine), (send_ref, 1 - mine)):
        ref[...] = sums_ref[pl.ds(pl.multiple_of(half * rows, rows), rows), :]


def put_attend_grads(out_ref, normed_ref, grad_proj_ref, mixed_ref, grad_ref):
    qkv = nt(normed_ref[...], grad_proj_ref[...])
    out = nt(mixed_ref[...], grad_ref[...])
    whole = 3 * E // LANES
    for tile in range(whole):
        out_ref[tile * E : (tile + 1) * E, :] = qkv[:, tile * LANES : (tile + 1) * LANES].astype(BF)
    mixed = jnp.concatenate([qkv[:, whole * LANES :], out[:, LANES:]], axis=1)
    out_ref[whole * E : (whole + 1) * E, :] = mixed.astype(BF)
    out_ref[(whole + 1) * E : (whole + 2) * E, :] = out[:, :LANES].astype(BF)


def take_attend_grads(in_ref, first, qkv_ref, out_ref, factor):
    whole = 3 * E // LANES

    def tile(number):
        return in_ref[first + number * E : first + (number + 1) * E, :].astype(F32) * factor

    for number in range(whole):
        qkv_ref[:, number * LANES : (number + 1) * LANES] = tile(number)
    mixed = tile(whole)
    qkv_ref[:, whole * LANES :] = mixed[:, : LANES // 2]
    out_ref[:, :LANES] = tile(whole + 1)
    out_ref[:, LANES:] = mixed[:, LANES // 2 :]


def rows_forward_kernel(plan, wait, *refs):
    tiles, refs = refs[: plan.ranks_attr], refs[plan.ranks_attr :]
    (qkv_t, out_t), refs = refs[:2], refs[2:]
    outs, refs = refs[: plan.ranks_attr], refs[plan.ranks_attr :]
    x_ref, normed_ref, proj_ref, probs_ref, mixed_ref = refs
    order = one_hot(plan.cells, plan.grouped_from_rows())
    x_ref[...] = nn(side_by_side(tiles), order).astype(BF)
    first = attend(x_ref, normed_ref, proj_ref, probs_ref, mixed_ref, qkv_t, out_t, plan.all_attr, None)
    put_tiles(outs, nt(jnp.concatenate(first, axis=1).astype(BF), order))


def rows_back_kernel(plan, wait, *refs):
    tiles, refs = refs[: plan.ranks_attr], refs[plan.ranks_attr :]
    (out, normed_ref, proj_ref, probs_ref, mixed_ref), refs = refs[:5], refs[5:]
    keep_ref, send_ref, grad_ref, grad_proj_ref, sums_ref, grad_mixed_ref = refs
    order = one_hot(plan.cells, plan.grouped_from_rows())
    grad_ref[...] = nn(side_by_side(tiles), order).astype(BF)
    wait()
    attend_back(grad_ref, proj_ref, probs_ref, grad_proj_ref, grad_mixed_ref, out, plan.all_attr)
    put_attend_grads(sums_ref, normed_ref, grad_proj_ref, mixed_ref, grad_ref)
    put_halves(bits_of("attr")[0], sums_ref, keep_ref, send_ref)


def rows_end_kernel(plan, wait, qkv, x_ref, grad_ref, grad_proj_ref, *outs):
    order = one_hot(plan.cells, plan.grouped_from_rows())
    wait()
    grads = project_back(grad_ref, x_ref, grad_proj_ref, qkv)
    put_tiles(outs, nt(jnp.concatenate(grads, axis=1).astype(BF), order))


def cols_kernel(plan, wait, *refs):
    count = plan.ranks_rec
    tiles, cot_tiles, refs = refs[:count], refs[count : 2 * count], refs[2 * count :]
    (train_ref, qkv, out, up, down, qkv_t, out_t, up_t), refs = refs[:8], refs[8:]
    outs, refs = refs[:count], refs[count:]
    normed_ref, mixed_ref, normed_second_ref, hidden_ref, cot_ref, grad_pre_ref, grad_ref, grad_proj_ref = refs[:8]
    x_ref, proj_ref, probs_ref, second_ref, slope_ref, wide_ref, mask_ref, grad_mixed_ref = refs[8:]
    width = max(LANES, plan.all_rec)
    order = one_hot(plan.cells, plan.grouped_from_cols())
    x_ref[...] = nn(side_by_side(tiles), order).astype(BF)

    row = lax.broadcasted_iota(jnp.int32, (width, 1), 0)
    sequence, far, near, own = digits(row, (width // plan.all_rec, plan.ranks_rec, plan.ranks_attr, plan.own_rec))
    record = plan.rec * wrap(lax.axis_index("rec") - far, plan.ranks_rec) + plan.record_of(near, own)
    chosen = (record == lane_index(plan.all_rec)) & (train_ref[...] > 0)
    allowed = jnp.max(jnp.where(chosen, 1.0, 0.0), axis=1, keepdims=True) > 0.5
    asker = digits(lane_index(width), (width // plan.all_rec, plan.all_rec))[0]
    mask_ref[...] = jnp.where(allowed & (sequence == asker), 0.0, -1e30)

    second = attend(x_ref, normed_ref, proj_ref, probs_ref, mixed_ref, qkv_t, out_t, width, mask_ref)
    for cols, value in zip(blocks_of(2 * LANES, plan.cells), second):
        second_ref[:, cols] = value.astype(BF)
        normed_second_ref[:, cols] = norm(second_ref[:, cols].astype(F32))[0].astype(BF)
    wide_ref[...] = nn(up_t[...], normed_second_ref[...])
    step = 32
    for start in range(0, FF, step):
        rows = slice(start, start + step)
        pre = wide_ref[rows, :]
        gate = 0.5 + 0.5 * lax.erf(pre * HALF_ROOT)
        hidden_ref[rows, :] = (pre * gate).astype(BF)
        slope_ref[rows, :] = gate + pre * (jnp.exp2(pre * pre * BELL_EXP2) * BELL)

    cot_ref[...] = nn(side_by_side(cot_tiles), order).astype(BF)
    wait()
    wide_ref[...] = nn(down[...], cot_ref[...])
    step = 64
    for start in range(0, FF, step):
        rows = slice(start, start + step)
        grad_pre_ref[rows, :] = (wide_ref[rows, :] * slope_ref[rows, :]).astype(BF)
    for cols in blocks_of(2 * LANES, plan.cells):
        grad_normed = nn(up[...], grad_pre_ref[:, cols]).astype(BF).astype(F32)
        table, root = norm(second_ref[:, cols].astype(F32))
        grad_ref[:, cols] = (norm_back(grad_normed, table, root) + cot_ref[:, cols].astype(F32)).astype(BF)
    attend_back(grad_ref, proj_ref, probs_ref, grad_proj_ref, grad_mixed_ref, out, width)
    grads = project_back(grad_ref, x_ref, grad_proj_ref, qkv)
    put_tiles(outs, nt(jnp.concatenate(grads, axis=1).astype(BF), order))


def cols_sums_kernel(wait, *refs):
    normed_ref, mixed_ref, normed_second_ref, hidden_ref, cot_ref, grad_pre_ref, grad_ref, grad_proj_ref = refs[:8]
    keep_ref, send_ref, sums_ref = refs[8:]
    for base, grad_weight in (
        (6 * E, nt(normed_second_ref[...], grad_pre_ref[...])),
        (12 * E, nt(cot_ref[...], hidden_ref[...])),
    ):
        for tile in range(FF // LANES):
            rows = slice(base + tile * E, base + (tile + 1) * E)
            sums_ref[rows, :] = grad_weight[:, tile * LANES : (tile + 1) * LANES].astype(BF)
    put_attend_grads(sums_ref, normed_ref, grad_proj_ref, mixed_ref, grad_ref)
    put_halves(bits_of("attr")[0], sums_ref, keep_ref, send_ref)


def finish_cols_kernel(factor, bits, wait, *refs):
    parts, (qkv_ref, out_ref, up_ref, down_ref, sums_ref) = refs[:-5], refs[-5:]
    lay_out(bits, parts, sums_ref)
    take_attend_grads(sums_ref, 0, qkv_ref, out_ref, factor)
    for base, ref in ((6 * E, up_ref), (12 * E, down_ref)):
        for tile in range(FF // LANES):
            rows = slice(base + tile * E, base + (tile + 1) * E)
            ref[:, tile * LANES : (tile + 1) * LANES] = sums_ref[rows, :].astype(F32) * factor


def finish_rows_kernel(factor, bits, wait, *refs):
    parts, (qkv_ref, out_ref, sums_ref) = refs[:-3], refs[-3:]
    lay_out(bits, parts, sums_ref)
    take_attend_grads(sums_ref, 0, qkv_ref, out_ref, factor)


class Far(NamedTuple):
    array: jax.Array


class Near(NamedTuple):
    array: jax.Array


def in_hbm(array):
    return pltpu.with_memory_space_constraint(array, pltpu.HBM)


def call(body, outs, scratch, *args, after=()):
    far = [n for n, arg in enumerate(args) if isinstance(arg, Far)]
    n_in, n_after, n_out, n_far = len(args), len(after), len(outs), len(far)
    whole, anywhere = pl.BlockSpec(memory_space=pltpu.VMEM), pl.BlockSpec(memory_space=pl.ANY)
    hbm = pl.BlockSpec(memory_space=pltpu.HBM)

    def kernel(*refs):
        given, refs = list(refs[:n_in]), refs[n_in + n_after :]
        copies = []
        if far:
            held, sems, refs = refs[-1 - n_far : -1], refs[-1], refs[: -1 - n_far]
            for order, (number, ref) in enumerate(zip(far, held)):
                copies.append(pltpu.make_async_copy(given[number], ref, sems.at[order]))
                given[number] = ref
        for copy in copies:
            copy.start()

        def wait():
            for copy in copies:
                copy.wait()

        body(wait, *given, *refs)

    arrays = []
    for arg in args:
        space = {Far: pltpu.HBM, Near: pltpu.VMEM}.get(type(arg))
        arrays.append(arg if space is None else pltpu.with_memory_space_constraint(arg.array, space))
    held = [pltpu.VMEM(arrays[n].shape, arrays[n].dtype) for n in far]
    return pl.pallas_call(
        kernel,
        out_shape=[
            (pltpu.VMEM if out[2:] else jax.ShapeDtypeStruct)(out[0], out[1]) for out in outs
        ],
        in_specs=[hbm if isinstance(arg, Far) else whole for arg in args] + [anywhere] * n_after,
        out_specs=[whole] * n_out,
        scratch_shapes=[pltpu.VMEM(shape, dtype) for shape, dtype in scratch]
        + held
        + ([pltpu.SemaphoreType.DMA((n_far,))] if far else []),
        compiler_params=pltpu.CompilerParams(vmem_limit_bytes=VMEM),
    )(*arrays, *[in_hbm(arg.array) if isinstance(arg, Far) else arg for arg in after])


def exchange(tiles, axis, sign):
    size = len(tiles)
    return [tiles[0]] + [
        lax.ppermute(tiles[k], axis, [(i, (i + sign * k) % size) for i in range(size)])
        for k in range(1, size)
    ]


def swap(part, axis, bit):
    size = lax.axis_size(axis)
    return lax.ppermute(part, axis, [(i, i ^ bit) for i in range(size)])


def has_bit(axis, bit):
    return digits(lax.axis_index(axis) // bit, (2,))[0]


def halve_kernel(axis, bit, wait, *refs):
    parts, (keep, send) = refs[:-2], refs[-2:]
    rows, mine = keep.shape[0], has_bit(axis, bit)
    for ref, half in ((keep, mine), (send, 1 - mine)):
        place = pl.ds(pl.multiple_of(half * rows, rows), rows)
        ref[...] = sum(part[place, :].astype(F32) for part in parts).astype(BF)


def add_kernel(wait, *refs):
    refs[-1][...] = sum(part[...].astype(F32) for part in refs[:-1]).astype(BF)


def lay_out_kernel(axis, bit, wait, own_ref, other_ref, out_ref):
    rows = own_ref.shape[0]
    mine = has_bit(axis, bit)
    for ref, half in ((own_ref, mine), (other_ref, 1 - mine)):
        out_ref[pl.ds(pl.multiple_of(half * rows, rows), rows), :] = ref[...]


def lay_out(bits, parts, rows_ref):
    rows = parts[0].shape[0]
    for number, ref in enumerate(parts):
        place = 0
        for order, bit in enumerate(bits):
            own = has_bit("attr", bit)
            place = place * 2 + (1 - own if number >> order & 1 else own)
        rows_ref[pl.ds(pl.multiple_of(place * rows, rows), rows), :] = ref[...]


def bits_of(axis):
    return [1 << n for n in range(lax.axis_size(axis).bit_length() - 1)]


class Total:
    def __init__(self, *parts):
        self.parts, self.rows = list(parts), parts[0].shape[0]

    def halve(self, axis, bit, after=()):
        self.rows //= 2
        keep, send = call(
            functools.partial(halve_kernel, axis, bit), [((self.rows, LANES), BF)] * 2, [], *self.parts, after=after
        )
        self.parts = [keep, swap(send, axis, bit)]
        return [keep]

    def back(self, axis, bit, after=()):
        self.rows *= 2
        body = functools.partial(lay_out_kernel, axis, bit)
        (part,) = call(body, [((self.rows, LANES), BF)], [], *self.parts, after=after)
        self.parts = [part]
        return [part]

    def add(self, bit=0, after=()):
        (part,) = call(add_kernel, [((self.rows, LANES), BF)], [], *self.parts, after=after)
        self.parts = [part] + ([swap(part, "rec", bit)] if bit else [])
        return [part]

    def spread_after(self, bits, middle):
        done = {0: self.parts[0]}
        for order, bit in reversed(list(enumerate(bits[1:], 1))):
            done.update({number | 1 << order: swap(part, "attr", bit) for number, part in sorted(done.items())})
        near = {1: swap(done[0], "attr", bits[0])}
        results, after = middle()
        for number, part in sorted(done.items()):
            if number:
                (part,) = call(add_kernel, [(part.shape, BF)], [], part, after=after)
                near[number | 1] = swap(part, "attr", bits[0])
        done.update(near)
        return results, [done[number] for number in sorted(done)]


def padded(rows):
    devices = 2 * lax.axis_size("attr")
    return -(-rows // (16 * devices)) * 16 * devices


def local(
    cells, cotangent, qkv_attr, out_attr, qkv_samp, out_samp, up_weight, down_weight, train_split
):
    ranks_rec, ranks_attr = lax.axis_size("rec"), lax.axis_size("attr")
    plan = Plan(cells, ranks_rec, ranks_attr)
    count = plan.cells
    factor = 1.0 / math.sqrt(plan.all_rec * plan.all_attr)
    row_tiles = [((E, plan.row_tile), BF)] * ranks_attr
    col_tiles = [((E, plan.col_tile), BF)] * ranks_rec
    table, wide = ((E, count), BF), ((3 * E, count), BF)

    def probs(width):
        return ((count // width * HEADS, width, width), BF)

    def kernel(body, *static):
        return functools.partial(body, plan, *static)

    rows = call(kernel(split_kernel, True), row_tiles, [((count, E), F32)], Far(cells))
    rows = exchange(rows, "attr", 1)
    weights = (qkv_attr, out_attr, qkv_samp, out_samp, up_weight, down_weight.T)
    got = call(
        kernel(split_turn_kernel, len(weights)),
        col_tiles + [(w.shape[::-1], BF, "near") for w in weights],
        [((count, E), F32)],
        Far(cotangent),
        *[Far(w) for w in weights],
        after=[rows[0]],
    )
    cot = exchange(got[:ranks_rec], "rec", 1)
    turned = [Near(w) for w in got[ranks_rec:]]

    got = call(
        kernel(rows_forward_kernel),
        row_tiles + [out + ("near",) for out in (table, table, wide, probs(plan.all_attr), table)],
        [],
        *rows,
        *turned[:2],
    )
    first, (x, normed, proj, weights, mixed) = got[:ranks_attr], [Near(array) for array in got[ranks_attr:]]
    first = exchange(first, "attr", -1)
    cols = exchange(call(kernel(to_cols_kernel), col_tiles, [], *first), "rec", 1)

    width = max(LANES, plan.all_rec)
    rows_sums, cols_sums = padded(6 * E), padded(18 * E)
    hidden, hidden_wide = ((FF, count), BF), ((FF, count), F32)
    got = call(
        kernel(cols_kernel),
        col_tiles + [out + ("near",) for out in (table, table, table, hidden, table, hidden, table, wide)],
        [table, wide, probs(width), table, hidden_wide, hidden_wide, ((width, width), F32), table],
        *cols,
        *cot,
        train_split.reshape(1, -1),
        Far(qkv_samp),
        Far(out_samp),
        Far(up_weight),
        turned[5],
        turned[2],
        turned[3],
        turned[4],
    )
    grads, saved = exchange(got[:ranks_rec], "rec", -1), [Near(array) for array in got[ranks_rec:]]
    near, far = bits_of("attr"), bits_of("rec")
    keep, send = call(
        cols_sums_kernel, [((cols_sums // 2, LANES), BF)] * 2, [((cols_sums, LANES), BF)], *saved
    )
    sums = Total(keep, swap(send, "attr", near[0]))
    rows_grads = call(kernel(to_rows_kernel), row_tiles, [], *grads, after=[keep])
    grads = exchange(rows_grads, "attr", 1)
    for bit in near[1:]:
        sums.halve("attr", bit)
    mark = sums.add(far[0])

    keep, send, grad, grad_proj = call(
        kernel(rows_back_kernel),
        [((rows_sums // 2, LANES), BF)] * 2 + [table + ("near",), wide + ("near",)],
        [((rows_sums, LANES), BF), table],
        *grads,
        Far(out_attr),
        normed,
        proj,
        weights,
        mixed,
        after=mark,
    )
    row_sums = Total(keep, swap(send, "attr", near[0]))
    mark = []
    for bit in near[1:]:
        mark = row_sums.halve("attr", bit, after=mark)
    for bit in far[1:]:
        mark = sums.add(bit, after=mark)
    grads = call(
        kernel(rows_end_kernel), row_tiles, [], Far(qkv_attr), x, Near(grad), Near(grad_proj), after=mark
    )
    row_sums.add(far[0], after=mark)
    grads = exchange(grads, "attr", -1)
    mark = grads[1:]
    for bit in far[1:]:
        mark = row_sums.add(bit, after=mark)
    mark = sums.add(after=mark)

    def last_sum():
        last = row_sums.add(after=mark)
        return last, last

    last, parts = sums.spread_after(near, last_sum)

    def middle():
        (cells_out,) = call(kernel(join_kernel), [(cells.shape, BF)], [((count, E), F32)], *grads, after=last)
        weights_out = call(
            functools.partial(finish_cols_kernel, factor, near),
            [((E, 3 * E), F32), ((E, E), F32), ((E, FF), F32), ((E, FF), F32)],
            [((cols_sums, LANES), BF)],
            *parts,
        )
        results = [cells_out, *weights_out]
        return results, [Far(cells_out), Far(weights_out[0])]

    results, row_parts = row_sums.spread_after(near, middle)
    grad_cells, grad_qkv_samp, grad_out_samp, grad_up, grad_down = results
    grad_qkv_attr, grad_out_attr = call(
        functools.partial(finish_rows_kernel, factor, near),
        [((E, 3 * E), F32), ((E, E), F32)],
        [((rows_sums, LANES), BF)],
        *row_parts,
    )
    grad_down = grad_down.T
    return (grad_cells, grad_qkv_attr, grad_out_attr, grad_qkv_samp, grad_out_samp, grad_up, grad_down)


def solution(mesh):
    own = P(("groups", "rec"), "attr")
    in_specs = (own, own) + (P(),) * 6 + (P("groups"),)
    out_specs = (own,) + (P("groups", None),) * 6
    return jax.shard_map(local, mesh=mesh, in_specs=in_specs, out_specs=out_specs, check_vma=False)
```

```python
import functools
import math
from typing import NamedTuple

import jax
import jax.numpy as jnp
from jax import lax
from jax.experimental import pallas as pl
from jax.experimental.pallas import tpu as pltpu
from jax.sharding import PartitionSpec as P

E = 192
HEADS = 6
FF = 768
HEAD = E // HEADS
LANES = 128
FORWARD_GROUP = 1
BACK_GROUP = 3
WIDE_FORWARD_GROUP = 3
WIDE_BACK_GROUP = 2
VMEM = 24 * 1024 * 1024
BF = jnp.bfloat16
F32 = jnp.float32
EXP2 = math.log2(math.e) / math.sqrt(HEAD)
SCALE = 1.0 / math.sqrt(HEAD)
HALF_ROOT = math.sqrt(0.5)
BELL_EXP2 = -0.5 * math.log2(math.e)
BELL = 1.0 / math.sqrt(2.0 * math.pi)


def nn(left, right):
    return lax.dot_general(left, right, (((1,), (0,)), ((), ())), preferred_element_type=F32)


def nt(left, right):
    return lax.dot_general(left, right, (((1,), (1,)), ((), ())), preferred_element_type=F32)


def tn(left, right):
    return lax.dot_general(left, right, (((0,), (0,)), ((), ())), preferred_element_type=F32)


def digits(index, sizes):
    out = []
    for size in reversed(sizes):
        if size & (size - 1) == 0:
            out.append(index & (size - 1))
            index = index >> (size.bit_length() - 1)
        else:
            out.append(lax.rem(index, size))
            index = lax.div(index, size)
    return out[::-1]


def wrap(index, size):
    return digits(index + size, (size,))[0]


def one_hot(rows, source):
    own = lax.broadcasted_iota(jnp.int32, (rows, source.shape[1]), 0)
    return jnp.where(own == source, 1.0, 0.0).astype(BF)


def lane_index(size):
    return lax.broadcasted_iota(jnp.int32, (1, size), 1)


def eye(size):
    return one_hot(size, lane_index(size))


def side_by_side(refs):
    return jnp.concatenate([ref[...] for ref in refs], axis=1)


def put_tiles(refs, table):
    width = refs[0].shape[1]
    for position, ref in enumerate(refs):
        ref[...] = table[:, position * width : (position + 1) * width].astype(ref.dtype)


class Plan:
    def __init__(self, cells, ranks_rec, ranks_attr):
        self.ranks_rec, self.ranks_attr = ranks_rec, ranks_attr
        self.rec, self.attr = cells.shape[0], cells.shape[1] // E
        self.cells = self.rec * self.attr
        self.own_rec = self.rec // ranks_attr
        self.own_attr = self.attr // ranks_rec
        self.all_rec = self.rec * ranks_rec
        self.all_attr = self.attr * ranks_attr
        self.row_tile = self.own_rec * self.attr
        self.col_tile = self.rec * self.own_attr

    def row_digits(self, index):
        return digits(index, (self.ranks_attr, self.own_rec, self.attr))

    def col_digits(self, index):
        return digits(index, (self.ranks_rec, self.ranks_attr, self.own_rec, self.own_attr))

    def record_of(self, step, own):
        return self.own_rec * wrap(step + lax.axis_index("attr"), self.ranks_attr) + own

    def attr_of(self, step, own):
        return self.own_attr * wrap(step + lax.axis_index("rec"), self.ranks_rec) + own

    def rows_from_owned(self):
        step, own, attr = self.row_digits(lane_index(self.cells))
        return attr * self.rec + self.record_of(step, own)

    def cols_from_owned(self):
        far, near, own, attr = self.col_digits(lane_index(self.cells))
        return self.attr_of(far, attr) * self.rec + self.record_of(near, own)

    def cols_from_rows(self):
        far, near, own, attr = self.col_digits(lane_index(self.cells))
        return (near * self.own_rec + own) * self.attr + self.attr_of(far, attr)

    def grouped_from_rows(self):
        own, step, attr = digits(lane_index(self.cells), (self.own_rec, self.ranks_attr, self.attr))
        return (step * self.own_rec + own) * self.attr + attr

    def grouped_from_cols(self):
        attr, place = digits(lane_index(self.cells), (self.own_attr, self.all_rec))
        return place * self.own_attr + attr


def split_kernel(plan, to_rows, wait, table_ref, *refs):
    wait()
    outs, rows = refs[:-1], refs[-1]
    for pair in range(plan.attr // 2):
        both = table_ref[:, 2 * E * pair : 2 * E * (pair + 1)].astype(F32)
        for side in range(2):
            start = (2 * pair + side) * plan.rec
            rows[start : start + plan.rec, :] = both[:, side * E : (side + 1) * E]
    turned = nt(eye(E), rows[...].astype(BF)).astype(BF)
    source = plan.rows_from_owned() if to_rows else plan.cols_from_owned()
    put_tiles(outs, nn(turned, one_hot(plan.cells, source)))


def join_kernel(plan, wait, *refs):
    tiles, out_ref, rows = refs[:-2], refs[-2], refs[-1]
    rows[...] = nt(one_hot(plan.cells, plan.rows_from_owned()), side_by_side(tiles))
    for pair in range(plan.attr // 2):
        start = 2 * pair * plan.rec
        both = [rows[start + side * plan.rec : start + (side + 1) * plan.rec, :] for side in range(2)]
        out_ref[:, 2 * E * pair : 2 * E * (pair + 1)] = jnp.concatenate(both, axis=1).astype(BF)


def to_cols_kernel(plan, wait, *refs):
    tiles, outs = refs[: plan.ranks_attr], refs[plan.ranks_attr :]
    put_tiles(outs, nn(side_by_side(tiles), one_hot(plan.cells, plan.cols_from_rows())))


def to_rows_kernel(plan, wait, *refs):
    tiles, outs = refs[: plan.ranks_rec], refs[plan.ranks_rec :]
    put_tiles(outs, nt(side_by_side(tiles), one_hot(plan.cells, plan.cols_from_rows())))


def turn_kernel(wait, weights, turned, kept):
    for source, target in zip(weights, turned):
        target[...] = source[...].astype(F32).T.astype(BF)
    for source, target in zip(weights, kept):
        target[...] = source[...]


def split_turn_kernel(plan, wait, table_ref, *refs):
    split_kernel(plan, False, wait, table_ref, *refs[2 : 2 + plan.ranks_rec], refs[-1])
    turn_kernel(wait, refs[:2], refs[2 + plan.ranks_rec : 4 + plan.ranks_rec], refs[4 + plan.ranks_rec : -1])


def turn_more_kernel(wait, *refs):
    wait()
    turn_kernel(wait, refs[:4], refs[4:8], refs[8:])


def norm(table):
    center = table - jnp.mean(table, axis=0, keepdims=True)
    spread = jnp.mean(center * center, axis=0, keepdims=True)
    root = lax.rsqrt(spread + 1e-05)
    return center * root, root


def norm_back(grad, normed, root):
    along = jnp.mean(grad * normed, axis=0, keepdims=True)
    return root * (grad - jnp.mean(grad, axis=0, keepdims=True) - normed * along)


def blocks_of(width, total):
    return [slice(start, start + width) for start in range(0, total, width)]


def heads_of(ref, part, head, cols):
    start = part * E + head * HEAD
    return ref[start : start + HEAD, cols]


def staged(count, group, *stages):
    held = {}
    groups = [range(start, min(start + group, count)) for start in range(0, count, group)]
    for step in range(len(groups) + len(stages) - 1):
        for lag, stage in enumerate(stages):
            if 0 <= step - lag < len(groups):
                for unit in groups[step - lag]:
                    held[unit] = stage(unit, held.get(unit))


def units_of(total, width):
    step = min(2 * LANES, width)
    return [
        (place, head, start, step, start == 0, start + step == width)
        for place in range(total // width)
        for head in range(HEADS)
        for start in range(0, width, step)
    ]


def attend(x_ref, normed_ref, proj_ref, probs_ref, mixed_ref, qkv_t, out_t, width, mask_ref):
    total = x_ref.shape[1]
    for cols in blocks_of(2 * LANES, total):
        normed_ref[:, cols] = norm(x_ref[:, cols].astype(F32))[0].astype(BF)
    for cols in blocks_of(2 * LANES, total):
        proj_ref[:, cols] = nn(qkv_t[...], normed_ref[:, cols]).astype(BF)
    units = units_of(total, width)

    def score(unit, _):
        place, head, start, step, _, _ = units[unit]
        cols = slice(place * width + start, place * width + start + step)
        keys = slice(place * width, (place + 1) * width)
        return tn(heads_of(proj_ref, 1, head, keys), heads_of(proj_ref, 0, head, cols))

    def weigh(unit, scores):
        place, head, start, step, _, _ = units[unit]
        if mask_ref is not None:
            scores = scores + mask_ref[:, start : start + step]
        expo = jnp.exp2((scores - jnp.max(scores, axis=0, keepdims=True)) * EXP2)
        probs = (expo * (1.0 / jnp.sum(expo, axis=0, keepdims=True))).astype(BF)
        probs_ref[place * HEADS + head, :, start : start + step] = probs
        return probs

    def mix(unit, probs):
        place, head, start, step, _, _ = units[unit]
        value = heads_of(proj_ref, 2, head, slice(place * width, (place + 1) * width))
        cols = slice(place * width + start, place * width + start + step)
        mixed_ref[head * HEAD : (head + 1) * HEAD, cols] = nn(value, probs).astype(BF)

    staged(len(units), FORWARD_GROUP if width <= LANES else WIDE_FORWARD_GROUP, score, weigh, mix)
    return [
        x_ref[:, cols].astype(F32) + nn(out_t[...], mixed_ref[:, cols])
        for cols in blocks_of(2 * LANES, total)
    ]


def attend_back(grad_ref, proj_ref, probs_ref, grad_proj_ref, grad_mixed_ref, out, width):
    total = grad_ref.shape[1]
    for cols in blocks_of(2 * LANES, total):
        grad_mixed_ref[:, cols] = nn(out[...], grad_ref[:, cols]).astype(BF)
    units = units_of(total, width)
    sums = {}

    def spans(unit):
        place, head, start, step, _, _ = units[unit]
        rows = slice(head * HEAD, (head + 1) * HEAD)
        keys = slice(place * width, (place + 1) * width)
        return rows, slice(place * width + start, place * width + start + step), keys

    def probs_of(unit):
        place, head, start, step, _, _ = units[unit]
        return probs_ref[place * HEADS + head, :, start : start + step]

    def to_probs(unit, _):
        rows, cols, keys = spans(unit)
        return tn(heads_of(proj_ref, 2, units[unit][1], keys), grad_mixed_ref[rows, cols])

    def to_scores(unit, grad_probs):
        wide = probs_of(unit).astype(F32)
        moved = grad_probs * wide
        return (moved - wide * jnp.sum(moved, axis=0, keepdims=True)).astype(BF)

    def to_proj(unit, grad_scores):
        _, head, _, _, first, last = units[unit]
        rows, cols, keys = spans(unit)
        query, key = heads_of(proj_ref, 0, head, cols), heads_of(proj_ref, 1, head, keys)
        grad_proj_ref[rows, cols] = (nn(key, grad_scores) * SCALE).astype(BF)
        both = nt(query, grad_scores), nt(grad_mixed_ref[rows, cols], probs_of(unit))
        if not first:
            both = both[0] + sums["key"], both[1] + sums["value"]
        sums["key"], sums["value"] = both
        if last:
            grad_proj_ref[E + rows.start : E + rows.stop, keys] = (both[0] * SCALE).astype(BF)
            grad_proj_ref[2 * E + rows.start : 2 * E + rows.stop, keys] = both[1].astype(BF)

    staged(len(units), BACK_GROUP if width <= LANES else WIDE_BACK_GROUP, to_probs, to_scores, to_proj)


def project_back(grad_ref, x_ref, grad_proj_ref, qkv):
    results = []
    for cols in blocks_of(2 * LANES, x_ref.shape[1]):
        grad_normed = nn(qkv[...], grad_proj_ref[:, cols]).astype(BF).astype(F32)
        normed, root = norm(x_ref[:, cols].astype(F32))
        results.append(norm_back(grad_normed, normed, root) + grad_ref[:, cols].astype(F32))
    return results


def put_halves(bit, sums_ref, keep_ref, send_ref):
    rows, mine = keep_ref.shape[0], has_bit("attr", bit)
    for ref, half in ((keep_ref, mine), (send_ref, 1 - mine)):
        ref[...] = sums_ref[pl.ds(pl.multiple_of(half * rows, rows), rows), :]


def put_attend_grads(out_ref, normed_ref, grad_proj_ref, mixed_ref, grad_ref):
    qkv = nt(normed_ref[...], grad_proj_ref[...])
    out = nt(mixed_ref[...], grad_ref[...])
    whole = 3 * E // LANES
    for tile in range(whole):
        out_ref[tile * E : (tile + 1) * E, :] = qkv[:, tile * LANES : (tile + 1) * LANES].astype(BF)
    mixed = jnp.concatenate([qkv[:, whole * LANES :], out[:, LANES:]], axis=1)
    out_ref[whole * E : (whole + 1) * E, :] = mixed.astype(BF)
    out_ref[(whole + 1) * E : (whole + 2) * E, :] = out[:, :LANES].astype(BF)


def take_attend_grads(in_ref, first, qkv_ref, out_ref, factor):
    whole = 3 * E // LANES

    def tile(number):
        return in_ref[first + number * E : first + (number + 1) * E, :].astype(F32) * factor

    for number in range(whole):
        qkv_ref[:, number * LANES : (number + 1) * LANES] = tile(number)
    mixed = tile(whole)
    qkv_ref[:, whole * LANES :] = mixed[:, : LANES // 2]
    out_ref[:, :LANES] = tile(whole + 1)
    out_ref[:, LANES:] = mixed[:, LANES // 2 :]


def rows_forward_kernel(plan, wait, *refs):
    tiles, refs = refs[: plan.ranks_attr], refs[plan.ranks_attr :]
    (qkv_t, out_t), refs = refs[:2], refs[2:]
    outs, refs = refs[: plan.ranks_attr], refs[plan.ranks_attr :]
    x_ref, normed_ref, proj_ref, probs_ref, mixed_ref = refs
    order = one_hot(plan.cells, plan.grouped_from_rows())
    x_ref[...] = nn(side_by_side(tiles), order).astype(BF)
    first = attend(x_ref, normed_ref, proj_ref, probs_ref, mixed_ref, qkv_t, out_t, plan.all_attr, None)
    put_tiles(outs, nt(jnp.concatenate(first, axis=1).astype(BF), order))


def rows_back_kernel(plan, wait, *refs):
    tiles, refs = refs[: plan.ranks_attr], refs[plan.ranks_attr :]
    (out, normed_ref, proj_ref, probs_ref, mixed_ref), refs = refs[:5], refs[5:]
    keep_ref, send_ref, grad_ref, grad_proj_ref, sums_ref, grad_mixed_ref = refs
    order = one_hot(plan.cells, plan.grouped_from_rows())
    grad_ref[...] = nn(side_by_side(tiles), order).astype(BF)
    wait()
    attend_back(grad_ref, proj_ref, probs_ref, grad_proj_ref, grad_mixed_ref, out, plan.all_attr)
    put_attend_grads(sums_ref, normed_ref, grad_proj_ref, mixed_ref, grad_ref)
    put_halves(bits_of("attr")[0], sums_ref, keep_ref, send_ref)


def end_kernel(plan, by_rows, wait, qkv, x_ref, grad_ref, grad_proj_ref, *outs):
    order = one_hot(plan.cells, plan.grouped_from_rows() if by_rows else plan.grouped_from_cols())
    wait()
    grads = project_back(grad_ref, x_ref, grad_proj_ref, qkv)
    put_tiles(outs, nt(jnp.concatenate(grads, axis=1).astype(BF), order))


def cols_kernel(plan, wait, *refs):
    count = plan.ranks_rec
    tiles, cot_tiles, refs = refs[:count], refs[count : 2 * count], refs[2 * count :]
    (train_ref, out, up, down, qkv_t, out_t, up_t), refs = refs[:7], refs[7:]
    normed_ref, mixed_ref, normed_second_ref, hidden_ref, cot_ref, grad_pre_ref, grad_ref, grad_proj_ref = refs[:8]
    x_ref, proj_ref, probs_ref, second_ref, slope_ref, wide_ref, mask_ref, grad_mixed_ref = refs[8:]
    width = max(LANES, plan.all_rec)
    order = one_hot(plan.cells, plan.grouped_from_cols())
    x_ref[...] = nn(side_by_side(tiles), order).astype(BF)

    row = lax.broadcasted_iota(jnp.int32, (width, 1), 0)
    sequence, far, near, own = digits(row, (width // plan.all_rec, plan.ranks_rec, plan.ranks_attr, plan.own_rec))
    record = plan.rec * wrap(lax.axis_index("rec") - far, plan.ranks_rec) + plan.record_of(near, own)
    chosen = (record == lane_index(plan.all_rec)) & (train_ref[...] > 0)
    allowed = jnp.max(jnp.where(chosen, 1.0, 0.0), axis=1, keepdims=True) > 0.5
    asker = digits(lane_index(width), (width // plan.all_rec, plan.all_rec))[0]
    mask_ref[...] = jnp.where(allowed & (sequence == asker), 0.0, -1e30)

    second = attend(x_ref, normed_ref, proj_ref, probs_ref, mixed_ref, qkv_t, out_t, width, mask_ref)
    for cols, value in zip(blocks_of(2 * LANES, plan.cells), second):
        second_ref[:, cols] = value.astype(BF)
        normed_second_ref[:, cols] = norm(second_ref[:, cols].astype(F32))[0].astype(BF)
    wide_ref[...] = nn(up_t[...], normed_second_ref[...])
    step = 32
    for start in range(0, FF, step):
        rows = slice(start, start + step)
        pre = wide_ref[rows, :]
        gate = 0.5 + 0.5 * lax.erf(pre * HALF_ROOT)
        hidden_ref[rows, :] = (pre * gate).astype(BF)
        slope_ref[rows, :] = gate + pre * (jnp.exp2(pre * pre * BELL_EXP2) * BELL)

    cot_ref[...] = nn(side_by_side(cot_tiles), order).astype(BF)
    wait()
    wide_ref[...] = nn(down[...], cot_ref[...])
    step = 64
    for start in range(0, FF, step):
        rows = slice(start, start + step)
        grad_pre_ref[rows, :] = (wide_ref[rows, :] * slope_ref[rows, :]).astype(BF)
    for cols in blocks_of(2 * LANES, plan.cells):
        grad_normed = nn(up[...], grad_pre_ref[:, cols]).astype(BF).astype(F32)
        table, root = norm(second_ref[:, cols].astype(F32))
        grad_ref[:, cols] = (norm_back(grad_normed, table, root) + cot_ref[:, cols].astype(F32)).astype(BF)
    attend_back(grad_ref, proj_ref, probs_ref, grad_proj_ref, grad_mixed_ref, out, width)


def cols_sums_kernel(wait, *refs):
    normed_ref, mixed_ref, normed_second_ref, hidden_ref, cot_ref, grad_pre_ref, grad_ref, grad_proj_ref = refs[:8]
    keep_ref, send_ref, sums_ref = refs[8:]
    for base, grad_weight in (
        (6 * E, nt(normed_second_ref[...], grad_pre_ref[...])),
        (12 * E, nt(cot_ref[...], hidden_ref[...])),
    ):
        for tile in range(FF // LANES):
            rows = slice(base + tile * E, base + (tile + 1) * E)
            sums_ref[rows, :] = grad_weight[:, tile * LANES : (tile + 1) * LANES].astype(BF)
    put_attend_grads(sums_ref, normed_ref, grad_proj_ref, mixed_ref, grad_ref)
    put_halves(bits_of("attr")[0], sums_ref, keep_ref, send_ref)


def finish_cols_kernel(factor, bits, wait, *refs):
    parts, (qkv_ref, out_ref, up_ref, down_ref, sums_ref) = refs[:-5], refs[-5:]
    lay_out(bits, parts, sums_ref)
    take_attend_grads(sums_ref, 0, qkv_ref, out_ref, factor)
    for base, ref in ((6 * E, up_ref), (12 * E, down_ref)):
        for tile in range(FF // LANES):
            rows = slice(base + tile * E, base + (tile + 1) * E)
            ref[:, tile * LANES : (tile + 1) * LANES] = sums_ref[rows, :].astype(F32) * factor


def finish_rows_kernel(factor, bits, wait, *refs):
    parts, (qkv_ref, out_ref, sums_ref) = refs[:-3], refs[-3:]
    lay_out(bits, parts, sums_ref)
    take_attend_grads(sums_ref, 0, qkv_ref, out_ref, factor)


class Far(NamedTuple):
    array: jax.Array


class Near(NamedTuple):
    array: jax.Array


def in_hbm(array):
    return pltpu.with_memory_space_constraint(array, pltpu.HBM)


def call(body, outs, scratch, *args, after=()):
    far = [n for n, arg in enumerate(args) if isinstance(arg, Far)]
    n_in, n_after, n_out, n_far = len(args), len(after), len(outs), len(far)
    whole, anywhere = pl.BlockSpec(memory_space=pltpu.VMEM), pl.BlockSpec(memory_space=pl.ANY)
    hbm = pl.BlockSpec(memory_space=pltpu.HBM)

    def kernel(*refs):
        given, refs = list(refs[:n_in]), refs[n_in + n_after :]
        copies = []
        if far:
            held, sems, refs = refs[-1 - n_far : -1], refs[-1], refs[: -1 - n_far]
            for order, (number, ref) in enumerate(zip(far, held)):
                copies.append(pltpu.make_async_copy(given[number], ref, sems.at[order]))
                given[number] = ref
        for copy in copies:
            copy.start()

        def wait():
            for copy in copies:
                copy.wait()

        body(wait, *given, *refs)

    arrays = []
    for arg in args:
        space = {Far: pltpu.HBM, Near: pltpu.VMEM}.get(type(arg))
        arrays.append(arg if space is None else pltpu.with_memory_space_constraint(arg.array, space))
    held = [pltpu.VMEM(arrays[n].shape, arrays[n].dtype) for n in far]
    return pl.pallas_call(
        kernel,
        out_shape=[
            (pltpu.VMEM if out[2:] else jax.ShapeDtypeStruct)(out[0], out[1]) for out in outs
        ],
        in_specs=[hbm if isinstance(arg, Far) else whole for arg in args] + [anywhere] * n_after,
        out_specs=[whole] * n_out,
        scratch_shapes=[pltpu.VMEM(shape, dtype) for shape, dtype in scratch]
        + held
        + ([pltpu.SemaphoreType.DMA((n_far,))] if far else []),
        compiler_params=pltpu.CompilerParams(vmem_limit_bytes=VMEM),
    )(*arrays, *[in_hbm(arg.array) if isinstance(arg, Far) else arg for arg in after])


def exchange(tiles, axis, sign):
    size = len(tiles)
    return [tiles[0]] + [
        lax.ppermute(tiles[k], axis, [(i, (i + sign * k) % size) for i in range(size)])
        for k in range(1, size)
    ]


def swap(part, axis, bit):
    size = lax.axis_size(axis)
    return lax.ppermute(part, axis, [(i, i ^ bit) for i in range(size)])


def has_bit(axis, bit):
    return digits(lax.axis_index(axis) // bit, (2,))[0]


def pass_kernel(wait, source, target):
    target[...] = source[...]


def row_tiles_of(arrays):
    return [(array.shape, array.dtype) for array in arrays]


def halve_kernel(axis, bit, wait, *refs):
    parts, (keep, send) = refs[:-2], refs[-2:]
    rows, mine = keep.shape[0], has_bit(axis, bit)
    for ref, half in ((keep, mine), (send, 1 - mine)):
        place = pl.ds(pl.multiple_of(half * rows, rows), rows)
        ref[...] = sum(part[place, :].astype(F32) for part in parts).astype(BF)


def add_kernel(wait, *refs):
    refs[-1][...] = sum(part[...].astype(F32) for part in refs[:-1]).astype(BF)


def lay_out_kernel(axis, bit, wait, own_ref, other_ref, out_ref):
    rows = own_ref.shape[0]
    mine = has_bit(axis, bit)
    for ref, half in ((own_ref, mine), (other_ref, 1 - mine)):
        out_ref[pl.ds(pl.multiple_of(half * rows, rows), rows), :] = ref[...]


def lay_out(bits, parts, rows_ref):
    rows = parts[0].shape[0]
    for number, ref in enumerate(parts):
        place = 0
        for order, bit in enumerate(bits):
            own = has_bit("attr", bit)
            place = place * 2 + (1 - own if number >> order & 1 else own)
        rows_ref[pl.ds(pl.multiple_of(place * rows, rows), rows), :] = ref[...]


def bits_of(axis):
    return [1 << n for n in range(lax.axis_size(axis).bit_length() - 1)]


class Total:
    def __init__(self, *parts):
        self.parts, self.rows = list(parts), parts[0].shape[0]

    def halve(self, axis, bit, after=()):
        self.rows //= 2
        keep, send = call(
            functools.partial(halve_kernel, axis, bit), [((self.rows, LANES), BF)] * 2, [], *self.parts, after=after
        )
        self.parts = [keep, swap(send, axis, bit)]
        return [keep]

    def back(self, axis, bit, after=()):
        self.rows *= 2
        body = functools.partial(lay_out_kernel, axis, bit)
        (part,) = call(body, [((self.rows, LANES), BF)], [], *self.parts, after=after)
        self.parts = [part]
        return [part]

    def add(self, bit=0, after=()):
        (part,) = call(add_kernel, [((self.rows, LANES), BF)], [], *self.parts, after=after)
        self.parts = [part] + ([swap(part, "rec", bit)] if bit else [])
        return [part]

    def spread_after(self, bits, middle):
        done = {0: self.parts[0]}
        for order, bit in reversed(list(enumerate(bits[1:], 1))):
            done.update({number | 1 << order: swap(part, "attr", bit) for number, part in sorted(done.items())})
        near = {1: swap(done[0], "attr", bits[0])}
        results, after = middle()
        for number, part in sorted(done.items()):
            if number:
                (part,) = call(add_kernel, [(part.shape, BF)], [], part, after=after)
                near[number | 1] = swap(part, "attr", bits[0])
        done.update(near)
        return results, [done[number] for number in sorted(done)]


def padded(rows):
    devices = 2 * lax.axis_size("attr")
    return -(-rows // (16 * devices)) * 16 * devices


def local(
    cells, cotangent, qkv_attr, out_attr, qkv_samp, out_samp, up_weight, down_weight, train_split
):
    ranks_rec, ranks_attr = lax.axis_size("rec"), lax.axis_size("attr")
    plan = Plan(cells, ranks_rec, ranks_attr)
    count = plan.cells
    factor = 1.0 / math.sqrt(plan.all_rec * plan.all_attr)
    row_tiles = [((E, plan.row_tile), BF)] * ranks_attr
    col_tiles = [((E, plan.col_tile), BF)] * ranks_rec
    table, wide = ((E, count), BF), ((3 * E, count), BF)

    def probs(width):
        return ((count // width * HEADS, width, width), BF)

    def kernel(body, *static):
        return functools.partial(body, plan, *static)

    rows = call(kernel(split_kernel, True), row_tiles, [((count, E), F32)], Far(cells))
    rows = exchange(rows, "attr", 1)
    weights = (qkv_attr, out_attr)
    got = call(
        kernel(split_turn_kernel),
        col_tiles + [(w.shape[::-1], BF, "near") for w in weights] + [(w.shape, BF, "near") for w in weights],
        [((count, E), F32)],
        Far(cotangent),
        *[Far(w) for w in weights],
        after=[rows[0]],
    )
    cot = exchange(got[:ranks_rec], "rec", 1)
    turned, kept = ([Near(w) for w in part] for part in (got[ranks_rec:-2], got[-2:]))

    got = call(
        kernel(rows_forward_kernel),
        row_tiles + [out + ("near",) for out in (table, table, wide, probs(plan.all_attr), table)],
        [],
        *rows,
        *turned[:2],
    )
    first, (x, normed, proj, weights, mixed) = got[:ranks_attr], [Near(array) for array in got[ranks_attr:]]
    first = exchange(first, "attr", -1)
    cols = exchange(call(kernel(to_cols_kernel), col_tiles, [], *first), "rec", 1)
    weights_more = (qkv_samp, out_samp, up_weight, down_weight.T)
    got = call(
        turn_more_kernel,
        [(w.shape[::-1], BF, "near") for w in weights_more] + [(w.shape, BF, "near") for w in weights_more[:3]],
        [],
        *[Far(w) for w in weights_more],
        after=cols[:1],
    )
    turned, kept = turned + [Near(w) for w in got[:4]], kept + [Near(w) for w in got[4:]]

    width = max(LANES, plan.all_rec)
    rows_sums, cols_sums = padded(6 * E), padded(18 * E)
    hidden, hidden_wide = ((FF, count), BF), ((FF, count), F32)
    got = call(
        kernel(cols_kernel),
        [out + ("near",) for out in (table, table, table, hidden, table, hidden, table, wide, table)],
        [wide, probs(width), table, hidden_wide, hidden_wide, ((width, width), F32), table],
        *cols,
        *cot,
        train_split.reshape(1, -1),
        kept[3],
        kept[4],
        turned[5],
        turned[2],
        turned[3],
        turned[4],
    )
    saved = [Near(array) for array in got]
    near, far = bits_of("attr"), bits_of("rec")
    keep, send = call(
        cols_sums_kernel, [((cols_sums // 2, LANES), BF)] * 2, [((cols_sums, LANES), BF)], *saved[:8]
    )
    grads = call(kernel(end_kernel, False), col_tiles, [], kept[2], saved[8], *saved[6:8], after=[keep])
    sums = Total(keep, swap(send, "attr", near[0]))
    mark = grads[:1]
    for bit in near[1:]:
        mark = sums.halve("attr", bit, after=mark)
    (last,) = call(pass_kernel, row_tiles_of(grads[-1:]), [], grads[-1], after=mark)
    grads = exchange([*grads[:-1], last], "rec", -1)
    arrived = grads[1:]
    rows_grads = call(kernel(to_rows_kernel), row_tiles, [], *grads, after=mark)
    grads = exchange(rows_grads, "attr", 1)
    mark = sums.add(far[0], after=arrived)

    keep, send, grad, grad_proj = call(
        kernel(rows_back_kernel),
        [((rows_sums // 2, LANES), BF)] * 2 + [table + ("near",), wide + ("near",)],
        [((rows_sums, LANES), BF), table],
        *grads,
        kept[1],
        normed,
        proj,
        weights,
        mixed,
        after=mark,
    )
    row_sums = Total(keep, swap(send, "attr", near[0]))
    mark = [keep]
    for bit in far[1:]:
        mark = sums.add(bit, after=mark)
    for bit in near[1:]:
        mark = row_sums.halve("attr", bit, after=mark)
    grads = call(
        kernel(end_kernel, True), row_tiles, [], kept[0], x, Near(grad), Near(grad_proj), after=mark
    )
    row_sums.add(far[0], after=mark)
    grads = exchange(grads, "attr", -1)
    mark = grads[1:]
    for bit in far[1:]:
        mark = row_sums.add(bit, after=mark)
    mark = sums.add(after=mark)

    def last_sum():
        last = row_sums.add(after=mark)
        return last, last

    last, parts = sums.spread_after(near, last_sum)

    def middle():
        (cells_out,) = call(kernel(join_kernel), [(cells.shape, BF)], [((count, E), F32)], *grads, after=last)
        weights_out = call(
            functools.partial(finish_cols_kernel, factor, near),
            [((E, 3 * E), F32), ((E, E), F32), ((E, FF), F32), ((E, FF), F32)],
            [((cols_sums, LANES), BF)],
            *parts,
        )
        results = [cells_out, *weights_out]
        return results, [Far(cells_out), Far(weights_out[0])]

    results, row_parts = row_sums.spread_after(near, middle)
    grad_cells, grad_qkv_samp, grad_out_samp, grad_up, grad_down = results
    grad_qkv_attr, grad_out_attr = call(
        functools.partial(finish_rows_kernel, factor, near),
        [((E, 3 * E), F32), ((E, E), F32)],
        [((rows_sums, LANES), BF)],
        *row_parts,
    )
    grad_down = grad_down.T
    return (grad_cells, grad_qkv_attr, grad_out_attr, grad_qkv_samp, grad_out_samp, grad_up, grad_down)


def solution(mesh):
    own = P(("groups", "rec"), "attr")
    in_specs = (own, own) + (P(),) * 6 + (P("groups"),)
    out_specs = (own,) + (P("groups", None),) * 6
    return jax.shard_map(local, mesh=mesh, in_specs=in_specs, out_specs=out_specs, check_vma=False)
```

```python
import functools
import math
from typing import NamedTuple

import jax
import jax.numpy as jnp
from jax import lax
from jax.experimental import pallas as pl
from jax.experimental.pallas import tpu as pltpu
from jax.sharding import PartitionSpec as P

E = 192
HEADS = 6
FF = 768
HEAD = E // HEADS
LANES = 128
FORWARD_GROUP = 1
BACK_GROUP = 3
WIDE_FORWARD_GROUP = 3
WIDE_BACK_GROUP = 2
VMEM = 24 * 1024 * 1024
BF = jnp.bfloat16
F32 = jnp.float32
EXP2 = math.log2(math.e) / math.sqrt(HEAD)
SCALE = 1.0 / math.sqrt(HEAD)
HALF_ROOT = math.sqrt(0.5)
BELL_EXP2 = -0.5 * math.log2(math.e)
BELL = 1.0 / math.sqrt(2.0 * math.pi)


def nn(left, right):
    return lax.dot_general(left, right, (((1,), (0,)), ((), ())), preferred_element_type=F32)


def nt(left, right):
    return lax.dot_general(left, right, (((1,), (1,)), ((), ())), preferred_element_type=F32)


def tn(left, right):
    return lax.dot_general(left, right, (((0,), (0,)), ((), ())), preferred_element_type=F32)


def digits(index, sizes):
    out = []
    for size in reversed(sizes):
        if size & (size - 1) == 0:
            out.append(index & (size - 1))
            index = index >> (size.bit_length() - 1)
        else:
            out.append(lax.rem(index, size))
            index = lax.div(index, size)
    return out[::-1]


def wrap(index, size):
    return digits(index + size, (size,))[0]


def one_hot(rows, source):
    own = lax.broadcasted_iota(jnp.int32, (rows, source.shape[1]), 0)
    return jnp.where(own == source, 1.0, 0.0).astype(BF)


def lane_index(size):
    return lax.broadcasted_iota(jnp.int32, (1, size), 1)


def eye(size):
    return one_hot(size, lane_index(size))


def side_by_side(refs):
    return jnp.concatenate([ref[...] for ref in refs], axis=1)


def put_tiles(refs, table):
    width = refs[0].shape[1]
    for position, ref in enumerate(refs):
        ref[...] = table[:, position * width : (position + 1) * width].astype(ref.dtype)


class Plan:
    def __init__(self, cells, ranks_rec, ranks_attr):
        self.ranks_rec, self.ranks_attr = ranks_rec, ranks_attr
        self.rec, self.attr = cells.shape[0], cells.shape[1] // E
        self.cells = self.rec * self.attr
        self.own_rec = self.rec // ranks_attr
        self.own_attr = self.attr // ranks_rec
        self.all_rec = self.rec * ranks_rec
        self.all_attr = self.attr * ranks_attr
        self.row_tile = self.own_rec * self.attr
        self.col_tile = self.rec * self.own_attr

    def row_digits(self, index):
        return digits(index, (self.ranks_attr, self.own_rec, self.attr))

    def col_digits(self, index):
        return digits(index, (self.ranks_rec, self.ranks_attr, self.own_rec, self.own_attr))

    def record_of(self, step, own):
        return self.own_rec * wrap(step + lax.axis_index("attr"), self.ranks_attr) + own

    def attr_of(self, step, own):
        return self.own_attr * wrap(step + lax.axis_index("rec"), self.ranks_rec) + own

    def rows_from_owned(self):
        step, own, attr = self.row_digits(lane_index(self.cells))
        return attr * self.rec + self.record_of(step, own)

    def cols_from_owned(self):
        far, near, own, attr = self.col_digits(lane_index(self.cells))
        return self.attr_of(far, attr) * self.rec + self.record_of(near, own)

    def cols_from_rows(self):
        far, near, own, attr = self.col_digits(lane_index(self.cells))
        return (near * self.own_rec + own) * self.attr + self.attr_of(far, attr)

    def grouped_from_rows(self):
        own, step, attr = digits(lane_index(self.cells), (self.own_rec, self.ranks_attr, self.attr))
        return (step * self.own_rec + own) * self.attr + attr

    def grouped_from_cols(self):
        attr, place = digits(lane_index(self.cells), (self.own_attr, self.all_rec))
        return place * self.own_attr + attr


def split_kernel(plan, to_rows, wait, table_ref, *refs):
    wait()
    outs, rows = refs[:-1], refs[-1]
    for pair in range(plan.attr // 2):
        both = table_ref[:, 2 * E * pair : 2 * E * (pair + 1)].astype(F32)
        for side in range(2):
            start = (2 * pair + side) * plan.rec
            rows[start : start + plan.rec, :] = both[:, side * E : (side + 1) * E]
    turned = nt(eye(E), rows[...].astype(BF)).astype(BF)
    source = plan.rows_from_owned() if to_rows else plan.cols_from_owned()
    put_tiles(outs, nn(turned, one_hot(plan.cells, source)))


def join_kernel(plan, wait, *refs):
    tiles, out_ref, rows = refs[:-2], refs[-2], refs[-1]
    rows[...] = nt(one_hot(plan.cells, plan.rows_from_owned()), side_by_side(tiles))
    for pair in range(plan.attr // 2):
        start = 2 * pair * plan.rec
        both = [rows[start + side * plan.rec : start + (side + 1) * plan.rec, :] for side in range(2)]
        out_ref[:, 2 * E * pair : 2 * E * (pair + 1)] = jnp.concatenate(both, axis=1).astype(BF)


def to_cols_kernel(plan, wait, *refs):
    tiles, outs = refs[: plan.ranks_attr], refs[plan.ranks_attr :]
    put_tiles(outs, nn(side_by_side(tiles), one_hot(plan.cells, plan.cols_from_rows())))


def to_rows_kernel(plan, wait, *refs):
    tiles, across, outs = refs[: plan.ranks_rec], refs[plan.ranks_rec], refs[plan.ranks_rec + 1 :]
    put_tiles(outs, nt(side_by_side(tiles), across[...]))


def turn_kernel(wait, weights, turned, kept):
    for source, target in zip(weights, turned):
        target[...] = source[...].astype(F32).T.astype(BF)
    for source, target in zip(weights, kept):
        target[...] = source[...]


def split_turn_kernel(plan, wait, table_ref, *refs):
    split_kernel(plan, False, wait, table_ref, *refs[2 : 2 + plan.ranks_rec], refs[-1])
    turn_kernel(wait, refs[:2], refs[2 + plan.ranks_rec : 4 + plan.ranks_rec], refs[4 + plan.ranks_rec : -1])


def prepare_kernel(plan, wait, train_ref, *refs):
    weights, turned, kept, (by_cols, by_rows, across, mask_ref) = refs[:4], refs[4:8], refs[8:11], refs[11:]
    by_cols[...] = one_hot(plan.cells, plan.grouped_from_cols())
    by_rows[...] = one_hot(plan.cells, plan.grouped_from_rows())
    across[...] = one_hot(plan.cells, plan.cols_from_rows())
    width = max(LANES, plan.all_rec)
    row = lax.broadcasted_iota(jnp.int32, (width, 1), 0)
    sequence, far, near, own = digits(row, (width // plan.all_rec, plan.ranks_rec, plan.ranks_attr, plan.own_rec))
    record = plan.rec * wrap(lax.axis_index("rec") - far, plan.ranks_rec) + plan.record_of(near, own)
    chosen = (record == lane_index(plan.all_rec)) & (train_ref[...] > 0)
    allowed = jnp.max(jnp.where(chosen, 1.0, 0.0), axis=1, keepdims=True) > 0.5
    asker = digits(lane_index(width), (width // plan.all_rec, plan.all_rec))[0]
    mask_ref[...] = jnp.where(allowed & (sequence == asker), 0.0, -1e30)
    wait()
    turn_kernel(wait, weights, turned, kept)


def norm(table):
    center = table - jnp.mean(table, axis=0, keepdims=True)
    spread = jnp.mean(center * center, axis=0, keepdims=True)
    root = lax.rsqrt(spread + 1e-05)
    return center * root, root


def norm_back(grad, normed, root):
    along = jnp.mean(grad * normed, axis=0, keepdims=True)
    return root * (grad - jnp.mean(grad, axis=0, keepdims=True) - normed * along)


def blocks_of(width, total):
    return [slice(start, start + width) for start in range(0, total, width)]


def heads_of(ref, part, head, cols):
    start = part * E + head * HEAD
    return ref[start : start + HEAD, cols]


def staged(count, group, *stages):
    held = {}
    groups = [range(start, min(start + group, count)) for start in range(0, count, group)]
    for step in range(len(groups) + len(stages) - 1):
        for lag, stage in enumerate(stages):
            if 0 <= step - lag < len(groups):
                for unit in groups[step - lag]:
                    held[unit] = stage(unit, held.get(unit))


def units_of(total, width):
    step = min(2 * LANES, width)
    return [
        (place, head, start, step, start == 0, start + step == width)
        for place in range(total // width)
        for head in range(HEADS)
        for start in range(0, width, step)
    ]


def attend(x_ref, normed_ref, proj_ref, probs_ref, mixed_ref, qkv_t, out_t, width, mask_ref):
    total = x_ref.shape[1]
    for cols in blocks_of(2 * LANES, total):
        normed_ref[:, cols] = norm(x_ref[:, cols].astype(F32))[0].astype(BF)
    for cols in blocks_of(2 * LANES, total):
        proj_ref[:, cols] = nn(qkv_t[...], normed_ref[:, cols]).astype(BF)
    units = units_of(total, width)

    def score(unit, _):
        place, head, start, step, _, _ = units[unit]
        cols = slice(place * width + start, place * width + start + step)
        keys = slice(place * width, (place + 1) * width)
        return tn(heads_of(proj_ref, 1, head, keys), heads_of(proj_ref, 0, head, cols))

    def weigh(unit, scores):
        place, head, start, step, _, _ = units[unit]
        if mask_ref is not None:
            scores = scores + mask_ref[:, start : start + step]
        expo = jnp.exp2((scores - jnp.max(scores, axis=0, keepdims=True)) * EXP2)
        probs = (expo * (1.0 / jnp.sum(expo, axis=0, keepdims=True))).astype(BF)
        probs_ref[place * HEADS + head, :, start : start + step] = probs
        return probs

    def mix(unit, probs):
        place, head, start, step, _, _ = units[unit]
        value = heads_of(proj_ref, 2, head, slice(place * width, (place + 1) * width))
        cols = slice(place * width + start, place * width + start + step)
        mixed_ref[head * HEAD : (head + 1) * HEAD, cols] = nn(value, probs).astype(BF)

    staged(len(units), FORWARD_GROUP if width <= LANES else WIDE_FORWARD_GROUP, score, weigh, mix)
    return [
        x_ref[:, cols].astype(F32) + nn(out_t[...], mixed_ref[:, cols])
        for cols in blocks_of(2 * LANES, total)
    ]


def attend_back(grad_ref, proj_ref, probs_ref, grad_proj_ref, grad_mixed_ref, out, width):
    total = grad_ref.shape[1]
    for cols in blocks_of(2 * LANES, total):
        grad_mixed_ref[:, cols] = nn(out[...], grad_ref[:, cols]).astype(BF)
    units = units_of(total, width)
    sums = {}

    def spans(unit):
        place, head, start, step, _, _ = units[unit]
        rows = slice(head * HEAD, (head + 1) * HEAD)
        keys = slice(place * width, (place + 1) * width)
        return rows, slice(place * width + start, place * width + start + step), keys

    def probs_of(unit):
        place, head, start, step, _, _ = units[unit]
        return probs_ref[place * HEADS + head, :, start : start + step]

    def to_probs(unit, _):
        rows, cols, keys = spans(unit)
        return tn(heads_of(proj_ref, 2, units[unit][1], keys), grad_mixed_ref[rows, cols])

    def to_scores(unit, grad_probs):
        wide = probs_of(unit).astype(F32)
        moved = grad_probs * wide
        return (moved - wide * jnp.sum(moved, axis=0, keepdims=True)).astype(BF)

    def to_query(unit, grad_scores):
        rows, cols, keys = spans(unit)
        key = heads_of(proj_ref, 1, units[unit][1], keys)
        grad_proj_ref[rows, cols] = (nn(key, grad_scores) * SCALE).astype(BF)
        return grad_scores

    def to_key(unit, grad_scores):
        _, head, _, _, first, last = units[unit]
        rows, cols, keys = spans(unit)
        grad_key = nt(heads_of(proj_ref, 0, head, cols), grad_scores)
        if not first:
            grad_key = grad_key + sums["key"]
        sums["key"] = grad_key
        if last:
            grad_proj_ref[E + rows.start : E + rows.stop, keys] = (grad_key * SCALE).astype(BF)

    def to_value(unit, _):
        _, head, _, _, first, last = units[unit]
        rows, cols, keys = spans(unit)
        grad_value = nt(grad_mixed_ref[rows, cols], probs_of(unit))
        if not first:
            grad_value = grad_value + sums["value"]
        sums["value"] = grad_value
        if last:
            grad_proj_ref[2 * E + rows.start : 2 * E + rows.stop, keys] = grad_value.astype(BF)

    staged(len(units), BACK_GROUP if width <= LANES else WIDE_BACK_GROUP, to_value, to_probs, to_scores, to_query, to_key)


def project_back(grad_ref, x_ref, grad_proj_ref, qkv):
    results = []
    for cols in blocks_of(2 * LANES, x_ref.shape[1]):
        grad_normed = nn(qkv[...], grad_proj_ref[:, cols]).astype(BF).astype(F32)
        normed, root = norm(x_ref[:, cols].astype(F32))
        results.append(norm_back(grad_normed, normed, root) + grad_ref[:, cols].astype(F32))
    return results


def put_halves(bit, sums_ref, keep_ref, send_ref):
    rows, mine = keep_ref.shape[0], has_bit("attr", bit)
    for ref, half in ((keep_ref, mine), (send_ref, 1 - mine)):
        ref[...] = sums_ref[pl.ds(pl.multiple_of(half * rows, rows), rows), :]


def put_attend_grads(out_ref, normed_ref, grad_proj_ref, mixed_ref, grad_ref):
    qkv = nt(normed_ref[...], grad_proj_ref[...])
    out = nt(mixed_ref[...], grad_ref[...])
    whole = 3 * E // LANES
    for tile in range(whole):
        out_ref[tile * E : (tile + 1) * E, :] = qkv[:, tile * LANES : (tile + 1) * LANES].astype(BF)
    mixed = jnp.concatenate([qkv[:, whole * LANES :], out[:, LANES:]], axis=1)
    out_ref[whole * E : (whole + 1) * E, :] = mixed.astype(BF)
    out_ref[(whole + 1) * E : (whole + 2) * E, :] = out[:, :LANES].astype(BF)


def take_attend_grads(in_ref, first, qkv_ref, out_ref, factor):
    whole = 3 * E // LANES

    def tile(number):
        return in_ref[first + number * E : first + (number + 1) * E, :].astype(F32) * factor

    for number in range(whole):
        qkv_ref[:, number * LANES : (number + 1) * LANES] = tile(number)
    mixed = tile(whole)
    qkv_ref[:, whole * LANES :] = mixed[:, : LANES // 2]
    out_ref[:, :LANES] = tile(whole + 1)
    out_ref[:, LANES:] = mixed[:, LANES // 2 :]


def rows_forward_kernel(plan, wait, *refs):
    tiles, refs = refs[: plan.ranks_attr], refs[plan.ranks_attr :]
    (qkv_t, out_t), refs = refs[:2], refs[2:]
    outs, refs = refs[: plan.ranks_attr], refs[plan.ranks_attr :]
    x_ref, normed_ref, proj_ref, probs_ref, mixed_ref = refs
    order = one_hot(plan.cells, plan.grouped_from_rows())
    x_ref[...] = nn(side_by_side(tiles), order).astype(BF)
    first = attend(x_ref, normed_ref, proj_ref, probs_ref, mixed_ref, qkv_t, out_t, plan.all_attr, None)
    put_tiles(outs, nt(jnp.concatenate(first, axis=1).astype(BF), order))


def rows_back_kernel(plan, wait, *refs):
    tiles, refs = refs[: plan.ranks_attr], refs[plan.ranks_attr :]
    (order, out, normed_ref, proj_ref, probs_ref, mixed_ref), refs = refs[:6], refs[6:]
    keep_ref, send_ref, grad_ref, grad_proj_ref, sums_ref, grad_mixed_ref = refs
    grad_ref[...] = nn(side_by_side(tiles), order[...]).astype(BF)
    attend_back(grad_ref, proj_ref, probs_ref, grad_proj_ref, grad_mixed_ref, out, plan.all_attr)
    put_attend_grads(sums_ref, normed_ref, grad_proj_ref, mixed_ref, grad_ref)
    put_halves(bits_of("attr")[0], sums_ref, keep_ref, send_ref)


def end_kernel(wait, order, qkv, x_ref, grad_ref, grad_proj_ref, *outs):
    grads = project_back(grad_ref, x_ref, grad_proj_ref, qkv)
    put_tiles(outs, nt(jnp.concatenate(grads, axis=1).astype(BF), order[...]))


def cols_kernel(plan, wait, *refs):
    count = plan.ranks_rec
    tiles, cot_tiles, refs = refs[:count], refs[count : 2 * count], refs[2 * count :]
    (order, mask_ref, out, up, down, qkv_t, out_t, up_t), refs = refs[:8], refs[8:]
    normed_ref, mixed_ref, normed_second_ref, hidden_ref, cot_ref, grad_pre_ref, grad_ref, grad_proj_ref = refs[:8]
    x_ref, proj_ref, probs_ref, second_ref, slope_ref, wide_ref, grad_mixed_ref = refs[8:]
    width = max(LANES, plan.all_rec)
    x_ref[...] = nn(side_by_side(tiles), order[...]).astype(BF)
    second = attend(x_ref, normed_ref, proj_ref, probs_ref, mixed_ref, qkv_t, out_t, width, mask_ref)
    for cols, value in zip(blocks_of(2 * LANES, plan.cells), second):
        second_ref[:, cols] = value.astype(BF)
        normed_second_ref[:, cols] = norm(second_ref[:, cols].astype(F32))[0].astype(BF)
    wide_ref[...] = nn(up_t[...], normed_second_ref[...])
    step = 32
    for start in range(0, FF, step):
        rows = slice(start, start + step)
        pre = wide_ref[rows, :]
        gate = 0.5 + 0.5 * lax.erf(pre * HALF_ROOT)
        hidden_ref[rows, :] = (pre * gate).astype(BF)
        slope_ref[rows, :] = gate + pre * (jnp.exp2(pre * pre * BELL_EXP2) * BELL)

    cot_ref[...] = nn(side_by_side(cot_tiles), order[...]).astype(BF)
    wide_ref[...] = nn(down[...], cot_ref[...])
    step = 64
    for start in range(0, FF, step):
        rows = slice(start, start + step)
        grad_pre_ref[rows, :] = (wide_ref[rows, :] * slope_ref[rows, :]).astype(BF)
    for cols in blocks_of(2 * LANES, plan.cells):
        grad_normed = nn(up[...], grad_pre_ref[:, cols]).astype(BF).astype(F32)
        table, root = norm(second_ref[:, cols].astype(F32))
        grad_ref[:, cols] = (norm_back(grad_normed, table, root) + cot_ref[:, cols].astype(F32)).astype(BF)
    attend_back(grad_ref, proj_ref, probs_ref, grad_proj_ref, grad_mixed_ref, out, width)


def cols_sums_kernel(wait, *refs):
    normed_ref, mixed_ref, normed_second_ref, hidden_ref, cot_ref, grad_pre_ref, grad_ref, grad_proj_ref = refs[:8]
    keep_ref, send_ref, sums_ref = refs[8:]
    for base, grad_weight in (
        (6 * E, nt(normed_second_ref[...], grad_pre_ref[...])),
        (12 * E, nt(cot_ref[...], hidden_ref[...])),
    ):
        for tile in range(FF // LANES):
            rows = slice(base + tile * E, base + (tile + 1) * E)
            sums_ref[rows, :] = grad_weight[:, tile * LANES : (tile + 1) * LANES].astype(BF)
    put_attend_grads(sums_ref, normed_ref, grad_proj_ref, mixed_ref, grad_ref)
    put_halves(bits_of("attr")[0], sums_ref, keep_ref, send_ref)


def finish_cols_kernel(factor, bits, wait, *refs):
    parts, (qkv_ref, out_ref, up_ref, down_ref, sums_ref) = refs[:-5], refs[-5:]
    lay_out(bits, parts, sums_ref)
    take_attend_grads(sums_ref, 0, qkv_ref, out_ref, factor)
    for base, ref in ((6 * E, up_ref), (12 * E, down_ref)):
        for tile in range(FF // LANES):
            rows = slice(base + tile * E, base + (tile + 1) * E)
            ref[:, tile * LANES : (tile + 1) * LANES] = sums_ref[rows, :].astype(F32) * factor


def finish_rows_kernel(factor, bits, wait, *refs):
    parts, (qkv_ref, out_ref, sums_ref) = refs[:-3], refs[-3:]
    lay_out(bits, parts, sums_ref)
    take_attend_grads(sums_ref, 0, qkv_ref, out_ref, factor)


class Far(NamedTuple):
    array: jax.Array


class Near(NamedTuple):
    array: jax.Array


def in_hbm(array):
    return pltpu.with_memory_space_constraint(array, pltpu.HBM)


def call(body, outs, scratch, *args, after=()):
    far = [n for n, arg in enumerate(args) if isinstance(arg, Far)]
    n_in, n_after, n_out, n_far = len(args), len(after), len(outs), len(far)
    whole, anywhere = pl.BlockSpec(memory_space=pltpu.VMEM), pl.BlockSpec(memory_space=pl.ANY)
    hbm = pl.BlockSpec(memory_space=pltpu.HBM)

    def kernel(*refs):
        given, refs = list(refs[:n_in]), refs[n_in + n_after :]
        copies = []
        if far:
            held, sems, refs = refs[-1 - n_far : -1], refs[-1], refs[: -1 - n_far]
            for order, (number, ref) in enumerate(zip(far, held)):
                copies.append(pltpu.make_async_copy(given[number], ref, sems.at[order]))
                given[number] = ref
        for copy in copies:
            copy.start()

        def wait():
            for copy in copies:
                copy.wait()

        body(wait, *given, *refs)

    arrays = []
    for arg in args:
        space = {Far: pltpu.HBM, Near: pltpu.VMEM}.get(type(arg))
        arrays.append(arg if space is None else pltpu.with_memory_space_constraint(arg.array, space))
    held = [pltpu.VMEM(arrays[n].shape, arrays[n].dtype) for n in far]
    return pl.pallas_call(
        kernel,
        out_shape=[
            (pltpu.VMEM if out[2:] else jax.ShapeDtypeStruct)(out[0], out[1]) for out in outs
        ],
        in_specs=[hbm if isinstance(arg, Far) else whole for arg in args] + [anywhere] * n_after,
        out_specs=[whole] * n_out,
        scratch_shapes=[pltpu.VMEM(shape, dtype) for shape, dtype in scratch]
        + held
        + ([pltpu.SemaphoreType.DMA((n_far,))] if far else []),
        compiler_params=pltpu.CompilerParams(vmem_limit_bytes=VMEM),
    )(*arrays, *[in_hbm(arg.array) if isinstance(arg, Far) else arg for arg in after])


def exchange(tiles, axis, sign):
    size = len(tiles)
    return [tiles[0]] + [
        lax.ppermute(tiles[k], axis, [(i, (i + sign * k) % size) for i in range(size)])
        for k in range(1, size)
    ]


def swap(part, axis, bit):
    size = lax.axis_size(axis)
    return lax.ppermute(part, axis, [(i, i ^ bit) for i in range(size)])


def has_bit(axis, bit):
    return digits(lax.axis_index(axis) // bit, (2,))[0]


def pass_kernel(wait, source, target):
    target[...] = source[...]


def row_tiles_of(arrays):
    return [(array.shape, array.dtype) for array in arrays]


def halve_kernel(axis, bit, wait, *refs):
    parts, (keep, send) = refs[:-2], refs[-2:]
    rows, mine = keep.shape[0], has_bit(axis, bit)
    for ref, half in ((keep, mine), (send, 1 - mine)):
        place = pl.ds(pl.multiple_of(half * rows, rows), rows)
        ref[...] = sum(part[place, :].astype(F32) for part in parts).astype(BF)


def add_kernel(wait, *refs):
    refs[-1][...] = sum(part[...].astype(F32) for part in refs[:-1]).astype(BF)


def lay_out_kernel(axis, bit, wait, own_ref, other_ref, out_ref):
    rows = own_ref.shape[0]
    mine = has_bit(axis, bit)
    for ref, half in ((own_ref, mine), (other_ref, 1 - mine)):
        out_ref[pl.ds(pl.multiple_of(half * rows, rows), rows), :] = ref[...]


def lay_out(bits, parts, rows_ref):
    rows = parts[0].shape[0]
    for number, ref in enumerate(parts):
        place = 0
        for order, bit in enumerate(bits):
            own = has_bit("attr", bit)
            place = place * 2 + (1 - own if number >> order & 1 else own)
        rows_ref[pl.ds(pl.multiple_of(place * rows, rows), rows), :] = ref[...]


def bits_of(axis):
    return [1 << n for n in range(lax.axis_size(axis).bit_length() - 1)]


class Total:
    def __init__(self, *parts):
        self.parts, self.rows = list(parts), parts[0].shape[0]

    def halve(self, axis, bit, after=()):
        self.rows //= 2
        keep, send = call(
            functools.partial(halve_kernel, axis, bit), [((self.rows, LANES), BF)] * 2, [], *self.parts, after=after
        )
        self.parts = [keep, swap(send, axis, bit)]
        return [keep]

    def back(self, axis, bit, after=()):
        self.rows *= 2
        body = functools.partial(lay_out_kernel, axis, bit)
        (part,) = call(body, [((self.rows, LANES), BF)], [], *self.parts, after=after)
        self.parts = [part]
        return [part]

    def add(self, bit=0, after=()):
        (part,) = call(add_kernel, [((self.rows, LANES), BF)], [], *self.parts, after=after)
        self.parts = [part] + ([swap(part, "rec", bit)] if bit else [])
        return [part]

    def spread_after(self, bits, middle):
        done = {0: self.parts[0]}
        for order, bit in reversed(list(enumerate(bits[1:], 1))):
            done.update({number | 1 << order: swap(part, "attr", bit) for number, part in sorted(done.items())})
        near = {1: swap(done[0], "attr", bits[0])}
        results, after = middle()
        for number, part in sorted(done.items()):
            if number:
                (part,) = call(add_kernel, [(part.shape, BF)], [], part, after=after)
                near[number | 1] = swap(part, "attr", bits[0])
        done.update(near)
        return results, [done[number] for number in sorted(done)]


def padded(rows):
    devices = 2 * lax.axis_size("attr")
    return -(-rows // (16 * devices)) * 16 * devices


def local(
    cells, cotangent, qkv_attr, out_attr, qkv_samp, out_samp, up_weight, down_weight, train_split
):
    ranks_rec, ranks_attr = lax.axis_size("rec"), lax.axis_size("attr")
    plan = Plan(cells, ranks_rec, ranks_attr)
    count = plan.cells
    factor = 1.0 / math.sqrt(plan.all_rec * plan.all_attr)
    row_tiles = [((E, plan.row_tile), BF)] * ranks_attr
    col_tiles = [((E, plan.col_tile), BF)] * ranks_rec
    table, wide = ((E, count), BF), ((3 * E, count), BF)

    def probs(width):
        return ((count // width * HEADS, width, width), BF)

    def kernel(body, *static):
        return functools.partial(body, plan, *static)

    rows = call(kernel(split_kernel, True), row_tiles, [((count, E), F32)], Far(cells))
    rows = exchange(rows, "attr", 1)
    weights = (qkv_attr, out_attr)
    got = call(
        kernel(split_turn_kernel),
        col_tiles + [(w.shape[::-1], BF, "near") for w in weights] + [(w.shape, BF, "near") for w in weights],
        [((count, E), F32)],
        Far(cotangent),
        *[Far(w) for w in weights],
        after=[rows[0]],
    )
    cot = exchange(got[:ranks_rec], "rec", 1)
    turned, kept = ([Near(w) for w in part] for part in (got[ranks_rec:-2], got[-2:]))

    got = call(
        kernel(rows_forward_kernel),
        row_tiles + [out + ("near",) for out in (table, table, wide, probs(plan.all_attr), table)],
        [],
        *rows,
        *turned[:2],
    )
    first, (x, normed, proj, weights, mixed) = got[:ranks_attr], [Near(array) for array in got[ranks_attr:]]
    first = exchange(first, "attr", -1)
    cols = exchange(call(kernel(to_cols_kernel), col_tiles, [], *first), "rec", 1)
    weights_more = (qkv_samp, out_samp, up_weight, down_weight.T)
    width = max(LANES, plan.all_rec)
    order = ((count, count), BF, "near")
    got = call(
        kernel(prepare_kernel),
        [(w.shape[::-1], BF, "near") for w in weights_more]
        + [(w.shape, BF, "near") for w in weights_more[:3]]
        + [order] * 3
        + [((width, width), F32, "near")],
        [],
        train_split.reshape(1, -1),
        *[Far(w) for w in weights_more],
        after=cols[:1],
    )
    got = [Near(array) for array in got]
    turned, kept, (by_cols, by_rows, across, mask) = turned + got[:4], kept + got[4:7], got[7:]

    rows_sums, cols_sums = padded(6 * E), padded(18 * E)
    hidden, hidden_wide = ((FF, count), BF), ((FF, count), F32)
    got = call(
        kernel(cols_kernel),
        [out + ("near",) for out in (table, table, table, hidden, table, hidden, table, wide, table)],
        [wide, probs(width), table, hidden_wide, hidden_wide, table],
        *cols,
        *cot,
        by_cols,
        mask,
        kept[3],
        kept[4],
        turned[5],
        turned[2],
        turned[3],
        turned[4],
    )
    saved = [Near(array) for array in got]
    near, far = bits_of("attr"), bits_of("rec")
    keep, send = call(
        cols_sums_kernel, [((cols_sums // 2, LANES), BF)] * 2, [((cols_sums, LANES), BF)], *saved[:8]
    )
    grads = call(end_kernel, col_tiles, [], by_cols, kept[2], saved[8], *saved[6:8], after=[keep])
    sums = Total(keep, swap(send, "attr", near[0]))
    mark = grads[:1]
    for bit in near[1:]:
        mark = sums.halve("attr", bit, after=mark)
    (last,) = call(pass_kernel, row_tiles_of(grads[-1:]), [], grads[-1], after=mark)
    grads = exchange([*grads[:-1], last], "rec", -1)
    arrived = grads[1:]
    rows_grads = call(kernel(to_rows_kernel), row_tiles, [], *grads, across, after=mark)
    grads = exchange(rows_grads, "attr", 1)
    mark = sums.add(far[0], after=arrived)

    keep, send, grad, grad_proj = call(
        kernel(rows_back_kernel),
        [((rows_sums // 2, LANES), BF)] * 2 + [table + ("near",), wide + ("near",)],
        [((rows_sums, LANES), BF), table],
        *grads,
        by_rows,
        kept[1],
        normed,
        proj,
        weights,
        mixed,
        after=mark,
    )
    row_sums = Total(keep, swap(send, "attr", near[0]))
    mark = [keep]
    for bit in far[1:]:
        mark = sums.add(bit, after=mark)
    for bit in near[1:]:
        mark = row_sums.halve("attr", bit, after=mark)
    grads = call(
        end_kernel, row_tiles, [], by_rows, kept[0], x, Near(grad), Near(grad_proj), after=mark
    )
    row_sums.add(far[0], after=mark)
    grads = exchange(grads, "attr", -1)
    mark = grads[1:]
    for bit in far[1:]:
        mark = row_sums.add(bit, after=mark)
    mark = sums.add(after=mark)

    def last_sum():
        last = row_sums.add(after=mark)
        return last, last

    last, parts = sums.spread_after(near, last_sum)

    def middle():
        (cells_out,) = call(kernel(join_kernel), [(cells.shape, BF)], [((count, E), F32)], *grads, after=last)
        weights_out = call(
            functools.partial(finish_cols_kernel, factor, near),
            [((E, 3 * E), F32), ((E, E), F32), ((E, FF), F32), ((E, FF), F32)],
            [((cols_sums, LANES), BF)],
            *parts,
        )
        results = [cells_out, *weights_out]
        return results, [Far(cells_out), Far(weights_out[0])]

    results, row_parts = row_sums.spread_after(near, middle)
    grad_cells, grad_qkv_samp, grad_out_samp, grad_up, grad_down = results
    grad_qkv_attr, grad_out_attr = call(
        functools.partial(finish_rows_kernel, factor, near),
        [((E, 3 * E), F32), ((E, E), F32)],
        [((rows_sums, LANES), BF)],
        *row_parts,
    )
    grad_down = grad_down.T
    return (grad_cells, grad_qkv_attr, grad_out_attr, grad_qkv_samp, grad_out_samp, grad_up, grad_down)


def solution(mesh):
    own = P(("groups", "rec"), "attr")
    in_specs = (own, own) + (P(),) * 6 + (P("groups"),)
    out_specs = (own,) + (P("groups", None),) * 6
    return jax.shard_map(local, mesh=mesh, in_specs=in_specs, out_specs=out_specs, check_vma=False)
```

```python
import functools
import math
from typing import NamedTuple

import jax
import jax.numpy as jnp
from jax import lax
from jax.experimental import pallas as pl
from jax.experimental.pallas import tpu as pltpu
from jax.sharding import PartitionSpec as P

E = 192
HEADS = 6
FF = 768
HEAD = E // HEADS
LANES = 128
FORWARD_GROUP = 1
BACK_GROUP = 3
WIDE_FORWARD_GROUP = 3
WIDE_BACK_GROUP = 2
VMEM = 24 * 1024 * 1024
BF = jnp.bfloat16
F32 = jnp.float32
EXP2 = math.log2(math.e) / math.sqrt(HEAD)
SCALE = 1.0 / math.sqrt(HEAD)
HALF_ROOT = math.sqrt(0.5)
BELL_EXP2 = -0.5 * math.log2(math.e)
BELL = 1.0 / math.sqrt(2.0 * math.pi)


def nn(left, right):
    return lax.dot_general(left, right, (((1,), (0,)), ((), ())), preferred_element_type=F32)


def nt(left, right):
    return lax.dot_general(left, right, (((1,), (1,)), ((), ())), preferred_element_type=F32)


def tn(left, right):
    return lax.dot_general(left, right, (((0,), (0,)), ((), ())), preferred_element_type=F32)


def digits(index, sizes):
    out = []
    for size in reversed(sizes):
        if size & (size - 1) == 0:
            out.append(index & (size - 1))
            index = index >> (size.bit_length() - 1)
        else:
            out.append(lax.rem(index, size))
            index = lax.div(index, size)
    return out[::-1]


def wrap(index, size):
    return digits(index + size, (size,))[0]


def one_hot(rows, source):
    own = lax.broadcasted_iota(jnp.int32, (rows, source.shape[1]), 0)
    return jnp.where(own == source, 1.0, 0.0).astype(BF)


def lane_index(size):
    return lax.broadcasted_iota(jnp.int32, (1, size), 1)


def eye(size):
    return one_hot(size, lane_index(size))


def side_by_side(refs):
    return jnp.concatenate([ref[...] for ref in refs], axis=1)


def put_tiles(refs, table):
    width = refs[0].shape[1]
    for position, ref in enumerate(refs):
        ref[...] = table[:, position * width : (position + 1) * width].astype(ref.dtype)


class Plan:
    def __init__(self, cells, ranks_rec, ranks_attr):
        self.ranks_rec, self.ranks_attr = ranks_rec, ranks_attr
        self.rec, self.attr = cells.shape[0], cells.shape[1] // E
        self.cells = self.rec * self.attr
        self.own_rec = self.rec // ranks_attr
        self.own_attr = self.attr // ranks_rec
        self.all_rec = self.rec * ranks_rec
        self.all_attr = self.attr * ranks_attr
        self.row_tile = self.own_rec * self.attr
        self.col_tile = self.rec * self.own_attr

    def row_digits(self, index):
        return digits(index, (self.ranks_attr, self.own_rec, self.attr))

    def col_digits(self, index):
        return digits(index, (self.ranks_rec, self.ranks_attr, self.own_rec, self.own_attr))

    def record_of(self, step, own):
        return self.own_rec * wrap(step + lax.axis_index("attr"), self.ranks_attr) + own

    def attr_of(self, step, own):
        return self.own_attr * wrap(step + lax.axis_index("rec"), self.ranks_rec) + own

    def rows_from_owned(self):
        step, own, attr = self.row_digits(lane_index(self.cells))
        return attr * self.rec + self.record_of(step, own)

    def cols_from_owned(self):
        far, near, own, attr = self.col_digits(lane_index(self.cells))
        return self.attr_of(far, attr) * self.rec + self.record_of(near, own)

    def cols_from_rows(self):
        far, near, own, attr = self.col_digits(lane_index(self.cells))
        return (near * self.own_rec + own) * self.attr + self.attr_of(far, attr)

    def grouped_from_rows(self):
        own, step, attr = digits(lane_index(self.cells), (self.own_rec, self.ranks_attr, self.attr))
        return (step * self.own_rec + own) * self.attr + attr

    def grouped_from_cols(self):
        attr, place = digits(lane_index(self.cells), (self.own_attr, self.all_rec))
        return place * self.own_attr + attr


def split_kernel(plan, to_rows, wait, table_ref, *refs):
    wait()
    outs, rows = refs[:-1], refs[-1]
    for pair in range(plan.attr // 2):
        both = table_ref[:, 2 * E * pair : 2 * E * (pair + 1)].astype(F32)
        for side in range(2):
            start = (2 * pair + side) * plan.rec
            rows[start : start + plan.rec, :] = both[:, side * E : (side + 1) * E]
    turned = nt(eye(E), rows[...].astype(BF)).astype(BF)
    source = plan.rows_from_owned() if to_rows else plan.cols_from_owned()
    put_tiles(outs, nn(turned, one_hot(plan.cells, source)))


def join_kernel(plan, wait, *refs):
    tiles, out_ref, rows = refs[:-2], refs[-2], refs[-1]
    rows[...] = nt(one_hot(plan.cells, plan.rows_from_owned()), side_by_side(tiles))
    for pair in range(plan.attr // 2):
        start = 2 * pair * plan.rec
        both = [rows[start + side * plan.rec : start + (side + 1) * plan.rec, :] for side in range(2)]
        out_ref[:, 2 * E * pair : 2 * E * (pair + 1)] = jnp.concatenate(both, axis=1).astype(BF)


def to_cols_kernel(plan, wait, *refs):
    tiles, outs = refs[: plan.ranks_attr], refs[plan.ranks_attr :]
    put_tiles(outs, nn(side_by_side(tiles), one_hot(plan.cells, plan.cols_from_rows())))


def to_rows_kernel(plan, wait, *refs):
    tiles, across, outs = refs[: plan.ranks_rec], refs[plan.ranks_rec], refs[plan.ranks_rec + 1 :]
    put_tiles(outs, nt(side_by_side(tiles), across[...]))


def turn_kernel(wait, weights, turned, kept):
    for source, target in zip(weights, turned):
        target[...] = source[...].astype(F32).T.astype(BF)
    for source, target in zip(weights, kept):
        target[...] = source[...]


def split_turn_kernel(plan, wait, table_ref, *refs):
    split_kernel(plan, False, wait, table_ref, *refs[2 : 2 + plan.ranks_rec], refs[-1])
    turn_kernel(wait, refs[:2], refs[2 + plan.ranks_rec : 4 + plan.ranks_rec], refs[4 + plan.ranks_rec : -1])


def prepare_kernel(plan, wait, train_ref, *refs):
    weights, turned, kept, (by_cols, by_rows, across, mask_ref) = refs[:4], refs[4:8], refs[8:11], refs[11:]
    by_cols[...] = one_hot(plan.cells, plan.grouped_from_cols())
    by_rows[...] = one_hot(plan.cells, plan.grouped_from_rows())
    across[...] = one_hot(plan.cells, plan.cols_from_rows())
    width = max(LANES, plan.all_rec)
    row = lax.broadcasted_iota(jnp.int32, (width, 1), 0)
    sequence, far, near, own = digits(row, (width // plan.all_rec, plan.ranks_rec, plan.ranks_attr, plan.own_rec))
    record = plan.rec * wrap(lax.axis_index("rec") - far, plan.ranks_rec) + plan.record_of(near, own)
    chosen = (record == lane_index(plan.all_rec)) & (train_ref[...] > 0)
    allowed = jnp.max(jnp.where(chosen, 1.0, 0.0), axis=1, keepdims=True) > 0.5
    asker = digits(lane_index(width), (width // plan.all_rec, plan.all_rec))[0]
    mask_ref[...] = jnp.where(allowed & (sequence == asker), 0.0, -1e30)
    wait()
    turn_kernel(wait, weights, turned, kept)


def norm(table):
    center = table - jnp.mean(table, axis=0, keepdims=True)
    spread = jnp.mean(center * center, axis=0, keepdims=True)
    root = lax.rsqrt(spread + 1e-05)
    return center * root, root


def norm_back(grad, normed, root):
    along = jnp.mean(grad * normed, axis=0, keepdims=True)
    return root * (grad - jnp.mean(grad, axis=0, keepdims=True) - normed * along)


def blocks_of(width, total):
    return [slice(start, start + width) for start in range(0, total, width)]


def heads_of(ref, part, head, cols):
    start = part * E + head * HEAD
    return ref[start : start + HEAD, cols]


def staged(count, group, *stages):
    held = {}
    groups = [range(start, min(start + group, count)) for start in range(0, count, group)]
    for step in range(len(groups) + len(stages) - 1):
        for lag, stage in enumerate(stages):
            if 0 <= step - lag < len(groups):
                for unit in groups[step - lag]:
                    held[unit] = stage(unit, held.get(unit))


def units_of(total, width):
    step = min(2 * LANES, width)
    return [
        (place, head, start, step, start == 0, start + step == width)
        for place in range(total // width)
        for head in range(HEADS)
        for start in range(0, width, step)
    ]


def attend(x_ref, normed_ref, proj_ref, probs_ref, mixed_ref, qkv_t, out_t, width, mask_ref):
    total = x_ref.shape[1]
    for cols in blocks_of(2 * LANES, total):
        normed_ref[:, cols] = norm(x_ref[:, cols].astype(F32))[0].astype(BF)
    for cols in blocks_of(2 * LANES, total):
        proj_ref[:, cols] = nn(qkv_t[...], normed_ref[:, cols]).astype(BF)
    units = units_of(total, width)

    def score(unit, _):
        place, head, start, step, _, _ = units[unit]
        cols = slice(place * width + start, place * width + start + step)
        keys = slice(place * width, (place + 1) * width)
        return tn(heads_of(proj_ref, 1, head, keys), heads_of(proj_ref, 0, head, cols))

    def weigh(unit, scores):
        place, head, start, step, _, _ = units[unit]
        if mask_ref is not None:
            scores = scores + mask_ref[:, start : start + step]
        expo = jnp.exp2((scores - jnp.max(scores, axis=0, keepdims=True)) * EXP2)
        probs = (expo * (1.0 / jnp.sum(expo, axis=0, keepdims=True))).astype(BF)
        probs_ref[place * HEADS + head, :, start : start + step] = probs
        return probs

    def mix(unit, probs):
        place, head, start, step, _, _ = units[unit]
        value = heads_of(proj_ref, 2, head, slice(place * width, (place + 1) * width))
        cols = slice(place * width + start, place * width + start + step)
        mixed_ref[head * HEAD : (head + 1) * HEAD, cols] = nn(value, probs).astype(BF)

    staged(len(units), FORWARD_GROUP if width <= LANES else WIDE_FORWARD_GROUP, score, weigh, mix)
    return [
        x_ref[:, cols].astype(F32) + nn(out_t[...], mixed_ref[:, cols])
        for cols in blocks_of(2 * LANES, total)
    ]


def attend_back(grad_ref, proj_ref, probs_ref, grad_proj_ref, grad_mixed_ref, out, width):
    total = grad_ref.shape[1]
    for cols in blocks_of(2 * LANES, total):
        grad_mixed_ref[:, cols] = nn(out[...], grad_ref[:, cols]).astype(BF)
    units = units_of(total, width)
    sums = {}

    def spans(unit):
        place, head, start, step, _, _ = units[unit]
        rows = slice(head * HEAD, (head + 1) * HEAD)
        keys = slice(place * width, (place + 1) * width)
        return rows, slice(place * width + start, place * width + start + step), keys

    def probs_of(unit):
        place, head, start, step, _, _ = units[unit]
        return probs_ref[place * HEADS + head, :, start : start + step]

    def to_probs(unit, _):
        rows, cols, keys = spans(unit)
        return tn(heads_of(proj_ref, 2, units[unit][1], keys), grad_mixed_ref[rows, cols])

    def to_scores(unit, grad_probs):
        wide = probs_of(unit).astype(F32)
        moved = grad_probs * wide
        return (moved - wide * jnp.sum(moved, axis=0, keepdims=True)).astype(BF)

    def to_query(unit, grad_scores):
        rows, cols, keys = spans(unit)
        key = heads_of(proj_ref, 1, units[unit][1], keys)
        grad_proj_ref[rows, cols] = (nn(key, grad_scores) * SCALE).astype(BF)
        return grad_scores

    def to_key(unit, grad_scores):
        _, head, _, _, first, last = units[unit]
        rows, cols, keys = spans(unit)
        grad_key = nt(heads_of(proj_ref, 0, head, cols), grad_scores)
        if not first:
            grad_key = grad_key + sums["key"]
        sums["key"] = grad_key
        if last:
            grad_proj_ref[E + rows.start : E + rows.stop, keys] = (grad_key * SCALE).astype(BF)

    def to_value(unit, _):
        _, head, _, _, first, last = units[unit]
        rows, cols, keys = spans(unit)
        grad_value = nt(grad_mixed_ref[rows, cols], probs_of(unit))
        if not first:
            grad_value = grad_value + sums["value"]
        sums["value"] = grad_value
        if last:
            grad_proj_ref[2 * E + rows.start : 2 * E + rows.stop, keys] = grad_value.astype(BF)

    staged(len(units), BACK_GROUP if width <= LANES else WIDE_BACK_GROUP, to_value, to_probs, to_scores, to_query, to_key)


def project_back(grad_ref, x_ref, grad_proj_ref, qkv):
    results = []
    for cols in blocks_of(2 * LANES, x_ref.shape[1]):
        grad_normed = nn(qkv[...], grad_proj_ref[:, cols]).astype(BF).astype(F32)
        normed, root = norm(x_ref[:, cols].astype(F32))
        results.append(norm_back(grad_normed, normed, root) + grad_ref[:, cols].astype(F32))
    return results


def put_halves(bit, sums_ref, keep_ref, send_ref):
    rows, mine = keep_ref.shape[0], has_bit("attr", bit)
    for ref, half in ((keep_ref, mine), (send_ref, 1 - mine)):
        ref[...] = sums_ref[pl.ds(pl.multiple_of(half * rows, rows), rows), :]


def put_attend_grads(out_ref, normed_ref, grad_proj_ref, mixed_ref, grad_ref):
    qkv = nt(normed_ref[...], grad_proj_ref[...])
    out = nt(mixed_ref[...], grad_ref[...])
    whole = 3 * E // LANES
    for tile in range(whole):
        out_ref[tile * E : (tile + 1) * E, :] = qkv[:, tile * LANES : (tile + 1) * LANES].astype(BF)
    mixed = jnp.concatenate([qkv[:, whole * LANES :], out[:, LANES:]], axis=1)
    out_ref[whole * E : (whole + 1) * E, :] = mixed.astype(BF)
    out_ref[(whole + 1) * E : (whole + 2) * E, :] = out[:, :LANES].astype(BF)


def take_attend_grads(in_ref, first, qkv_ref, out_ref, factor):
    whole = 3 * E // LANES

    def tile(number):
        return in_ref[first + number * E : first + (number + 1) * E, :].astype(F32) * factor

    for number in range(whole):
        qkv_ref[:, number * LANES : (number + 1) * LANES] = tile(number)
    mixed = tile(whole)
    qkv_ref[:, whole * LANES :] = mixed[:, : LANES // 2]
    out_ref[:, :LANES] = tile(whole + 1)
    out_ref[:, LANES:] = mixed[:, LANES // 2 :]


def rows_forward_kernel(plan, wait, *refs):
    tiles, refs = refs[: plan.ranks_attr], refs[plan.ranks_attr :]
    (qkv_t, out_t), refs = refs[:2], refs[2:]
    outs, refs = refs[: plan.ranks_attr], refs[plan.ranks_attr :]
    x_ref, normed_ref, proj_ref, probs_ref, mixed_ref = refs
    order = one_hot(plan.cells, plan.grouped_from_rows())
    x_ref[...] = nn(side_by_side(tiles), order).astype(BF)
    first = attend(x_ref, normed_ref, proj_ref, probs_ref, mixed_ref, qkv_t, out_t, plan.all_attr, None)
    put_tiles(outs, nt(jnp.concatenate(first, axis=1).astype(BF), order))


def rows_back_kernel(plan, wait, *refs):
    tiles, refs = refs[: plan.ranks_attr], refs[plan.ranks_attr :]
    (order, out, normed_ref, proj_ref, probs_ref, mixed_ref), refs = refs[:6], refs[6:]
    keep_ref, send_ref, grad_ref, grad_proj_ref, sums_ref, grad_mixed_ref = refs
    grad_ref[...] = nn(side_by_side(tiles), order[...]).astype(BF)
    attend_back(grad_ref, proj_ref, probs_ref, grad_proj_ref, grad_mixed_ref, out, plan.all_attr)
    put_attend_grads(sums_ref, normed_ref, grad_proj_ref, mixed_ref, grad_ref)
    put_halves(bits_of("attr")[0], sums_ref, keep_ref, send_ref)


def end_kernel(wait, order, qkv, x_ref, grad_ref, grad_proj_ref, *outs):
    grads = project_back(grad_ref, x_ref, grad_proj_ref, qkv)
    put_tiles(outs, nt(jnp.concatenate(grads, axis=1).astype(BF), order[...]))


def cols_kernel(plan, wait, *refs):
    count = plan.ranks_rec
    tiles, cot_tiles, refs = refs[:count], refs[count : 2 * count], refs[2 * count :]
    (order, mask_ref, out, up, down, qkv_t, out_t, up_t), refs = refs[:8], refs[8:]
    normed_ref, mixed_ref, normed_second_ref, hidden_ref, cot_ref, grad_pre_ref, grad_ref, grad_proj_ref = refs[:8]
    x_ref, proj_ref, probs_ref, second_ref, slope_ref, wide_ref, grad_mixed_ref = refs[8:]
    width = max(LANES, plan.all_rec)
    x_ref[...] = nn(side_by_side(tiles), order[...]).astype(BF)
    second = attend(x_ref, normed_ref, proj_ref, probs_ref, mixed_ref, qkv_t, out_t, width, mask_ref)
    for cols, value in zip(blocks_of(2 * LANES, plan.cells), second):
        second_ref[:, cols] = value.astype(BF)
        normed_second_ref[:, cols] = norm(second_ref[:, cols].astype(F32))[0].astype(BF)
    wide_ref[...] = nn(up_t[...], normed_second_ref[...])
    step = 32
    for start in range(0, FF, step):
        rows = slice(start, start + step)
        pre = wide_ref[rows, :]
        gate = 0.5 + 0.5 * lax.erf(pre * HALF_ROOT)
        hidden_ref[rows, :] = (pre * gate).astype(BF)
        slope_ref[rows, :] = gate + pre * (jnp.exp2(pre * pre * BELL_EXP2) * BELL)

    cot_ref[...] = nn(side_by_side(cot_tiles), order[...]).astype(BF)
    wide_ref[...] = nn(down[...], cot_ref[...])
    step = 64
    for start in range(0, FF, step):
        rows = slice(start, start + step)
        grad_pre_ref[rows, :] = (wide_ref[rows, :] * slope_ref[rows, :]).astype(BF)
    for cols in blocks_of(2 * LANES, plan.cells):
        grad_normed = nn(up[...], grad_pre_ref[:, cols]).astype(BF).astype(F32)
        table, root = norm(second_ref[:, cols].astype(F32))
        grad_ref[:, cols] = (norm_back(grad_normed, table, root) + cot_ref[:, cols].astype(F32)).astype(BF)
    attend_back(grad_ref, proj_ref, probs_ref, grad_proj_ref, grad_mixed_ref, out, width)


def cols_sums_kernel(wait, *refs):
    normed_ref, mixed_ref, normed_second_ref, hidden_ref, cot_ref, grad_pre_ref, grad_ref, grad_proj_ref = refs[:8]
    keep_ref, send_ref, sums_ref = refs[8:]
    for base, grad_weight in (
        (6 * E, nt(normed_second_ref[...], grad_pre_ref[...])),
        (12 * E, nt(cot_ref[...], hidden_ref[...])),
    ):
        for tile in range(FF // LANES):
            rows = slice(base + tile * E, base + (tile + 1) * E)
            sums_ref[rows, :] = grad_weight[:, tile * LANES : (tile + 1) * LANES].astype(BF)
    put_attend_grads(sums_ref, normed_ref, grad_proj_ref, mixed_ref, grad_ref)
    put_halves(bits_of("attr")[0], sums_ref, keep_ref, send_ref)


def finish_cols_kernel(factor, bits, wait, *refs):
    parts, (qkv_ref, out_ref, up_ref, down_ref, sums_ref) = refs[:-5], refs[-5:]
    lay_out(bits, parts, sums_ref)
    take_attend_grads(sums_ref, 0, qkv_ref, out_ref, factor)
    for base, ref in ((6 * E, up_ref), (12 * E, down_ref)):
        for tile in range(FF // LANES):
            rows = slice(base + tile * E, base + (tile + 1) * E)
            ref[:, tile * LANES : (tile + 1) * LANES] = sums_ref[rows, :].astype(F32) * factor


def finish_rows_kernel(factor, bits, wait, *refs):
    parts, (qkv_ref, out_ref, sums_ref) = refs[:-3], refs[-3:]
    lay_out(bits, parts, sums_ref)
    take_attend_grads(sums_ref, 0, qkv_ref, out_ref, factor)


class Far(NamedTuple):
    array: jax.Array


class Near(NamedTuple):
    array: jax.Array


def in_hbm(array):
    return pltpu.with_memory_space_constraint(array, pltpu.HBM)


def call(body, outs, scratch, *args, after=()):
    far = [n for n, arg in enumerate(args) if isinstance(arg, Far)]
    n_in, n_after, n_out, n_far = len(args), len(after), len(outs), len(far)
    whole, anywhere = pl.BlockSpec(memory_space=pltpu.VMEM), pl.BlockSpec(memory_space=pl.ANY)
    hbm = pl.BlockSpec(memory_space=pltpu.HBM)

    def kernel(*refs):
        given, refs = list(refs[:n_in]), refs[n_in + n_after :]
        copies = []
        if far:
            held, sems, refs = refs[-1 - n_far : -1], refs[-1], refs[: -1 - n_far]
            for order, (number, ref) in enumerate(zip(far, held)):
                copies.append(pltpu.make_async_copy(given[number], ref, sems.at[order]))
                given[number] = ref
        for copy in copies:
            copy.start()

        def wait():
            for copy in copies:
                copy.wait()

        body(wait, *given, *refs)

    arrays = []
    for arg in args:
        space = {Far: pltpu.HBM, Near: pltpu.VMEM}.get(type(arg))
        arrays.append(arg if space is None else pltpu.with_memory_space_constraint(arg.array, space))
    held = [pltpu.VMEM(arrays[n].shape, arrays[n].dtype) for n in far]
    return pl.pallas_call(
        kernel,
        out_shape=[
            (pltpu.VMEM if out[2:] else jax.ShapeDtypeStruct)(out[0], out[1]) for out in outs
        ],
        in_specs=[hbm if isinstance(arg, Far) else whole for arg in args] + [anywhere] * n_after,
        out_specs=[whole] * n_out,
        scratch_shapes=[pltpu.VMEM(shape, dtype) for shape, dtype in scratch]
        + held
        + ([pltpu.SemaphoreType.DMA((n_far,))] if far else []),
        compiler_params=pltpu.CompilerParams(vmem_limit_bytes=VMEM),
    )(*arrays, *[in_hbm(arg.array) if isinstance(arg, Far) else arg for arg in after])


def exchange(tiles, axis, sign):
    size = len(tiles)
    return [tiles[0]] + [
        lax.ppermute(tiles[k], axis, [(i, (i + sign * k) % size) for i in range(size)])
        for k in range(1, size)
    ]


def swap(part, axis, bit):
    size = lax.axis_size(axis)
    return lax.ppermute(part, axis, [(i, i ^ bit) for i in range(size)])


def has_bit(axis, bit):
    return digits(lax.axis_index(axis) // bit, (2,))[0]


def pass_kernel(wait, source, target):
    target[...] = source[...]


def row_tiles_of(arrays):
    return [(array.shape, array.dtype) for array in arrays]


def halve_kernel(axis, bit, wait, *refs):
    parts, (keep, send) = refs[:-2], refs[-2:]
    rows, mine = keep.shape[0], has_bit(axis, bit)
    for ref, half in ((keep, mine), (send, 1 - mine)):
        place = pl.ds(pl.multiple_of(half * rows, rows), rows)
        ref[...] = sum(part[place, :].astype(F32) for part in parts).astype(BF)


def add_kernel(wait, *refs):
    refs[-1][...] = sum(part[...].astype(F32) for part in refs[:-1]).astype(BF)


def lay_out_kernel(axis, bit, wait, own_ref, other_ref, out_ref):
    rows = own_ref.shape[0]
    mine = has_bit(axis, bit)
    for ref, half in ((own_ref, mine), (other_ref, 1 - mine)):
        out_ref[pl.ds(pl.multiple_of(half * rows, rows), rows), :] = ref[...]


def lay_out(bits, parts, rows_ref):
    rows = parts[0].shape[0]
    for number, ref in enumerate(parts):
        place = 0
        for order, bit in enumerate(bits):
            own = has_bit("attr", bit)
            place = place * 2 + (1 - own if number >> order & 1 else own)
        rows_ref[pl.ds(pl.multiple_of(place * rows, rows), rows), :] = ref[...]


def bits_of(axis):
    return [1 << n for n in range(lax.axis_size(axis).bit_length() - 1)]


class Total:
    def __init__(self, *parts):
        self.parts, self.rows = list(parts), parts[0].shape[0]

    def halve(self, axis, bit, after=()):
        self.rows //= 2
        keep, send = call(
            functools.partial(halve_kernel, axis, bit), [((self.rows, LANES), BF)] * 2, [], *self.parts, after=after
        )
        self.parts = [keep, swap(send, axis, bit)]
        return [keep]

    def back(self, axis, bit, after=()):
        self.rows *= 2
        body = functools.partial(lay_out_kernel, axis, bit)
        (part,) = call(body, [((self.rows, LANES), BF)], [], *self.parts, after=after)
        self.parts = [part]
        return [part]

    def add(self, bit=0, after=()):
        (part,) = call(add_kernel, [((self.rows, LANES), BF)], [], *self.parts, after=after)
        self.parts = [part] + ([swap(part, "rec", bit)] if bit else [])
        return [part]

    def spread_after(self, bits, middle):
        done = {0: self.parts[0]}
        for order, bit in reversed(list(enumerate(bits[1:], 1))):
            done.update({number | 1 << order: swap(part, "attr", bit) for number, part in sorted(done.items())})
        near = {1: swap(done[0], "attr", bits[0])}
        results, after = middle()
        for number, part in sorted(done.items()):
            if number:
                (part,) = call(add_kernel, [(part.shape, BF)], [], part, after=after)
                near[number | 1] = swap(part, "attr", bits[0])
        done.update(near)
        return results, [done[number] for number in sorted(done)]


def padded(rows):
    devices = 2 * lax.axis_size("attr")
    return -(-rows // (16 * devices)) * 16 * devices


def local(
    cells, cotangent, qkv_attr, out_attr, qkv_samp, out_samp, up_weight, down_weight, train_split
):
    ranks_rec, ranks_attr = lax.axis_size("rec"), lax.axis_size("attr")
    plan = Plan(cells, ranks_rec, ranks_attr)
    count = plan.cells
    factor = 1.0 / math.sqrt(plan.all_rec * plan.all_attr)
    row_tiles = [((E, plan.row_tile), BF)] * ranks_attr
    col_tiles = [((E, plan.col_tile), BF)] * ranks_rec
    table, wide = ((E, count), BF), ((3 * E, count), BF)

    def probs(width):
        return ((count // width * HEADS, width, width), BF)

    def kernel(body, *static):
        return functools.partial(body, plan, *static)

    rows = call(kernel(split_kernel, True), row_tiles, [((count, E), F32)], Far(cells))
    rows = exchange(rows, "attr", 1)
    weights = (qkv_attr, out_attr)
    got = call(
        kernel(split_turn_kernel),
        col_tiles + [(w.shape[::-1], BF, "near") for w in weights] + [(w.shape, BF, "near") for w in weights],
        [((count, E), F32)],
        Far(cotangent),
        *[Far(w) for w in weights],
        after=[rows[0]],
    )
    cot = exchange(got[:ranks_rec], "rec", 1)
    turned, kept = ([Near(w) for w in part] for part in (got[ranks_rec:-2], got[-2:]))

    got = call(
        kernel(rows_forward_kernel),
        row_tiles + [out + ("near",) for out in (table, table, wide, probs(plan.all_attr), table)],
        [],
        *rows,
        *turned[:2],
    )
    first, (x, normed, proj, weights, mixed) = got[:ranks_attr], [Near(array) for array in got[ranks_attr:]]
    first = exchange(first, "attr", -1)
    cols = exchange(call(kernel(to_cols_kernel), col_tiles, [], *first), "rec", 1)
    weights_more = (qkv_samp, out_samp, up_weight, down_weight.T)
    width = max(LANES, plan.all_rec)
    order = ((count, count), BF, "near")
    got = call(
        kernel(prepare_kernel),
        [(w.shape[::-1], BF, "near") for w in weights_more]
        + [(w.shape, BF, "near") for w in weights_more[:3]]
        + [order] * 3
        + [((width, width), F32, "near")],
        [],
        train_split.reshape(1, -1),
        *[Far(w) for w in weights_more],
        after=cols[:1],
    )
    got = [Near(array) for array in got]
    turned, kept, (by_cols, by_rows, across, mask) = turned + got[:4], kept + got[4:7], got[7:]

    rows_sums, cols_sums = padded(6 * E), padded(18 * E)
    hidden, hidden_wide = ((FF, count), BF), ((FF, count), F32)
    got = call(
        kernel(cols_kernel),
        [out + ("near",) for out in (table, table, table, hidden, table, hidden, table, wide, table)],
        [wide, probs(width), table, hidden_wide, hidden_wide, table],
        *cols,
        *cot,
        by_cols,
        mask,
        kept[3],
        kept[4],
        turned[5],
        turned[2],
        turned[3],
        turned[4],
    )
    saved = [Near(array) for array in got]
    near, far = bits_of("attr"), bits_of("rec")
    keep, send = call(
        cols_sums_kernel, [((cols_sums // 2, LANES), BF)] * 2, [((cols_sums, LANES), BF)], *saved[:8]
    )
    grads = call(end_kernel, col_tiles, [], by_cols, kept[2], saved[8], *saved[6:8], after=[keep])
    sums = Total(keep, swap(send, "attr", near[0]))
    mark = grads[:1]
    for bit in near[1:]:
        mark = sums.halve("attr", bit, after=mark)
    (last,) = call(pass_kernel, row_tiles_of(grads[-1:]), [], grads[-1], after=mark)
    grads = exchange([*grads[:-1], last], "rec", -1)
    arrived = grads[1:]
    rows_grads = call(kernel(to_rows_kernel), row_tiles, [], *grads, across, after=mark)
    grads = exchange(rows_grads, "attr", 1)
    mark = sums.add(far[-1], after=arrived)

    keep, send, grad, grad_proj = call(
        kernel(rows_back_kernel),
        [((rows_sums // 2, LANES), BF)] * 2 + [table + ("near",), wide + ("near",)],
        [((rows_sums, LANES), BF), table],
        *grads,
        by_rows,
        kept[1],
        normed,
        proj,
        weights,
        mixed,
        after=mark,
    )
    row_sums = Total(keep, swap(send, "attr", near[0]))
    grads = call(end_kernel, row_tiles, [], by_rows, kept[0], x, Near(grad), Near(grad_proj), after=[keep])
    mark = grads[:1]
    for bit in near[1:]:
        mark = row_sums.halve("attr", bit, after=mark)
    for bit in far[-2::-1]:
        mark = sums.add(bit, after=mark)
    grads = exchange(grads, "attr", -1)
    mark = row_sums.add(far[0], after=mark + grads[1:])
    for bit in far[1:]:
        mark = row_sums.add(bit, after=mark)
    mark = sums.add(after=mark)

    def last_sum():
        last = row_sums.add(after=mark)
        return last, last

    last, parts = sums.spread_after(near, last_sum)

    def middle():
        (cells_out,) = call(kernel(join_kernel), [(cells.shape, BF)], [((count, E), F32)], *grads, after=last)
        weights_out = call(
            functools.partial(finish_cols_kernel, factor, near),
            [((E, 3 * E), F32), ((E, E), F32), ((E, FF), F32), ((E, FF), F32)],
            [((cols_sums, LANES), BF)],
            *parts,
        )
        results = [cells_out, *weights_out]
        return results, [Far(cells_out), Far(weights_out[0])]

    results, row_parts = row_sums.spread_after(near, middle)
    grad_cells, grad_qkv_samp, grad_out_samp, grad_up, grad_down = results
    grad_qkv_attr, grad_out_attr = call(
        functools.partial(finish_rows_kernel, factor, near),
        [((E, 3 * E), F32), ((E, E), F32)],
        [((rows_sums, LANES), BF)],
        *row_parts,
    )
    grad_down = grad_down.T
    return (grad_cells, grad_qkv_attr, grad_out_attr, grad_qkv_samp, grad_out_samp, grad_up, grad_down)


def solution(mesh):
    own = P(("groups", "rec"), "attr")
    in_specs = (own, own) + (P(),) * 6 + (P("groups"),)
    out_specs = (own,) + (P("groups", None),) * 6
    return jax.shard_map(local, mesh=mesh, in_specs=in_specs, out_specs=out_specs, check_vma=False)
```
